32 devices in a mesh: rep: 2 (over x), shard: 16 (over z, y, core).
Axes of the slice: x: 2, y: 2, z: 4, core: 2. Of those that a mesh axis runs over, the one named last changes fastest.
Arguments:
- tokens: bfloat16 [16384, 1536], P(('rep', 'shard')), may hold values from -6 to 6
- cotangent: bfloat16 [16384, 1536], P(('rep', 'shard')), may hold values from -6 to 6
- lengths: int32 [32, 2], P(('rep', 'shard')), may hold values from 0 to 512, as said below
- weight_in: float32 [2, 1536, 6448], P(None, 'shard'), may hold values from -0.15625 to 0.15625
- moment_in: float32 [2, 1536, 6448], P(None, 'shard')
- second_in: float32 [2, 1536, 6448], P(None, 'shard'), as said below
- weight_out: float32 [2, 3072, 1536], P(None, 'shard'), may hold values from -0.109375 to 0.109375
- moment_out: float32 [2, 3072, 1536], P(None, 'shard')
- second_out: float32 [2, 3072, 1536], P(None, 'shard'), as said below
- side_params: float32 [2, 21392], replicated, as said below
- side_moment: float32 [2, 21392], replicated
- side_second: float32 [2, 21392], replicated, as said below
Outputs:
- layer_out: float32 [2, 16384, 1536], P(None, ('rep', 'shard'))
- token_grad: float32 [16384, 1536], P(('rep', 'shard'))
- new_weight_in: float32 [2, 1536, 6448], P(None, 'shard')
- new_moment_in: float32 [2, 1536, 6448], P(None, 'shard')
- new_second_in: float32 [2, 1536, 6448], P(None, 'shard')
- new_weight_out: float32 [2, 3072, 1536], P(None, 'shard')
- new_moment_out: float32 [2, 3072, 1536], P(None, 'shard')
- new_second_out: float32 [2, 3072, 1536], P(None, 'shard')
- new_side: float32 [2, 21392], replicated
- new_side_moment: float32 [2, 21392], replicated
- new_side_second: float32 [2, 21392], replicated
The draws below stay inside these ranges and needn't reach their ends.
Inputs may be any that keep to these rules, and one draw needn't show every extreme that they name: Each row holds the lengths of the sequences of one device in order, multiples of 256 summing to 512, then zeros; some device holds one sequence of 512. `second_in`: positive. `second_out`: positive. `side_params`: gains and skip positive. `side_second`: positive.
All inputs are finite; a program needn't handle non-finite values.
Results may differ from the reference program's by a relative error of at most 0.017.
Values may be sent and summed in bfloat16 or wider, within the bound.
A program may use at most 448 MiB of HBM per device.

```python
import math
from functools import partial
import jax
import jax.numpy as jnp
from jax import lax

D = 1536
INNER = 3072
HEAD_DIM = 64
STATE = 128
CONV = 4
SPAN = 256
TOK_DEV = 512
LAYERS = 2
STEP = 10
HEADS = 48
XBC = 3328
PROJ = 6448
SMALL = 21392
TOKENS = 16384


def moment_first(key, array_shape, grad_scale):
    return 0.111 * grad_scale * jax.random.normal(key, array_shape, jnp.float32)


def moment_second(key, array_shape, grad_scale):
    factor = jnp.exp(jax.random.uniform(key, array_shape, jnp.float32, 0.0, math.log(4.0)))
    return 0.0526 * grad_scale * grad_scale * factor


def draw_lengths(key, part):
    key = jax.random.fold_in(key, 1)
    devices = TOKENS // TOK_DEV
    span_total = TOK_DEV // SPAN
    cut_bits = jax.random.randint(key, (devices, span_total), 0, 2)
    whole_dev = jax.random.randint(jax.random.fold_in(key, 7), (), 0, devices)
    row_ids = jnp.arange(devices, dtype=jnp.int32)[:, None]
    column = jnp.arange(span_total, dtype=jnp.int32)[None, :]
    cut_bits = jnp.where(row_ids == whole_dev, 0, cut_bits)
    cut_bits = jnp.where(column == 0, 1, cut_bits)
    seq_rank = jnp.cumsum(cut_bits, axis=1) - 1
    counted = (seq_rank[:, :, None] == jnp.arange(span_total, dtype=jnp.int32)[None, None, :]).astype(jnp.int32)
    return (SPAN * jnp.sum(counted, axis=1)).astype(jnp.int32)


def draw_moment_in(key, part):
    key = jax.random.fold_in(key, 2)
    return moment_first(key, (LAYERS, D, PROJ), 0.5 * math.sqrt(TOKENS))


def draw_second_in(key, part):
    key = jax.random.fold_in(key, 3)
    return moment_second(key, (LAYERS, D, PROJ), 0.5 * math.sqrt(TOKENS))


def draw_moment_out(key, part):
    key = jax.random.fold_in(key, 4)
    return moment_first(key, (LAYERS, INNER, D), math.sqrt(TOKENS))


def draw_second_out(key, part):
    key = jax.random.fold_in(key, 5)
    return moment_second(key, (LAYERS, INNER, D), math.sqrt(TOKENS))


def draw_side_moment(key, part):
    key = jax.random.fold_in(key, 6)
    return moment_first(key, (LAYERS, SMALL), math.sqrt(TOKENS))


def draw_side_second(key, part):
    key = jax.random.fold_in(key, 9)
    return moment_second(key, (LAYERS, SMALL), math.sqrt(TOKENS))


def draw_side_params(key, part):
    key = jax.random.fold_in(key, 8)
    subkeys = jax.random.split(key, 7)
    norm_gain = jax.random.uniform(subkeys[0], (LAYERS, D), jnp.float32, 0.6, 1.4)
    gate_gain = jax.random.uniform(subkeys[1], (LAYERS, INNER), jnp.float32, 0.6, 1.4)
    conv_weight = jax.random.uniform(subkeys[2], (LAYERS, CONV * XBC), jnp.float32, -0.5, 0.5)
    conv_bias = jax.random.uniform(subkeys[3], (LAYERS, XBC), jnp.float32, -0.3, 0.3)
    base_step = jnp.exp(jax.random.uniform(subkeys[4], (LAYERS, HEADS), jnp.float32, math.log(0.001), math.log(0.1)))
    dt_bias = jnp.log(jnp.expm1(base_step))
    a_log = jnp.log(jax.random.uniform(subkeys[5], (LAYERS, HEADS), jnp.float32, 1.0, 16.0))
    d_skip = jax.random.uniform(subkeys[6], (LAYERS, HEADS), jnp.float32, 0.5, 1.5)
    return jnp.concatenate([norm_gain, gate_gain, conv_weight, conv_bias, dt_bias, a_log, d_skip], axis=1)


def level_of(stream_key, shape, cuts, least, top_value):
    def one(position, shards_of):
        heights = jax.random.uniform(jax.random.fold_in(jax.random.fold_in(stream_key, 6), position), (shards_of,), jnp.float32, least / len(cuts), top_value / len(cuts))
        return jnp.repeat(jnp.exp(heights), shape[position] // shards_of).reshape((-1,) + (1,) * (len(shape) - position - 1))

    loudness = one(*cuts[0])
    for cut in cuts[1:]:
        loudness = loudness * one(*cut)
    return loudness


def bell_draw(key, extent, width, most, shards=(), held_as=jnp.bfloat16):
    drawn = width * jax.random.normal(key, extent, jnp.float32)
    if shards:
        drawn = drawn * level_of(key, extent, shards, -0.22, 0.18)
    return jnp.clip(drawn, -most, most).astype(held_as)


def setup_inputs(seed: int = 0) -> dict:
    seeds = jax.random.split(jax.random.key(seed), 13)
    tokens = bell_draw(seeds[0], (TOKENS, D), 1.0, 6.0, ((0, 32),))
    cotangent = bell_draw(seeds[1], (TOKENS, D), 1.0, 6.0, ((0, 32),))
    lengths = draw_lengths(jax.random.fold_in(seeds[12], 71), 0)
    weight_in = bell_draw(seeds[3], (LAYERS, D, PROJ), D ** -0.5, 0.15625, ((1, 16),), jnp.float32)
    moment_in = draw_moment_in(jax.random.fold_in(seeds[12], 71), 0)
    second_in = draw_second_in(jax.random.fold_in(seeds[12], 71), 0)
    weight_out = bell_draw(seeds[6], (LAYERS, INNER, D), INNER ** -0.5, 0.109375, ((1, 16),), jnp.float32)
    moment_out = draw_moment_out(jax.random.fold_in(seeds[12], 71), 0)
    second_out = draw_second_out(jax.random.fold_in(seeds[12], 71), 0)
    side_params = draw_side_params(jax.random.fold_in(seeds[12], 71), 0)
    side_moment = draw_side_moment(jax.random.fold_in(seeds[12], 71), 0)
    side_second = draw_side_second(jax.random.fold_in(seeds[12], 71), 0)
    return dict(tokens=tokens, cotangent=cotangent, lengths=lengths, weight_in=weight_in, moment_in=moment_in, second_in=second_in, weight_out=weight_out, moment_out=moment_out, second_out=second_out, side_params=side_params, side_moment=side_moment, side_second=side_second)


EPSILON = 1e-05
BETA_ONE = 0.9
BETA_TWO = 0.95
ADAM_EPSILON = 1e-08
RATE_MATRIX = 0.05
RATE_SIDE = 0.5
DECAY_MATRIX = 0.1
HIGHEST_PRECISION = lax.Precision.HIGHEST

@jax.custom_vjp
def low(v):
    return lax.optimization_barrier(v.astype(jnp.bfloat16)).astype(jnp.float32)

@jax.custom_vjp
def low_back(v):
    return v

def low_keep(v):
    return (low(v), None)

def low_pass(kept, grad):
    return (grad,)

def back_keep(v):
    return (v, None)

def back_low(kept, grad):
    return (low(grad),)
low.defvjp(low_keep, low_pass)
low_back.defvjp(back_keep, back_low)

def span_starts(seq_lengths):
    offsets = jnp.cumsum(seq_lengths) - seq_lengths
    places = jnp.arange(seq_lengths.shape[0], dtype=jnp.int32) * SPAN
    matches = (offsets[None, :] == places[:, None]) & (seq_lengths[None, :] > 0)
    return jnp.any(matches, axis=1)

def unpack(side_row):
    cursor = D + INNER
    gate_gain = side_row[D:cursor]
    conv_weight = side_row[cursor:cursor + CONV * XBC].reshape(CONV, XBC)
    cursor = cursor + CONV * XBC
    conv_bias = side_row[cursor:cursor + XBC]
    cursor = cursor + XBC
    dt_bias = side_row[cursor:cursor + HEADS]
    a_log = side_row[cursor + HEADS:cursor + 2 * HEADS]
    d_skip = side_row[cursor + 2 * HEADS:cursor + 3 * HEADS]
    return (gate_gain, conv_weight, conv_bias, dt_bias, a_log, d_skip)

def prenorm(hidden, side_row):
    inverse = lax.rsqrt(lax.optimization_barrier(jnp.mean(hidden * hidden, axis=-1, keepdims=True)) + EPSILON)
    return hidden * inverse * side_row[:D]

def mixer_core(projected, side_row, starts):
    gate_gain, conv_weight, conv_bias, dt_bias, a_log, d_skip = unpack(side_row)
    token_count = projected.shape[0]
    span_count = token_count // SPAN
    gate_part = projected[:, :INNER]
    conv_in = projected[:, INNER:INNER + XBC]
    dt_raw = projected[:, INNER + XBC:]
    token_index = jnp.arange(token_count, dtype=jnp.int32)
    block_first = jnp.arange(span_count, dtype=jnp.int32) * SPAN
    span_begin = lax.cummax(jnp.where(starts, block_first, jnp.zeros_like(block_first)), axis=0)
    offset = token_index - jnp.repeat(span_begin, SPAN)
    conv_sum = conv_bias + conv_weight[CONV - 1] * conv_in
    for back_step in range(1, CONV):
        shifted = jnp.concatenate([jnp.zeros((back_step, XBC), jnp.float32), conv_in[:-back_step]], axis=0)
        conv_sum = conv_sum + conv_weight[CONV - 1 - back_step] * jnp.where((offset >= back_step)[:, None], shifted, 0.0)
    activated = jax.nn.silu(conv_sum)
    values_all = activated[:, :INNER].reshape(span_count, SPAN, HEADS, HEAD_DIM)
    input_b = activated[:, INNER:INNER + STATE].reshape(span_count, SPAN, STATE)
    output_c = activated[:, INNER + STATE:].reshape(span_count, SPAN, STATE)
    step_sizes = jax.nn.softplus(dt_raw + dt_bias)
    log_decay = -jnp.exp(a_log) * step_sizes
    step_sizes = step_sizes.reshape(span_count, SPAN, HEADS)
    log_decay = log_decay.reshape(span_count, SPAN, HEADS)
    causal = token_index[:SPAN][:, None] >= token_index[:SPAN][None, :]

    def span_step(carry_state, pieces):
        values_span, b_span, c_span, steps_span, decays, begins = pieces
        cumulative = jnp.cumsum(decays, axis=0)
        log_gaps = cumulative[:, None, :] - cumulative[None, :, :]
        weights_tri = jnp.exp(jnp.where(causal[:, :, None], log_gaps, -jnp.inf))
        intersection = jnp.einsum('tn,sn->ts', c_span, b_span, precision=HIGHEST_PRECISION)
        mixing = intersection[:, :, None] * weights_tri * steps_span[None, :, :]
        within = jnp.einsum('tsh,shp->thp', mixing, values_span, precision=HIGHEST_PRECISION)
        prior_state = jnp.where(begins, jnp.zeros_like(carry_state), carry_state)
        carried = jnp.exp(cumulative)[:, :, None] * jnp.einsum('tn,hnp->thp', c_span, prior_state, precision=HIGHEST_PRECISION)
        to_end = jnp.exp(cumulative[-1][None, :] - cumulative) * steps_span
        new_state = jnp.exp(cumulative[-1])[:, None, None] * prior_state + jnp.einsum('sh,sn,shp->hnp', to_end, b_span, values_span, precision=HIGHEST_PRECISION)
        result = within + carried + d_skip[None, :, None] * values_span
        return (new_state, result)
    zero_state = jnp.zeros((HEADS, STATE, HEAD_DIM), jnp.float32)
    _, mixed_out = lax.scan(jax.checkpoint(span_step), zero_state, (values_all, input_b, output_c, step_sizes, log_decay, starts))
    mixed_out = mixed_out.reshape(token_count, INNER)
    gated_out = mixed_out * jax.nn.silu(gate_part)
    inverse = lax.rsqrt(lax.optimization_barrier(jnp.mean(gated_out * gated_out, axis=-1, keepdims=True)) + EPSILON)
    return gated_out * inverse * gate_gain

def layer_block(hidden, starts, weight_in, weight_out, side_row):
    normed = low(prenorm(hidden, side_row))
    projected = low_back(jnp.dot(normed, weight_in, precision=HIGHEST_PRECISION))
    mixed_out = low(mixer_core(projected, side_row, starts))
    branch = low_back(jnp.dot(mixed_out, weight_out, precision=HIGHEST_PRECISION))
    return hidden + branch

def forward(tokens_f, weight_in, weight_out, side_params, starts_all):
    weights_in_low = low(weight_in)
    weights_out_low = low(weight_out)
    devices = tokens_f.shape[0] // TOK_DEV
    hidden = tokens_f.reshape(devices, TOK_DEV, D)
    layer_outs = []
    for layer_idx in range(LAYERS):
        step_fn = jax.checkpoint(partial(layer_block, weight_in=weights_in_low[layer_idx], weight_out=weights_out_low[layer_idx], side_row=side_params[layer_idx]))
        hidden = lax.map(lambda paired, step_fn=step_fn: step_fn(paired[0], paired[1]), (hidden, starts_all))
        layer_outs.append(hidden)
    return jnp.stack(layer_outs).reshape(LAYERS, devices * TOK_DEV, D)

def adamw_step(parameter, first_moment, second_moment, gradient, step_rate, decay_rate):
    first_new = BETA_ONE * first_moment + (1.0 - BETA_ONE) * gradient
    second_new = BETA_TWO * second_moment + (1.0 - BETA_TWO) * gradient * gradient
    correction_one = 1.0 - BETA_ONE ** STEP
    correction_two = 1.0 - BETA_TWO ** STEP
    update = first_new / correction_one / (jnp.sqrt(second_new / correction_two) + ADAM_EPSILON)
    return (parameter - step_rate * (update + decay_rate * parameter), first_new, second_new)

def reference(tokens, cotangent, lengths, weight_in, moment_in, second_in, weight_out, moment_out, second_out, side_params, side_moment, side_second):
    starts_all = jax.vmap(span_starts)(lengths)
    primal, pullback = jax.vjp(lambda tok_f, w_one, w_two, side_all: forward(tok_f, w_one, w_two, side_all, starts_all), tokens.astype(jnp.float32), weight_in, weight_out, side_params)
    zero_rows = jnp.zeros((LAYERS - 1,) + cotangent.shape, jnp.float32)
    cot_full = jnp.concatenate([zero_rows, cotangent.astype(jnp.float32)[None]], axis=0)
    token_grad, grad_in, grad_out, grad_side = pullback(cot_full)
    new_w_in, new_m_in, new_v_in = adamw_step(weight_in, moment_in, second_in, grad_in, RATE_MATRIX, DECAY_MATRIX)
    new_w_out, new_m_out, new_v_out = adamw_step(weight_out, moment_out, second_out, grad_out, RATE_MATRIX, DECAY_MATRIX)
    new_side, new_side_m, new_side_v = adamw_step(side_params, side_moment, side_second, grad_side, RATE_SIDE, 0.0)
    return (primal, token_grad, new_w_in, new_m_in, new_v_in, new_w_out, new_m_out, new_v_out, new_side, new_side_m, new_side_v)
```

```python
from functools import partial

import jax
import jax.numpy as jnp
from jax import lax
from jax.experimental import pallas as pl
from jax.experimental.pallas import tpu as pltpu
from jax.sharding import PartitionSpec as P

D = 1536
LAYERS = 2
STEP = 10
BETA_ONE = 0.9
BETA_TWO = 0.95
ADAM_EPSILON = 1e-08
RATE_MATRIX = 0.05
RATE_SIDE = 0.5
DECAY_MATRIX = 0.1
INNER = 3072
HEAD_DIM = 64
STATE = 128
CONV = 4
SPAN = 256
HEADS = 48
XBC = 3328
TOK = 512
GROUP = 8
WIDE = GROUP * HEAD_DIM
STEPS = HEADS // GROUP
HALO = 8
EPSILON = 1e-05
HIGHEST = lax.Precision.HIGHEST
BF = jnp.bfloat16
F32 = jnp.float32


def dot(a, b, dims=((1,), (0,)), precision=None):
    return lax.dot_general(a, b, (dims, ((), ())), precision=precision, preferred_element_type=F32)


NT = ((1,), (1,))
TN = ((0,), (0,))


def sigmoid(v):
    return 1.0 / (1.0 + jnp.exp(-v))


def softplus(v):
    e = jnp.exp(-jnp.abs(v))
    u = 1.0 + e
    tail = jnp.where(u == 1.0, e, jnp.log(u) * (e / jnp.where(u == 1.0, 1.0, u - 1.0)))
    return jnp.maximum(v, 0.0) + tail


def load_halo(buf, xin, cont, width):
    buf[0:HALO, :width] = jnp.zeros((HALO, width), F32)
    buf[HALO : HALO + SPAN, :width] = xin[0:SPAN]
    buf[HALO + SPAN : 2 * HALO + SPAN, :width] = xin[SPAN - HALO : SPAN] * cont
    buf[2 * HALO + SPAN : 2 * (HALO + SPAN), :width] = xin[SPAN : 2 * SPAN]


def shifted(buf, k, span, width, lo=0, rows=SPAN):
    base = span * (HALO + SPAN) + HALO - k + lo
    return buf[base : base + rows, :width]


def conv_of(buf, cw, span, width, lo=0, rows=SPAN):
    total = cw[4:5, :] + cw[3:4, :] * shifted(buf, 0, span, width, lo, rows)
    for k in range(1, CONV):
        total = total + cw[3 - k : 4 - k, :] * shifted(buf, k, span, width, lo, rows)
    return total


def lower_tri():
    return (
        lax.broadcasted_iota(jnp.int32, (SPAN, SPAN), 0)
        >= lax.broadcasted_iota(jnp.int32, (SPAN, SPAN), 1)
    )


def setup(cont, bc_ref, dt_ref, cwbc_ref, hp_ref, buf, bct, scores, dts, cum, cumt):
    load_halo(buf, bc_ref[...], cont, 2 * STATE)
    for span in range(2):
        lo = span * SPAN
        s = conv_of(buf, cwbc_ref[...], span, 2 * STATE)
        bct[lo : lo + SPAN, :] = (s * sigmoid(s)).astype(BF)
        sc = dot(bct[lo : lo + SPAN, STATE:], bct[lo : lo + SPAN, :STATE], NT)
        scores[lo : lo + SPAN, :] = jnp.where(lower_tri(), sc, 0.0)
    lane = lax.broadcasted_iota(jnp.int32, (TOK, 128), 1)
    raw = jnp.where(lane < HEADS, dt_ref[...], 0.0) + hp_ref[0:1, :]
    step = jnp.where(lane < HEADS, softplus(raw), 0.0)
    dts[...] = step
    a = -jnp.exp(hp_ref[1:2, :]) * step
    tri = jnp.where(lower_tri(), 1.0, 0.0)
    for span in range(2):
        lo = span * SPAN
        cum[lo : lo + SPAN, :] = dot(tri, a[lo : lo + SPAN, :], precision=HIGHEST)
    cumt[...] = cum[...].T


def pair_lanes(col, j, rows):
    lane = lax.broadcasted_iota(jnp.int32, (rows, 2 * HEAD_DIM), 1)
    return jnp.where(lane < HEAD_DIM, col[:, j : j + 1], col[:, j + 1 : j + 2])


def fwd_kernel(
    cont_ref, z_ref, x_ref, bc_ref, dt_ref, cwx_ref, cwbc_ref, hp_ref, cp_ref, gain_ref,
    m_ref, y_ref, inv_ref,
    buf, bct, scores, dts, cum, cumt, mix, xt, g_s, ssq, grp, state,
):
    g = pl.program_id(0)
    cont = cont_ref[0, 0]

    @pl.when(g == 0)
    def _():
        setup(cont, bc_ref, dt_ref, cwbc_ref, hp_ref, buf, bct, scores, dts, cum, cumt)
        ssq[...] = jnp.zeros_like(ssq)

    shift = lax.rem(128 - GROUP * g, 128)
    grp[0] = pltpu.roll(dts[...], shift, 1)
    grp[1] = pltpu.roll(cum[...], shift, 1)
    rows8 = cumt[pl.ds(pl.multiple_of(g * GROUP, GROUP), GROUP), :]
    load_halo(buf, x_ref[...], cont, WIDE)
    for span in range(2):
        lo = span * SPAN
        s = conv_of(buf, cwx_ref[...], span, WIDE)
        x = s * sigmoid(s)
        y_ref[lo : lo + SPAN, :] = x * cp_ref[1:2, :]
        for j in range(0, GROUP, 2):
            c0 = j * HEAD_DIM
            xt[lo : lo + SPAN, c0 : c0 + 128] = x[:, c0 : c0 + 128] * pair_lanes(
                grp[0, lo : lo + SPAN, :], j, SPAN
            )
    last = grp[1, SPAN - 1 : SPAN, :]
    w0 = jnp.exp(last - grp[1, 0:SPAN, :])
    for j in range(0, GROUP, 2):
        c0 = j * HEAD_DIM
        xw = xt[0:SPAN, c0 : c0 + 128] * pair_lanes(w0, j, SPAN)
        st = dot(bct[0:SPAN, :STATE], xw.astype(BF), TN) * cont
        e1 = pair_lanes(jnp.exp(grp[1, SPAN:, :]), j, SPAN)
        y_ref[SPAN:, c0 : c0 + 128] += e1 * dot(bct[SPAN:, STATE:], st.astype(BF))
    for span in range(2):
        lo = span * SPAN
        for j in range(GROUP):
            c0 = j * HEAD_DIM
            slot = j % 2
            fill_mix(mix, slot, scores, grp, rows8, span, j)
            y_ref[lo : lo + SPAN, c0 : c0 + HEAD_DIM] += dot(
                mix[slot], xt[lo : lo + SPAN, c0 : c0 + HEAD_DIM].astype(BF)
            )
    z = z_ref[...]
    gated = y_ref[...] * (z * sigmoid(z))
    g_s[g] = gated
    ssq[...] += jnp.broadcast_to(jnp.sum(gated * gated, axis=1, keepdims=True), ssq.shape)

    @pl.when(g == STEPS - 1)
    def _():
        inv = lax.rsqrt(ssq[...] * (1.0 / INNER) + EPSILON)
        inv_ref[...] = inv
        col = inv[:, 0:1]
        for k in range(STEPS):
            m_ref[:, k * WIDE : (k + 1) * WIDE] = (
                g_s[k] * col * gain_ref[0:1, k * WIDE : (k + 1) * WIDE]
            ).astype(BF)


CHUNK = 64


def fill_mix(mix, slot, scores, grp, rows8, span, j):
    lo = span * SPAN
    for r in range(0, SPAN, CHUNK):
        wide = 128 if r + CHUNK <= 128 else 256
        gap = grp[1, lo + r : lo + r + CHUNK, j : j + 1] - rows8[j : j + 1, lo : lo + wide]
        val = scores[lo + r : lo + r + CHUNK, :wide] * jnp.exp(jnp.minimum(gap, 0.0))
        mix[slot, r : r + CHUNK, :wide] = val.astype(BF)
        if wide < 256:
            mix[slot, r : r + CHUNK, wide:] = jnp.zeros((CHUNK, 256 - wide), BF)


def head_rows(side_row):
    cur = D + INNER + CONV * XBC + XBC
    rows = side_row[cur : cur + 3 * HEADS].reshape(3, HEADS)
    return jnp.pad(rows, ((0, 5), (0, 128 - HEADS)))


def conv_rows(side_row):
    cur = D + INNER
    rows = side_row[cur : cur + (CONV + 1) * XBC].reshape(CONV + 1, XBC)
    return jnp.pad(rows, ((0, 3), (0, 0)))


def column_rows(side_row):
    gain = side_row[D : D + INNER]
    skip = jnp.repeat(side_row[-HEADS:], HEAD_DIM)
    return jnp.pad(jnp.stack([gain, skip]), ((0, 6), (0, 0)))


def mixer_fwd(zx, cont, side_row):
    hp, cw, cp = head_rows(side_row), conv_rows(side_row), column_rows(side_row)
    full = lambda shape: pl.BlockSpec(shape, lambda g: (0,) * len(shape))
    return pl.pallas_call(
        fwd_kernel,
        grid=(STEPS,),
        out_shape=(
            jax.ShapeDtypeStruct((TOK, INNER), BF),
            jax.ShapeDtypeStruct((TOK, INNER), F32),
            jax.ShapeDtypeStruct((TOK, 128), F32),
        ),
        in_specs=[
            pl.BlockSpec(memory_space=pltpu.SMEM),
            pl.BlockSpec((TOK, WIDE), lambda g: (0, g)),
            pl.BlockSpec((TOK, WIDE), lambda g: (0, STEPS + g)),
            pl.BlockSpec((TOK, 2 * STATE), lambda g: (0, 2 * INNER // (2 * STATE))),
            pl.BlockSpec((TOK, 128), lambda g: (0, (INNER + XBC) // 128)),
            pl.BlockSpec((8, WIDE), lambda g: (0, g)),
            pl.BlockSpec((8, 2 * STATE), lambda g: (0, INNER // (2 * STATE))),
            full((8, 128)),
            pl.BlockSpec((8, WIDE), lambda g: (0, g)),
            full((8, INNER)),
        ],
        out_specs=(
            full((TOK, INNER)),
            pl.BlockSpec((TOK, WIDE), lambda g: (0, g)),
            full((TOK, 128)),
        ),
        scratch_shapes=[
            pltpu.VMEM((2 * (HALO + SPAN), WIDE), F32),
            pltpu.VMEM((TOK, 2 * STATE), BF),
            pltpu.VMEM((TOK, SPAN), F32),
            pltpu.VMEM((TOK, 128), F32),
            pltpu.VMEM((TOK, 128), F32),
            pltpu.VMEM((128, TOK), F32),
            pltpu.VMEM((2, SPAN, SPAN), BF),
            pltpu.VMEM((TOK, WIDE), F32),
            pltpu.VMEM((STEPS, TOK, WIDE), F32),
            pltpu.VMEM((TOK, 128), F32),
            pltpu.VMEM((2, TOK, 128), F32),
            pltpu.VMEM((STATE, WIDE), F32),
        ],
        compiler_params=pltpu.CompilerParams(vmem_limit_bytes=48 * 2**20),
        cost_estimate=pl.CostEstimate(flops=6 * 10**9, bytes_accessed=25 * 2**20, transcendentals=10**7),
        name="mixer_fwd",
    )(cont, zx, zx, zx, zx, cw, cw, hp, cp, cp)


def bwd_kernel(
    cont_ref, z_ref, x_ref, bc_ref, dt_ref, cwx_ref, cwbc_ref, hp_ref, cp_ref, y_ref, dm_ref, row_ref,
    dz_ref, dx_ref, dbc_ref, dcol_ref, dcw_ref, dcwbc_ref, dhp_ref,
    buf, bct, scores, dts, cum, cumt, mix, decay, xt, xf, sig, dy, dxt, dscore, dbcs, dcum, ddt, grp,
):
    g = pl.program_id(0)
    cont = cont_ref[0, 0]

    @pl.when(g == 0)
    def _():
        setup(cont, bc_ref, dt_ref, cwbc_ref, hp_ref, buf, bct, scores, dts, cum, cumt)
        dscore[...] = jnp.zeros_like(dscore)
        dbcs[...] = jnp.zeros_like(dbcs)
        dcum[...] = jnp.zeros_like(dcum)
        ddt[...] = jnp.zeros_like(ddt)

    shift = lax.rem(128 - GROUP * g, 128)
    grp[0] = pltpu.roll(dts[...], shift, 1)
    grp[1] = pltpu.roll(cum[...], shift, 1)
    rows8 = cumt[pl.ds(pl.multiple_of(g * GROUP, GROUP), GROUP), :]
    load_halo(buf, x_ref[...], cont, WIDE)
    gain = cp_ref[0:1, :]
    skip = cp_ref[1:2, :]
    dcol_ref[...] = jnp.zeros_like(dcol_ref)
    pick = jnp.where(
        lax.broadcasted_iota(jnp.int32, (WIDE, 128), 0) // HEAD_DIM + GROUP * g
        == lax.broadcasted_iota(jnp.int32, (WIDE, 128), 1),
        1.0,
        0.0,
    )
    for span in range(2):
        lo = span * SPAN
        hi = lo + SPAN
        s = conv_of(buf, cwx_ref[...], span, WIDE)
        sg = sigmoid(s)
        x = s * sg
        xf[lo:hi, :] = x
        sig[lo:hi, :] = sg * (1.0 + s * (1.0 - sg))
        for j in range(0, GROUP, 2):
            c0 = j * HEAD_DIM
            xt[lo:hi, c0 : c0 + 128] = x[:, c0 : c0 + 128] * pair_lanes(grp[0, lo:hi, :], j, SPAN)
        z = z_ref[lo:hi, :]
        sz = sigmoid(z)
        gate = z * sz
        y = y_ref[lo:hi, :]
        inv = row_ref[lo:hi, 0:1]
        gn = y * gate * inv
        dm = dm_ref[lo:hi, :]
        dcol_ref[0:1, :] += jnp.sum(dm * gn, axis=0, keepdims=True)
        dg = inv * (dm * gain - gn * row_ref[lo:hi, 1:2])
        dz_ref[lo:hi, :] = (dg * y * (sz * (1.0 + z * (1.0 - sz)))).astype(BF)
        dyv = dg * gate
        dcol_ref[1:2, :] += jnp.sum(dyv * x, axis=0, keepdims=True)
        dy[lo:hi, :] = dyv
        yin = y - skip * x
        dcum[lo:hi, :] += dot(dyv.astype(BF).astype(F32) * yin, pick, precision=HIGHEST)

    last = grp[1, SPAN - 1 : SPAN, :]
    w0 = jnp.exp(last - grp[1, 0:SPAN, :])
    ecum1 = jnp.exp(grp[1, SPAN:, :])
    for j in range(0, GROUP, 2):
        cs = slice(j * HEAD_DIM, j * HEAD_DIM + 128)
        wl = pair_lanes(w0, j, SPAN)
        xw = (xt[0:SPAN, cs] * wl).astype(BF)
        prior = (dot(bct[0:SPAN, :STATE], xw, TN) * cont).astype(BF)
        dye = (dy[SPAN:, cs] * pair_lanes(ecum1, j, SPAN)).astype(BF)
        dprior = (dot(bct[SPAN:, STATE:], dye, TN) * cont).astype(BF)
        dbcs[SPAN:, STATE:] += dot(dye, prior, NT)
        dbcs[0:SPAN, :STATE] += dot(xw, dprior, NT)
        v = dot(bct[0:SPAN, :STATE], dprior) * wl
        dxt[0:SPAN, cs] = v
        dxt[SPAN:, cs] = jnp.zeros((SPAN, 128), F32)
    through = dxt[0:SPAN, :] * xt[0:SPAN, :]
    dcum[SPAN - 1 : SPAN, :] += dot(jnp.sum(through, axis=0, keepdims=True), pick, precision=HIGHEST)

    for span in range(2):
        lo = span * SPAN
        hi = lo + SPAN
        for j in range(0, GROUP, 2):
            cs = slice(j * HEAD_DIM, j * HEAD_DIM + 128)
            dyp = dy[lo:hi, cs]
            dyb = dyp.astype(BF)
            dyt = dyp.T.astype(BF)
            xtb = xt[lo:hi, cs].astype(BF)
            parts = []
            for i in range(2):
                hs = slice(i * HEAD_DIM, (i + 1) * HEAD_DIM)
                fill_both(mix, decay, i, scores, grp, rows8, span, j + i)
                dmix = dot(dyb[:, hs], xtb[:, hs], NT)
                dscore[lo:hi, :] += dmix * decay[...]
                parts.append(dot(dyt[hs, :], mix[i]))
            dxt[lo:hi, cs] += jnp.concatenate(parts, axis=0).T

    load_back = []
    dcw_ref[...] = jnp.zeros_like(dcw_ref)
    for span in range(2):
        lo = span * SPAN
        hi = lo + SPAN
        x = xf[lo:hi, :]
        xtv = xt[lo:hi, :]
        dv = dxt[lo:hi, :]
        dcum[lo:hi, :] -= dot(dv * xtv.astype(BF).astype(F32), pick, precision=HIGHEST)
        ddt[lo:hi, :] += dot(dv * x, pick, precision=HIGHEST)
        for j in range(0, GROUP, 2):
            cs = slice(j * HEAD_DIM, j * HEAD_DIM + 128)
            dc = dxt[lo:hi, cs] * pair_lanes(grp[0, lo:hi, :], j, SPAN) + dy[lo:hi, cs] * skip[:, cs]
            dxt[lo:hi, cs] = dc * sig[lo:hi, cs]
        conv_weights(dcw_ref, buf, dxt[lo:hi, :], span, WIDE)
    back_halo(buf, dxt[...], cont, WIDE)
    for span in range(2):
        lo = span * SPAN
        dx_ref[lo : lo + SPAN, :] = conv_back(buf, cwx_ref[...], span, WIDE).astype(BF)

    @pl.when(g == STEPS - 1)
    def _():
        load_halo(buf, bc_ref[...], cont, 2 * STATE)
        dcwbc_ref[...] = jnp.zeros_like(dcwbc_ref)
        for span in range(2):
            lo = span * SPAN
            hi = lo + SPAN
            ds = jnp.where(lower_tri(), dscore[lo:hi, :], 0.0).astype(BF)
            dbcs[lo:hi, :STATE] += dot(ds, bct[lo:hi, STATE:], TN)
            dbcs[lo:hi, STATE:] += dot(ds, bct[lo:hi, :STATE])
            s = conv_of(buf, cwbc_ref[...], span, 2 * STATE)
            sg = sigmoid(s)
            dcv = dbcs[lo:hi, :] * (sg * (1.0 + s * (1.0 - sg)))
            dbcs[lo:hi, :] = dcv
            conv_weights(dcwbc_ref, buf, dcv, span, 2 * STATE)
        back_halo(buf, dbcs[...], cont, 2 * STATE)
        for span in range(2):
            lo = span * SPAN
            dbc_ref[lo : lo + SPAN, : 2 * STATE] = conv_back(buf, cwbc_ref[...], span, 2 * STATE).astype(BF)
        lane = lax.broadcasted_iota(jnp.int32, (TOK, 128), 1)
        raw = jnp.where(lane < HEADS, dt_ref[...], 0.0) + hp_ref[0:1, :]
        decay_rate = -jnp.exp(hp_ref[1:2, :])
        tri = jnp.where(lower_tri(), 1.0, 0.0)
        da = jnp.concatenate(
            [dot(tri, dcum[lo : lo + SPAN, :], TN, HIGHEST) for lo in (0, SPAN)], axis=0
        )
        draw = jnp.where(lane < HEADS, (ddt[...] + decay_rate * da) * sigmoid(raw), 0.0)
        dbc_ref[:, 2 * STATE :] = draw.astype(BF)
        dhp_ref[...] = jnp.zeros_like(dhp_ref)
        dhp_ref[0:1, :] = jnp.sum(draw, axis=0, keepdims=True)
        dhp_ref[1:2, :] = jnp.sum(da * decay_rate * dts[...], axis=0, keepdims=True)


def conv_weights(out, buf, dcv, span, width):
    for k in range(CONV):
        out[3 - k : 4 - k, :] += jnp.sum(dcv * shifted(buf, k, span, width), axis=0, keepdims=True)
    out[4:5, :] += jnp.sum(dcv, axis=0, keepdims=True)


def back_halo(buf, dcv, cont, width):
    buf[0:SPAN, :width] = dcv[0:SPAN]
    buf[SPAN : SPAN + HALO, :width] = dcv[SPAN : SPAN + HALO] * cont
    buf[SPAN + HALO : 2 * SPAN + HALO, :width] = dcv[SPAN:]
    buf[2 * SPAN + HALO : 2 * (SPAN + HALO), :width] = jnp.zeros((HALO, width), F32)


def conv_back(buf, cw, span, width):
    base = span * (SPAN + HALO)
    total = cw[3:4, :] * buf[base : base + SPAN, :width]
    for k in range(1, CONV):
        total = total + cw[3 - k : 4 - k, :] * buf[base + k : base + k + SPAN, :width]
    return total


def fill_both(mix, decay, slot, scores, grp, rows8, span, j):
    lo = span * SPAN
    for r in range(0, SPAN, CHUNK):
        wide = 128 if r + CHUNK <= 128 else 256
        gap = grp[1, lo + r : lo + r + CHUNK, j : j + 1] - rows8[j : j + 1, lo : lo + wide]
        e = jnp.exp(jnp.minimum(gap, 0.0))
        decay[r : r + CHUNK, :wide] = e
        mix[slot, r : r + CHUNK, :wide] = (scores[lo + r : lo + r + CHUNK, :wide] * e).astype(BF)
        if wide < 256:
            mix[slot, r : r + CHUNK, wide:] = jnp.zeros((CHUNK, 256 - wide), BF)
            decay[r : r + CHUNK, wide:] = jnp.zeros((CHUNK, 256 - wide), F32)


def mixer_bwd(zx, cont, side_row, y, dm, rows):
    hp, cw, cp = head_rows(side_row), conv_rows(side_row), column_rows(side_row)
    full = lambda shape: pl.BlockSpec(shape, lambda g: (0,) * len(shape))
    by_g = lambda rows_: pl.BlockSpec((rows_, WIDE), lambda g: (0, g))
    dz, dx, dbc, dcol, dcw, dcwbc, dhp = pl.pallas_call(
        bwd_kernel,
        grid=(STEPS,),
        out_shape=(
            jax.ShapeDtypeStruct((TOK, INNER), BF),
            jax.ShapeDtypeStruct((TOK, INNER), BF),
            jax.ShapeDtypeStruct((TOK, 2 * STATE + 128), BF),
            jax.ShapeDtypeStruct((8, INNER), F32),
            jax.ShapeDtypeStruct((8, INNER), F32),
            jax.ShapeDtypeStruct((8, 2 * STATE), F32),
            jax.ShapeDtypeStruct((8, 128), F32),
        ),
        in_specs=[
            pl.BlockSpec(memory_space=pltpu.SMEM),
            by_g(TOK),
            pl.BlockSpec((TOK, WIDE), lambda g: (0, STEPS + g)),
            pl.BlockSpec((TOK, 2 * STATE), lambda g: (0, 2 * INNER // (2 * STATE))),
            pl.BlockSpec((TOK, 128), lambda g: (0, (INNER + XBC) // 128)),
            by_g(8),
            pl.BlockSpec((8, 2 * STATE), lambda g: (0, INNER // (2 * STATE))),
            full((8, 128)),
            by_g(8),
            by_g(TOK),
            by_g(TOK),
            full((TOK, 128)),
        ],
        out_specs=(
            by_g(TOK),
            by_g(TOK),
            full((TOK, 2 * STATE + 128)),
            by_g(8),
            by_g(8),
            full((8, 2 * STATE)),
            full((8, 128)),
        ),
        scratch_shapes=[
            pltpu.VMEM((2 * (HALO + SPAN), WIDE), F32),
            pltpu.VMEM((TOK, 2 * STATE), BF),
            pltpu.VMEM((TOK, SPAN), F32),
            pltpu.VMEM((TOK, 128), F32),
            pltpu.VMEM((TOK, 128), F32),
            pltpu.VMEM((128, TOK), F32),
            pltpu.VMEM((2, SPAN, SPAN), BF),
            pltpu.VMEM((SPAN, SPAN), F32),
            pltpu.VMEM((TOK, WIDE), F32),
            pltpu.VMEM((TOK, WIDE), F32),
            pltpu.VMEM((TOK, WIDE), F32),
            pltpu.VMEM((TOK, WIDE), F32),
            pltpu.VMEM((TOK, WIDE), F32),
            pltpu.VMEM((TOK, SPAN), F32),
            pltpu.VMEM((TOK, 2 * STATE), F32),
            pltpu.VMEM((TOK, 128), F32),
            pltpu.VMEM((TOK, 128), F32),
            pltpu.VMEM((2, TOK, 128), F32),
        ],
        compiler_params=pltpu.CompilerParams(vmem_limit_bytes=48 * 2**20),
        cost_estimate=pl.CostEstimate(flops=12 * 10**9, bytes_accessed=40 * 2**20, transcendentals=2 * 10**7),
        name="mixer_bwd",
    )(cont, zx, zx, zx, zx, cw, cw, hp, cp, y, dm, rows)
    dskip = jnp.sum(dcol[1].reshape(HEADS, HEAD_DIM), axis=1)
    side = jnp.concatenate(
        [
            dcol[0],
            jnp.concatenate([dcw[: CONV + 1], dcwbc[: CONV + 1]], axis=1).reshape(-1),
            dhp[0, :HEADS],
            dhp[1, :HEADS],
            dskip,
        ]
    )
    return dz, dx, dbc, side


def span_starts(seq_lengths):
    offsets = jnp.cumsum(seq_lengths) - seq_lengths
    places = jnp.arange(seq_lengths.shape[0], dtype=jnp.int32) * SPAN
    matches = (offsets[None, :] == places[:, None]) & (seq_lengths[None, :] > 0)
    return jnp.any(matches, axis=1)


def prenorm(hidden, gain):
    inverse = lax.rsqrt(jnp.mean(hidden * hidden, axis=-1, keepdims=True) + EPSILON)
    return hidden * inverse * gain


def swap(value, axis, count, bit):
    return lax.ppermute(value, axis, [(i, i ^ bit) for i in range(count)])


def sum_everywhere(value, reps, shards):
    for axis, count in (("shard", shards), ("rep", reps)):
        bit = 1
        while bit < count:
            value = value + swap(value, axis, count, bit)
            bit *= 2
    return value


def adamw_step(parameter, first_moment, second_moment, gradient, step_rate, decay_rate):
    first_new = BETA_ONE * first_moment + (1.0 - BETA_ONE) * gradient
    second_new = BETA_TWO * second_moment + (1.0 - BETA_TWO) * gradient * gradient
    correction_one = 1.0 - BETA_ONE**STEP
    correction_two = 1.0 - BETA_TWO**STEP
    update = first_new / correction_one / (jnp.sqrt(second_new / correction_two) + ADAM_EPSILON)
    return (parameter - step_rate * (update + decay_rate * parameter), first_new, second_new)


def reduce_owner(partial_sum, reps):
    mine = lax.psum_scatter(partial_sum.astype(BF), "shard", scatter_dimension=0, tiled=True)
    total = mine.astype(F32)
    for bit in [1 << k for k in range(reps.bit_length() - 1)]:
        total = total + swap(total.astype(BF), "rep", reps, bit).astype(F32)
    return total


def per_device(
    tokens, cotangent, lengths,
    weight_in, moment_in, second_in,
    weight_out, moment_out, second_out,
    side_params, side_moment, side_second,
    *, reps, shards,
):
    cont = jnp.where(span_starts(lengths[0])[1], 0.0, 1.0).astype(F32).reshape(1, 1)
    hidden = tokens.astype(F32)
    saved = []
    layer_outs = []
    for layer in range(LAYERS):
        full_in = lax.all_gather(weight_in[layer].astype(BF), "shard", axis=0, tiled=True)
        full_out = lax.all_gather(weight_out[layer].astype(BF), "shard", axis=0, tiled=True)
        normed, norm_pull = jax.vjp(prenorm, hidden, side_params[layer, :D])
        normed = normed.astype(BF)
        zx = jnp.dot(normed, full_in, preferred_element_type=F32)
        mixed, y, inverse = mixer_fwd(zx, cont, side_params[layer])
        branch = jnp.dot(mixed, full_out, preferred_element_type=F32)
        hidden = hidden + branch
        layer_outs.append(hidden)
        saved.append((full_in, full_out, norm_pull, normed, zx, mixed, y, inverse, branch))
    gradient = cotangent.astype(F32)
    side_total = [None] * LAYERS
    reduced = [None] * LAYERS
    for layer in reversed(range(LAYERS)):
        full_in, full_out, norm_pull, normed, zx, mixed, y, inverse, branch = saved[layer]
        low = gradient.astype(BF)
        grad_out = reduce_owner(dot(mixed, low, TN), reps)
        back = dot(low, full_out, NT)
        factor = jnp.sum(low.astype(F32) * branch, axis=1, keepdims=True) * (1.0 / INNER)
        rows = jnp.concatenate([inverse[:, :1], factor, jnp.zeros((TOK, 126), F32)], axis=1)
        dz, dx, dbc, side_mixer = mixer_bwd(zx, cont, side_params[layer], y, back, rows)
        dzx = jnp.concatenate([dz, dx, dbc[:, : 2 * STATE + HEADS]], axis=1)
        back_normed = dot(dzx, full_in, NT)
        grad_in = reduce_owner(dot(normed, dzx, TN), reps)
        back_hidden, side_norm = norm_pull(back_normed)
        side_total[layer] = sum_everywhere(jnp.concatenate([side_norm, side_mixer]), reps, shards)
        reduced[layer] = (grad_in, grad_out)
        gradient = gradient + back_hidden
    new_in = [
        adamw_step(weight_in[l], moment_in[l], second_in[l], reduced[l][0], RATE_MATRIX, DECAY_MATRIX)
        for l in range(LAYERS)
    ]
    new_out = [
        adamw_step(weight_out[l], moment_out[l], second_out[l], reduced[l][1], RATE_MATRIX, DECAY_MATRIX)
        for l in range(LAYERS)
    ]
    new_side = adamw_step(side_params, side_moment, side_second, jnp.stack(side_total), RATE_SIDE, 0.0)
    return (
        jnp.stack(layer_outs),
        gradient,
        *(jnp.stack([new_in[l][k] for l in range(LAYERS)]) for k in range(3)),
        *(jnp.stack([new_out[l][k] for l in range(LAYERS)]) for k in range(3)),
        *new_side,
    )


def solution(mesh):
    rows = P(("rep", "shard"), None)
    owned = P(None, "shard", None)
    body = partial(per_device, reps=mesh.shape["rep"], shards=mesh.shape["shard"])
    return jax.shard_map(
        body,
        mesh=mesh,
        in_specs=(rows, rows, rows) + (owned,) * 6 + (P(),) * 3,
        out_specs=(P(None, ("rep", "shard"), None), rows) + (owned,) * 6 + (P(),) * 3,
        check_vma=False,
    )
```

```python
from functools import partial

import jax
import jax.numpy as jnp
from jax import lax
from jax.experimental import pallas as pl
from jax.experimental.pallas import tpu as pltpu
from jax.sharding import PartitionSpec as P

LAYERS = 2
STEP = 10
BETA_ONE = 0.9
BETA_TWO = 0.95
ADAM_EPSILON = 1e-08
RATE_MATRIX = 0.05
RATE_SIDE = 0.5
DECAY_MATRIX = 0.1
D = 1536
INNER = 3072
HEAD_DIM = 64
STATE = 128
CONV = 4
SPAN = 256
HEADS = 48
XBC = 3328
TOK = 512
GROUP = 8
WIDE = GROUP * HEAD_DIM
STEPS = HEADS // GROUP
HALO = 8
EPSILON = 1e-05
HIGHEST = lax.Precision.HIGHEST
BF = jnp.bfloat16
F32 = jnp.float32


def dot(a, b, dims=((1,), (0,)), precision=None):
    return lax.dot_general(a, b, (dims, ((), ())), precision=precision, preferred_element_type=F32)


NT = ((1,), (1,))
TN = ((0,), (0,))


def sigmoid(v):
    return 1.0 / (1.0 + jnp.exp(-v))


def softplus(v):
    e = jnp.exp(-jnp.abs(v))
    u = 1.0 + e
    tail = jnp.where(u == 1.0, e, jnp.log(u) * (e / jnp.where(u == 1.0, 1.0, u - 1.0)))
    return jnp.maximum(v, 0.0) + tail


def load_halo(buf, xin, cont, width):
    buf[0:HALO, :width] = jnp.zeros((HALO, width), F32)
    buf[HALO : HALO + SPAN, :width] = xin[0:SPAN]
    buf[HALO + SPAN : 2 * HALO + SPAN, :width] = xin[SPAN - HALO : SPAN] * cont
    buf[2 * HALO + SPAN : 2 * (HALO + SPAN), :width] = xin[SPAN : 2 * SPAN]


def shifted(buf, k, span, width, lo=0, rows=SPAN):
    base = span * (HALO + SPAN) + HALO - k + lo
    return buf[base : base + rows, :width]


def conv_of(buf, cw, span, width, lo=0, rows=SPAN):
    total = cw[4:5, :] + cw[3:4, :] * shifted(buf, 0, span, width, lo, rows)
    for k in range(1, CONV):
        total = total + cw[3 - k : 4 - k, :] * shifted(buf, k, span, width, lo, rows)
    return total


def lower_tri():
    return (
        lax.broadcasted_iota(jnp.int32, (SPAN, SPAN), 0)
        >= lax.broadcasted_iota(jnp.int32, (SPAN, SPAN), 1)
    )


def setup(cont, bc_ref, dt_ref, cwbc_ref, hp_ref, buf, bct, scores, dts, cum, cumt):
    load_halo(buf, bc_ref[...], cont, 2 * STATE)
    for span in range(2):
        lo = span * SPAN
        s = conv_of(buf, cwbc_ref[...], span, 2 * STATE)
        bct[lo : lo + SPAN, :] = (s * sigmoid(s)).astype(BF)
        sc = dot(bct[lo : lo + SPAN, STATE:], bct[lo : lo + SPAN, :STATE], NT)
        scores[lo : lo + SPAN, :] = jnp.where(lower_tri(), sc, 0.0)
    lane = lax.broadcasted_iota(jnp.int32, (TOK, 128), 1)
    raw = jnp.where(lane < HEADS, dt_ref[...], 0.0) + hp_ref[0:1, :]
    step = jnp.where(lane < HEADS, softplus(raw), 0.0)
    dts[...] = step
    a = -jnp.exp(hp_ref[1:2, :]) * step
    tri = jnp.where(lower_tri(), 1.0, 0.0)
    for span in range(2):
        lo = span * SPAN
        cum[lo : lo + SPAN, :] = dot(tri, a[lo : lo + SPAN, :], precision=HIGHEST)
    cumt[...] = cum[...].T


def pair_lanes(col, j, rows):
    lane = lax.broadcasted_iota(jnp.int32, (rows, 2 * HEAD_DIM), 1)
    return jnp.where(lane < HEAD_DIM, col[:, j : j + 1], col[:, j + 1 : j + 2])


def fwd_kernel(
    cont_ref, z_ref, x_ref, bc_ref, dt_ref, cwx_ref, cwbc_ref, hp_ref, cp_ref, gain_ref,
    m_ref, y_ref, inv_ref,
    buf, bct, scores, dts, cum, cumt, mix, xt, g_s, ssq, grp, state,
):
    g = pl.program_id(0)
    cont = cont_ref[0, 0]

    @pl.when(g == 0)
    def _():
        setup(cont, bc_ref, dt_ref, cwbc_ref, hp_ref, buf, bct, scores, dts, cum, cumt)
        ssq[...] = jnp.zeros_like(ssq)

    shift = lax.rem(128 - GROUP * g, 128)
    grp[0] = pltpu.roll(dts[...], shift, 1)
    grp[1] = pltpu.roll(cum[...], shift, 1)
    rows8 = cumt[pl.ds(pl.multiple_of(g * GROUP, GROUP), GROUP), :]
    load_halo(buf, x_ref[...], cont, WIDE)
    for span in range(2):
        lo = span * SPAN
        s = conv_of(buf, cwx_ref[...], span, WIDE)
        x = s * sigmoid(s)
        y_ref[lo : lo + SPAN, :] = x * cp_ref[1:2, :]
        for j in range(0, GROUP, 2):
            c0 = j * HEAD_DIM
            xt[lo : lo + SPAN, c0 : c0 + 128] = x[:, c0 : c0 + 128] * pair_lanes(
                grp[0, lo : lo + SPAN, :], j, SPAN
            )
    last = grp[1, SPAN - 1 : SPAN, :]
    w0 = jnp.exp(last - grp[1, 0:SPAN, :])
    for j in range(0, GROUP, 2):
        c0 = j * HEAD_DIM
        xw = xt[0:SPAN, c0 : c0 + 128] * pair_lanes(w0, j, SPAN)
        st = dot(bct[0:SPAN, :STATE], xw.astype(BF), TN) * cont
        e1 = pair_lanes(jnp.exp(grp[1, SPAN:, :]), j, SPAN)
        y_ref[SPAN:, c0 : c0 + 128] += e1 * dot(bct[SPAN:, STATE:], st.astype(BF))
    for span in range(2):
        lo = span * SPAN
        for j in range(GROUP):
            c0 = j * HEAD_DIM
            slot = j % 2
            fill_mix(mix, slot, scores, grp, rows8, span, j)
            y_ref[lo : lo + SPAN, c0 : c0 + HEAD_DIM] += dot(
                mix[slot], xt[lo : lo + SPAN, c0 : c0 + HEAD_DIM].astype(BF)
            )
    z = z_ref[...]
    gated = y_ref[...] * (z * sigmoid(z))
    g_s[g] = gated
    ssq[...] += jnp.broadcast_to(jnp.sum(gated * gated, axis=1, keepdims=True), ssq.shape)

    @pl.when(g == STEPS - 1)
    def _():
        inv = lax.rsqrt(ssq[...] * (1.0 / INNER) + EPSILON)
        inv_ref[...] = inv
        col = inv[:, 0:1]
        for k in range(STEPS):
            m_ref[:, k * WIDE : (k + 1) * WIDE] = (
                g_s[k] * col * gain_ref[0:1, k * WIDE : (k + 1) * WIDE]
            ).astype(BF)


CHUNK = 64


def fill_mix(mix, slot, scores, grp, rows8, span, j):
    lo = span * SPAN
    for r in range(0, SPAN, CHUNK):
        wide = 128 if r + CHUNK <= 128 else 256
        gap = grp[1, lo + r : lo + r + CHUNK, j : j + 1] - rows8[j : j + 1, lo : lo + wide]
        val = scores[lo + r : lo + r + CHUNK, :wide] * jnp.exp(jnp.minimum(gap, 0.0))
        mix[slot, r : r + CHUNK, :wide] = val.astype(BF)
        if wide < 256:
            mix[slot, r : r + CHUNK, wide:] = jnp.zeros((CHUNK, 256 - wide), BF)


def head_rows(side_row):
    cur = D + INNER + CONV * XBC + XBC
    rows = side_row[cur : cur + 3 * HEADS].reshape(3, HEADS)
    return jnp.pad(rows, ((0, 5), (0, 128 - HEADS)))


def conv_rows(side_row):
    cur = D + INNER
    rows = side_row[cur : cur + (CONV + 1) * XBC].reshape(CONV + 1, XBC)
    return jnp.pad(rows, ((0, 3), (0, 0)))


def column_rows(side_row):
    gain = side_row[D : D + INNER]
    skip = jnp.repeat(side_row[-HEADS:], HEAD_DIM)
    return jnp.pad(jnp.stack([gain, skip]), ((0, 6), (0, 0)))


def mixer_fwd(zx, cont, side_row):
    hp, cw, cp = head_rows(side_row), conv_rows(side_row), column_rows(side_row)
    full = lambda shape: pl.BlockSpec(shape, lambda g: (0,) * len(shape))
    return pl.pallas_call(
        fwd_kernel,
        grid=(STEPS,),
        out_shape=(
            jax.ShapeDtypeStruct((TOK, INNER), BF),
            jax.ShapeDtypeStruct((TOK, INNER), F32),
            jax.ShapeDtypeStruct((TOK, 128), F32),
        ),
        in_specs=[
            pl.BlockSpec(memory_space=pltpu.SMEM),
            pl.BlockSpec((TOK, WIDE), lambda g: (0, g)),
            pl.BlockSpec((TOK, WIDE), lambda g: (0, STEPS + g)),
            pl.BlockSpec((TOK, 2 * STATE), lambda g: (0, 2 * INNER // (2 * STATE))),
            pl.BlockSpec((TOK, 128), lambda g: (0, (INNER + XBC) // 128)),
            pl.BlockSpec((8, WIDE), lambda g: (0, g)),
            pl.BlockSpec((8, 2 * STATE), lambda g: (0, INNER // (2 * STATE))),
            full((8, 128)),
            pl.BlockSpec((8, WIDE), lambda g: (0, g)),
            full((8, INNER)),
        ],
        out_specs=(
            full((TOK, INNER)),
            pl.BlockSpec((TOK, WIDE), lambda g: (0, g)),
            full((TOK, 128)),
        ),
        scratch_shapes=[
            pltpu.VMEM((2 * (HALO + SPAN), WIDE), F32),
            pltpu.VMEM((TOK, 2 * STATE), BF),
            pltpu.VMEM((TOK, SPAN), F32),
            pltpu.VMEM((TOK, 128), F32),
            pltpu.VMEM((TOK, 128), F32),
            pltpu.VMEM((128, TOK), F32),
            pltpu.VMEM((2, SPAN, SPAN), BF),
            pltpu.VMEM((TOK, WIDE), F32),
            pltpu.VMEM((STEPS, TOK, WIDE), F32),
            pltpu.VMEM((TOK, 128), F32),
            pltpu.VMEM((2, TOK, 128), F32),
            pltpu.VMEM((STATE, WIDE), F32),
        ],
        compiler_params=pltpu.CompilerParams(vmem_limit_bytes=48 * 2**20),
        cost_estimate=pl.CostEstimate(flops=6 * 10**9, bytes_accessed=25 * 2**20, transcendentals=10**7),
        name="mixer_fwd",
    )(cont, zx, zx, zx, zx, cw, cw, hp, cp, cp)


def gate_kernel(low_ref, w_ref, z_ref, cp_ref, y_ref, row_ref, dz_ref, dy_ref, dgain_ref):
    dm = dot(low_ref[...], w_ref[...], NT)
    z = z_ref[...]
    sz = sigmoid(z)
    gate = z * sz
    y = y_ref[...]
    inv = row_ref[:, 0:1]
    gn = y * gate * inv
    dgain_ref[...] = jnp.zeros_like(dgain_ref)
    dgain_ref[0:1, :] = jnp.sum(dm * gn, axis=0, keepdims=True)
    dg = inv * (dm * cp_ref[0:1, :] - gn * row_ref[:, 1:2])
    dz_ref[...] = (dg * y * (sz * (1.0 + z * (1.0 - sz)))).astype(BF)
    dy_ref[...] = dg * gate


def gate_bwd(low, full_out, zx, side_row, y, rows):
    cp = column_rows(side_row)
    by_g = lambda rows_: pl.BlockSpec((rows_, WIDE), lambda g: (0, g))
    full = lambda shape: pl.BlockSpec(shape, lambda g: (0,) * len(shape))
    return pl.pallas_call(
        gate_kernel,
        grid=(STEPS,),
        out_shape=(
            jax.ShapeDtypeStruct((TOK, INNER), BF),
            jax.ShapeDtypeStruct((TOK, INNER), F32),
            jax.ShapeDtypeStruct((8, INNER), F32),
        ),
        in_specs=[
            full((TOK, D)),
            pl.BlockSpec((WIDE, D), lambda g: (g, 0)),
            by_g(TOK),
            by_g(8),
            by_g(TOK),
            full((TOK, 128)),
        ],
        out_specs=(by_g(TOK), by_g(TOK), by_g(8)),
        compiler_params=pltpu.CompilerParams(vmem_limit_bytes=48 * 2**20),
        cost_estimate=pl.CostEstimate(flops=5 * 10**9, bytes_accessed=40 * 2**20, transcendentals=2 * 10**6),
        name="gate_bwd",
    )(low, full_out, zx, cp, y, rows)


def bwd_kernel(
    first, last_call,
    cont_ref, x_ref, bc_ref, dt_ref, cwx_ref, cwbc_ref, hp_ref, cp_ref, y_ref, dy, wide_in, narrow_in,
    dx_ref, dskip_ref, dcw_ref, *rest,
):
    if last_call:
        (dbc_ref, dcwbc_ref, dhp_ref), rest = rest[:3], rest[3:]
    else:
        (wide_out, narrow_out), rest = rest[:2], rest[2:]
    buf, bct, scores, dts, cum, cumt, mix, decay, xt, xf, sig, dxt, dscore, dbcs, dcum, ddt, grp = rest
    g = pl.program_id(0) + first
    cont = cont_ref[0, 0]

    @pl.when(g == first)
    def _():
        setup(cont, bc_ref, dt_ref, cwbc_ref, hp_ref, buf, bct, scores, dts, cum, cumt)
        for ref, ref_in, k in ((dscore, wide_in, 0), (dbcs, wide_in, 1), (dcum, narrow_in, 0), (ddt, narrow_in, 1)):
            ref[...] = jnp.zeros_like(ref) if first == 0 else ref_in[k]

    shift = lax.rem(128 - GROUP * g, 128)
    grp[0] = pltpu.roll(dts[...], shift, 1)
    grp[1] = pltpu.roll(cum[...], shift, 1)
    rows8 = cumt[pl.ds(pl.multiple_of(g * GROUP, GROUP), GROUP), :]
    load_halo(buf, x_ref[...], cont, WIDE)
    skip = cp_ref[1:2, :]
    dskip_ref[...] = jnp.zeros_like(dskip_ref)
    pick = jnp.where(
        lax.broadcasted_iota(jnp.int32, (WIDE, 128), 0) // HEAD_DIM + GROUP * g
        == lax.broadcasted_iota(jnp.int32, (WIDE, 128), 1),
        1.0,
        0.0,
    )
    for span in range(2):
        lo = span * SPAN
        hi = lo + SPAN
        s = conv_of(buf, cwx_ref[...], span, WIDE)
        sg = sigmoid(s)
        x = s * sg
        xf[lo:hi, :] = x
        sig[lo:hi, :] = sg * (1.0 + s * (1.0 - sg))
        for j in range(0, GROUP, 2):
            c0 = j * HEAD_DIM
            xt[lo:hi, c0 : c0 + 128] = x[:, c0 : c0 + 128] * pair_lanes(grp[0, lo:hi, :], j, SPAN)
        dyv = dy[lo:hi, :]
        dskip_ref[0:1, :] += jnp.sum(dyv * x, axis=0, keepdims=True)
        yin = y_ref[lo:hi, :] - skip * x
        dcum[lo:hi, :] += dot(dyv.astype(BF).astype(F32) * yin, pick, precision=HIGHEST)

    last = grp[1, SPAN - 1 : SPAN, :]
    w0 = jnp.exp(last - grp[1, 0:SPAN, :])
    ecum1 = jnp.exp(grp[1, SPAN:, :])
    for j in range(0, GROUP, 2):
        cs = slice(j * HEAD_DIM, j * HEAD_DIM + 128)
        wl = pair_lanes(w0, j, SPAN)
        xw = (xt[0:SPAN, cs] * wl).astype(BF)
        prior = (dot(bct[0:SPAN, :STATE], xw, TN) * cont).astype(BF)
        dye = (dy[SPAN:, cs] * pair_lanes(ecum1, j, SPAN)).astype(BF)
        dprior = (dot(bct[SPAN:, STATE:], dye, TN) * cont).astype(BF)
        dbcs[SPAN:, STATE:] += dot(dye, prior, NT)
        dbcs[0:SPAN, :STATE] += dot(xw, dprior, NT)
        v = dot(bct[0:SPAN, :STATE], dprior) * wl
        dxt[0:SPAN, cs] = v
        dxt[SPAN:, cs] = jnp.zeros((SPAN, 128), F32)
    through = dxt[0:SPAN, :] * xt[0:SPAN, :]
    dcum[SPAN - 1 : SPAN, :] += dot(jnp.sum(through, axis=0, keepdims=True), pick, precision=HIGHEST)

    for span in range(2):
        lo = span * SPAN
        hi = lo + SPAN
        for j in range(0, GROUP, 2):
            cs = slice(j * HEAD_DIM, j * HEAD_DIM + 128)
            dyp = dy[lo:hi, cs]
            dyb = dyp.astype(BF)
            dyt = dyp.T.astype(BF)
            xtb = xt[lo:hi, cs].astype(BF)
            parts = []
            for i in range(2):
                hs = slice(i * HEAD_DIM, (i + 1) * HEAD_DIM)
                fill_both(mix, decay, i, scores, grp, rows8, span, j + i)
                dmix = dot(dyb[:, hs], xtb[:, hs], NT)
                dscore[lo:hi, :] += dmix * decay[...]
                parts.append(dot(dyt[hs, :], mix[i]))
            dxt[lo:hi, cs] += jnp.concatenate(parts, axis=0).T

    dcw_ref[...] = jnp.zeros_like(dcw_ref)
    for span in range(2):
        lo = span * SPAN
        hi = lo + SPAN
        x = xf[lo:hi, :]
        xtv = xt[lo:hi, :]
        dv = dxt[lo:hi, :]
        dcum[lo:hi, :] -= dot(dv * xtv.astype(BF).astype(F32), pick, precision=HIGHEST)
        ddt[lo:hi, :] += dot(dv * x, pick, precision=HIGHEST)
        for j in range(0, GROUP, 2):
            cs = slice(j * HEAD_DIM, j * HEAD_DIM + 128)
            dc = dxt[lo:hi, cs] * pair_lanes(grp[0, lo:hi, :], j, SPAN) + dy[lo:hi, cs] * skip[:, cs]
            dxt[lo:hi, cs] = dc * sig[lo:hi, cs]
        conv_weights(dcw_ref, buf, dxt[lo:hi, :], span, WIDE)
    back_halo(buf, dxt[...], cont, WIDE)
    for span in range(2):
        lo = span * SPAN
        dx_ref[lo : lo + SPAN, :] = conv_back(buf, cwx_ref[...], span, WIDE).astype(BF)

    if not last_call:

        @pl.when(pl.program_id(0) == pl.num_programs(0) - 1)
        def _():
            wide_out[0] = dscore[...]
            wide_out[1] = dbcs[...]
            narrow_out[0] = dcum[...]
            narrow_out[1] = ddt[...]

        return

    @pl.when(g == STEPS - 1)
    def _():
        load_halo(buf, bc_ref[...], cont, 2 * STATE)
        dcwbc_ref[...] = jnp.zeros_like(dcwbc_ref)
        for span in range(2):
            lo = span * SPAN
            hi = lo + SPAN
            ds = jnp.where(lower_tri(), dscore[lo:hi, :], 0.0).astype(BF)
            dbcs[lo:hi, :STATE] += dot(ds, bct[lo:hi, STATE:], TN)
            dbcs[lo:hi, STATE:] += dot(ds, bct[lo:hi, :STATE])
            s = conv_of(buf, cwbc_ref[...], span, 2 * STATE)
            sg = sigmoid(s)
            dcv = dbcs[lo:hi, :] * (sg * (1.0 + s * (1.0 - sg)))
            dbcs[lo:hi, :] = dcv
            conv_weights(dcwbc_ref, buf, dcv, span, 2 * STATE)
        back_halo(buf, dbcs[...], cont, 2 * STATE)
        for span in range(2):
            lo = span * SPAN
            dbc_ref[lo : lo + SPAN, : 2 * STATE] = conv_back(buf, cwbc_ref[...], span, 2 * STATE).astype(BF)
        lane = lax.broadcasted_iota(jnp.int32, (TOK, 128), 1)
        raw = jnp.where(lane < HEADS, dt_ref[...], 0.0) + hp_ref[0:1, :]
        decay_rate = -jnp.exp(hp_ref[1:2, :])
        tri = jnp.where(lower_tri(), 1.0, 0.0)
        da = jnp.concatenate(
            [dot(tri, dcum[lo : lo + SPAN, :], TN, HIGHEST) for lo in (0, SPAN)], axis=0
        )
        draw = jnp.where(lane < HEADS, (ddt[...] + decay_rate * da) * sigmoid(raw), 0.0)
        dbc_ref[:, 2 * STATE :] = draw.astype(BF)
        dhp_ref[...] = jnp.zeros_like(dhp_ref)
        dhp_ref[0:1, :] = jnp.sum(draw, axis=0, keepdims=True)
        dhp_ref[1:2, :] = jnp.sum(da * decay_rate * dts[...], axis=0, keepdims=True)


def conv_weights(out, buf, dcv, span, width):
    for k in range(CONV):
        out[3 - k : 4 - k, :] += jnp.sum(dcv * shifted(buf, k, span, width), axis=0, keepdims=True)
    out[4:5, :] += jnp.sum(dcv, axis=0, keepdims=True)


def back_halo(buf, dcv, cont, width):
    buf[0:SPAN, :width] = dcv[0:SPAN]
    buf[SPAN : SPAN + HALO, :width] = dcv[SPAN : SPAN + HALO] * cont
    buf[SPAN + HALO : 2 * SPAN + HALO, :width] = dcv[SPAN:]
    buf[2 * SPAN + HALO : 2 * (SPAN + HALO), :width] = jnp.zeros((HALO, width), F32)


def conv_back(buf, cw, span, width):
    base = span * (SPAN + HALO)
    total = cw[3:4, :] * buf[base : base + SPAN, :width]
    for k in range(1, CONV):
        total = total + cw[3 - k : 4 - k, :] * buf[base + k : base + k + SPAN, :width]
    return total


def fill_both(mix, decay, slot, scores, grp, rows8, span, j):
    lo = span * SPAN
    for r in range(0, SPAN, CHUNK):
        wide = 128 if r + CHUNK <= 128 else 256
        gap = grp[1, lo + r : lo + r + CHUNK, j : j + 1] - rows8[j : j + 1, lo : lo + wide]
        e = jnp.exp(jnp.minimum(gap, 0.0))
        decay[r : r + CHUNK, :wide] = e
        mix[slot, r : r + CHUNK, :wide] = (scores[lo + r : lo + r + CHUNK, :wide] * e).astype(BF)
        if wide < 256:
            mix[slot, r : r + CHUNK, wide:] = jnp.zeros((CHUNK, 256 - wide), BF)
            decay[r : r + CHUNK, wide:] = jnp.zeros((CHUNK, 256 - wide), F32)


def scan_bwd(zx, cont, side_row, y, dy, first, count, carry):
    hp, cw, cp = head_rows(side_row), conv_rows(side_row), column_rows(side_row)
    last_call = first + count == STEPS
    full = lambda shape: pl.BlockSpec(shape, lambda g: (0,) * len(shape))
    by_g = lambda rows_: pl.BlockSpec((rows_, WIDE), lambda g: (0, first + g))
    out_g = lambda rows_: pl.BlockSpec((rows_, WIDE), lambda g: (0, g))
    if carry is None:
        carry = (jnp.zeros((2, 8, 128), F32),) * 2
    if last_call:
        tail_shapes = ((TOK, 2 * STATE + 128), BF), ((8, 2 * STATE), F32), ((8, 128), F32)
    else:
        tail_shapes = ((2, TOK, 2 * STATE), F32), ((2, TOK, 128), F32)
    shapes = (((TOK, count * WIDE), BF), ((8, count * WIDE), F32), ((8, count * WIDE), F32)) + tail_shapes
    return pl.pallas_call(
        partial(bwd_kernel, first, last_call),
        grid=(count,),
        out_shape=tuple(jax.ShapeDtypeStruct(*s) for s in shapes),
        in_specs=[
            pl.BlockSpec(memory_space=pltpu.SMEM),
            pl.BlockSpec((TOK, WIDE), lambda g: (0, STEPS + first + g)),
            pl.BlockSpec((TOK, 2 * STATE), lambda g: (0, 2 * INNER // (2 * STATE))),
            pl.BlockSpec((TOK, 128), lambda g: (0, (INNER + XBC) // 128)),
            by_g(8),
            pl.BlockSpec((8, 2 * STATE), lambda g: (0, INNER // (2 * STATE))),
            full((8, 128)),
            by_g(8),
            by_g(TOK),
            by_g(TOK),
            full(carry[0].shape),
            full(carry[1].shape),
        ],
        out_specs=(out_g(TOK), out_g(8), out_g(8)) + tuple(full(s[0]) for s in tail_shapes),
        scratch_shapes=[
            pltpu.VMEM((2 * (HALO + SPAN), WIDE), F32),
            pltpu.VMEM((TOK, 2 * STATE), BF),
            pltpu.VMEM((TOK, SPAN), F32),
            pltpu.VMEM((TOK, 128), F32),
            pltpu.VMEM((TOK, 128), F32),
            pltpu.VMEM((128, TOK), F32),
            pltpu.VMEM((2, SPAN, SPAN), BF),
            pltpu.VMEM((SPAN, SPAN), F32),
            pltpu.VMEM((TOK, WIDE), F32),
            pltpu.VMEM((TOK, WIDE), F32),
            pltpu.VMEM((TOK, WIDE), F32),
            pltpu.VMEM((TOK, WIDE), F32),
            pltpu.VMEM((TOK, SPAN), F32),
            pltpu.VMEM((TOK, 2 * STATE), F32),
            pltpu.VMEM((TOK, 128), F32),
            pltpu.VMEM((TOK, 128), F32),
            pltpu.VMEM((2, TOK, 128), F32),
        ],
        compiler_params=pltpu.CompilerParams(vmem_limit_bytes=48 * 2**20),
        cost_estimate=pl.CostEstimate(
            flops=2 * 10**9 * count, bytes_accessed=6 * 2**20 * count, transcendentals=4 * 10**6 * count
        ),
        name=f"scan_bwd_{first}",
    )(cont, zx, zx, zx, cw, cw, hp, cp, y, dy, *carry)


def mixer_side(dgain, dskips, dcws, dcwbc, dhp):
    skip_rows = jnp.concatenate([d[0] for d in dskips])
    return jnp.concatenate(
        [
            dgain[0],
            jnp.concatenate([d[: CONV + 1] for d in dcws] + [dcwbc[: CONV + 1]], axis=1).reshape(-1),
            dhp[0, :HEADS],
            dhp[1, :HEADS],
            jnp.sum(skip_rows.reshape(HEADS, HEAD_DIM), axis=1),
        ]
    )


ROWS = 96
COLS = 256
HALF = COLS // 2
LAG = 2
SLOTS = 2 * LAG
MESH = pl.DeviceIdType.MESH
STAGES_A = ("core", "y", "z", "far", "rep")
STAGES_B = ("core", "rep", "y", "z", "far", "rep")
SIZES_A = (8 * ROWS, 4 * ROWS, 2 * ROWS, ROWS, ROWS)
SIZES_B = (8 * ROWS, 4 * ROWS, 2 * ROWS, ROWS, ROWS // 2, ROWS // 2)
WIDTH = 6528
IN_BLOCKS = 26
OUT_BLOCKS = 6
SIDE_ROWS = 176
SIDE_LINKS = ("core", "rep", "y", "z", "far")


class Place:
    def __init__(self):
        self.me = lax.axis_index("shard")
        self.rep = lax.axis_index("rep")
        me = self.me
        self.bits = (me // 8 % 2, me // 4 % 2, me // 2 % 2, me % 2)
        flips = {"far": 0, "z": 1, "y": 2, "core": 3}
        self.targets = {
            name: (self.rep, self.owner(*(int(k == bit) for k in range(4)))) for name, bit in flips.items()
        }
        self.targets["rep"] = (1 - self.rep, me)

    def owner(self, far, z, y, core):
        bits = [1 - b if d else b for b, d in zip(self.bits, (far, z, y, core))]
        return bits[0] * 8 + bits[1] * 4 + bits[2] * 2 + bits[3]

    def greet(self):
        barrier = pltpu.get_barrier_semaphore()
        for target in self.targets.values():
            pl.semaphore_signal(barrier, inc=1, device_id=target, device_id_type=MESH)
        pl.semaphore_wait(barrier, len(self.targets))


def sum_kernel(
    ticks, lt_ref, rt_ref, w_ref, side_ref, out_ref, dr_ref, side_out, tmp, wbuf, wtail, wsem, side_in, side_sems, *rest
):
    n_a, n_b = len(STAGES_A), len(STAGES_B)
    kinds = {}
    for kind, links in (("a", STAGES_A), ("b", STAGES_B)):
        n = len(links)
        src, rest = rest[:n], rest[n:]
        dst, rest = rest[:n], rest[n:]
        acc, rest = rest[: n - 1], rest[n - 1 :]
        ss, rs = rest[:2]
        rest = rest[2:]
        kinds[kind] = (links, src, dst, acc, ss, rs)
    place = Place()
    rep = place.rep
    place.greet()

    def copy(kind, s, j):
        links, src, dst, _, ss, rs = kinds[kind]
        slot = j % SLOTS
        return pltpu.make_async_remote_copy(
            src_ref=src[s].at[slot],
            dst_ref=dst[s].at[slot],
            send_sem=ss.at[s, slot],
            recv_sem=rs.at[s, slot],
            device_id=place.targets[links[s]],
            device_id_type=MESH,
        )

    def weights(j):
        cols = pl.ds(pl.multiple_of(j * COLS, COLS), COLS)
        return pltpu.make_async_copy(w_ref.at[:, cols], wbuf.at[j % 2], wsem.at[j % 2])

    tail = pltpu.make_async_copy(w_ref.at[:, (IN_BLOCKS - 1) * COLS : WIDTH], wtail, wsem.at[2])

    def begin(j):
        slot = j % SLOTS
        cols = pl.ds(pl.multiple_of(j * COLS, COLS), COLS)
        left = jnp.where(j < IN_BLOCKS, 0, 1 + (j - IN_BLOCKS) // OUT_BLOCKS)
        tmp[...] = dot(lt_ref[left], rt_ref[:, cols])
        for d_core in range(2):
            for b in range(8):
                owner = place.owner(b & 1, b >> 1 & 1, b >> 2 & 1, d_core)
                block = tmp[pl.ds(pl.multiple_of(owner * ROWS, ROWS), ROWS), :HALF]
                to = slice(b * ROWS, (b + 1) * ROWS)
                _, src, _, acc, _, _ = kinds["a"]
                if d_core:
                    src[0][slot, to, :] = block.astype(BF)
                else:
                    acc[0][slot, to, :] = block
                _, src, _, acc, _, _ = kinds["b"]
                for d_rep in range(2):
                    top = owner * ROWS + (1 - rep if d_rep else rep) * (ROWS // 2)
                    block = tmp[pl.ds(pl.multiple_of(top, ROWS // 2), ROWS // 2), HALF:]
                    to = slice((d_rep * 8 + b) * (ROWS // 2), (d_rep * 8 + b + 1) * (ROWS // 2))
                    if d_core:
                        src[0][slot, to, :] = block.astype(BF)
                    else:
                        acc[0][slot, to, :] = block
        copy("a", 0, j).start()
        copy("b", 0, j).start()

        @pl.when(j < IN_BLOCKS - 1)
        def _():
            weights(j).wait()
            dr_ref[...] += dot(rt_ref[:, cols], wbuf[j % 2], NT)

            @pl.when(j + 2 < IN_BLOCKS - 1)
            def _():
                weights(j + 2).start()

    def go_on(kind, s, j):
        links, src, dst, acc, _, _ = kinds[kind]
        slot = j % SLOTS
        copy(kind, s - 1, j).wait()
        size = src[s].shape[1]
        if s == len(links) - 1:
            src[s][slot] = (acc[s - 1][slot] + dst[s - 1][slot].astype(F32)).astype(BF)
        else:
            src[s][slot] = (acc[s - 1][slot, size:, :] + dst[s - 1][slot, size:, :].astype(F32)).astype(BF)
            acc[s][slot] = acc[s - 1][slot, :size, :] + dst[s - 1][slot, :size, :].astype(F32)
        copy(kind, s, j).start()

    def finish(kind, j):
        _, src, dst, _, _, _ = kinds[kind]
        slot = j % SLOTS
        if kind == "a":
            copy("a", n_a - 1, j).wait()
            cols = pl.ds(pl.multiple_of(j * COLS, HALF), HALF)
            out_ref[:, cols] = src[-1][slot].astype(F32) + dst[-1][slot].astype(F32)
        else:
            copy("b", n_b - 1, j).wait()
            cols = pl.ds(pl.multiple_of(j * COLS + HALF, HALF), HALF)
            mine = pl.ds(pl.multiple_of(rep * (ROWS // 2), ROWS // 2), ROWS // 2)
            theirs = pl.ds(pl.multiple_of((1 - rep) * (ROWS // 2), ROWS // 2), ROWS // 2)
            out_ref[mine, cols] = src[-1][slot].astype(F32)
            out_ref[theirs, cols] = dst[-1][slot].astype(F32)

    def side_copy(k):
        return pltpu.make_async_remote_copy(
            src_ref=side_out.at[k],
            dst_ref=side_in.at[k],
            send_sem=side_sems.at[0, k],
            recv_sem=side_sems.at[1, k],
            device_id=place.targets[SIDE_LINKS[k]],
            device_id_type=MESH,
        )

    side_out[0] = side_ref[...]
    side_copy(0).start()
    weights(0).start()
    weights(1).start()
    tail.start()
    dr_ref[...] = jnp.zeros_like(dr_ref)

    def tick(t, _):
        for s in range(n_b, -1, -1):
            j = t - LAG * s

            @pl.when((j >= 0) & (j < ticks))
            def _():
                if s == 0:
                    begin(j)
                    return
                if s < n_b:
                    go_on("b", s, j)
                else:
                    finish("b", j)
                if s < n_a:
                    go_on("a", s, j)
                elif s == n_a:
                    finish("a", j)

        for k in range(len(SIDE_LINKS)):

            @pl.when(t == 4 * (k + 1))
            def _():
                side_copy(k).wait()
                side_out[k + 1] = side_out[k] + side_in[k]
                if k + 1 < len(SIDE_LINKS):
                    side_copy(k + 1).start()

        return 0

    lax.fori_loop(0, ticks + LAG * n_b, tick, 0)
    tail.wait()
    dr_ref[...] += dot(rt_ref[:, (IN_BLOCKS - 1) * COLS : WIDTH], wtail[...], NT)


def summed(lt, rt, full_in, side):
    ticks = rt.shape[1] // COLS
    scratch = []
    for links, sizes in ((STAGES_A, SIZES_A), (STAGES_B, SIZES_B)):
        scratch += [pltpu.VMEM((SLOTS, r, HALF), BF) for r in sizes] * 2
        scratch += [pltpu.VMEM((SLOTS, r, HALF), F32) for r in sizes[:1] + sizes[1:-1]]
        scratch += [pltpu.SemaphoreType.DMA((len(links), SLOTS))] * 2
    vmem = pl.BlockSpec(memory_space=pltpu.VMEM)
    return pl.pallas_call(
        partial(sum_kernel, ticks),
        out_shape=(
            jax.ShapeDtypeStruct((ROWS, rt.shape[1]), F32),
            jax.ShapeDtypeStruct((TOK, D), F32),
            jax.ShapeDtypeStruct((len(SIDE_LINKS) + 1, SIDE_ROWS, 128), F32),
        ),
        in_specs=[vmem, vmem, pl.BlockSpec(memory_space=pl.ANY), vmem],
        out_specs=(vmem, vmem, vmem),
        scratch_shapes=[
            pltpu.VMEM((16 * ROWS, COLS), F32),
            pltpu.VMEM((2, D, COLS), BF),
            pltpu.VMEM((D, WIDTH - (IN_BLOCKS - 1) * COLS), BF),
            pltpu.SemaphoreType.DMA((3,)),
            pltpu.VMEM((len(SIDE_LINKS), SIDE_ROWS, 128), F32),
            pltpu.SemaphoreType.DMA((2, len(SIDE_LINKS))),
            *scratch,
        ],
        compiler_params=pltpu.CompilerParams(
            collective_id=1, has_side_effects=True, vmem_limit_bytes=60 * 2**20
        ),
        cost_estimate=pl.CostEstimate(flops=3 * 10**10, bytes_accessed=50 * 2**20, transcendentals=0),
        name="summed",
    )(lt, rt, full_in, side)


def span_starts(seq_lengths):
    offsets = jnp.cumsum(seq_lengths) - seq_lengths
    places = jnp.arange(seq_lengths.shape[0], dtype=jnp.int32) * SPAN
    matches = (offsets[None, :] == places[:, None]) & (seq_lengths[None, :] > 0)
    return jnp.any(matches, axis=1)


def prenorm(hidden, gain):
    inverse = lax.rsqrt(jnp.mean(hidden * hidden, axis=-1, keepdims=True) + EPSILON)
    return hidden * inverse * gain


def adamw_step(parameter, first_moment, second_moment, gradient, step_rate, decay_rate):
    first_new = BETA_ONE * first_moment + (1.0 - BETA_ONE) * gradient
    second_new = BETA_TWO * second_moment + (1.0 - BETA_TWO) * gradient * gradient
    correction_one = 1.0 - BETA_ONE**STEP
    correction_two = 1.0 - BETA_TWO**STEP
    update = first_new / correction_one / (jnp.sqrt(second_new / correction_two) + ADAM_EPSILON)
    return (parameter - step_rate * (update + decay_rate * parameter), first_new, second_new)


def swap(value, axis, count, bit):
    return lax.ppermute(value, axis, [(i, i ^ bit) for i in range(count)])


def plain_owner_sum(left, right, reps):
    mine = lax.psum_scatter(dot(left, right, TN).astype(BF), "shard", scatter_dimension=0, tiled=True)
    total = mine.astype(F32)
    for bit in [1 << k for k in range(reps.bit_length() - 1)]:
        total = total + swap(total.astype(BF), "rep", reps, bit).astype(F32)
    return total


def sum_everywhere(value, reps, shards):
    for axis, count in (("shard", shards), ("rep", reps)):
        bit = 1
        while bit < count:
            value = value + swap(value, axis, count, bit)
            bit *= 2
    return value


def left_rows(normed, mixed):
    halves = mixed.T.reshape(16, 2, ROWS, TOK).transpose(1, 0, 2, 3).reshape(2, 16 * ROWS, TOK)
    return jnp.concatenate([normed.T[None], halves], axis=0)


def sums_direct(left, dz, dxs, dbc, low, full_in, side):
    pad = jnp.zeros((TOK, IN_BLOCKS * COLS - 2 * INNER - dbc.shape[1]), BF)
    right = jnp.concatenate([dz, *dxs, dbc, pad, low, low], axis=1)
    side = jnp.pad(side, (0, SIDE_ROWS * 128 - side.shape[0])).reshape(SIDE_ROWS, 128)
    sums, back, side = summed(left, right, full_in, side)
    cut = IN_BLOCKS * COLS
    return sums[:, : INNER + XBC + HEADS], sums[:, cut:].reshape(ROWS, 2, D).transpose(1, 0, 2), back, side[-1].reshape(-1)


def sums_plain(normed, mixed, dz, dxs, dbc, low, full_in, side, reps):
    right = jnp.concatenate([dz, *dxs, dbc], axis=1)
    used = 2 * INNER + 2 * STATE + HEADS
    sum_in = plain_owner_sum(normed, right[:, :used], reps)
    sum_out = plain_owner_sum(mixed, low, reps)
    return sum_in, sum_out, dot(right, full_in, NT), lax.psum(side, ("rep", "shard"))


def per_device(
    tokens, cotangent, lengths,
    weight_in, moment_in, second_in,
    weight_out, moment_out, second_out,
    side_params, side_moment, side_second,
    *, reps, shards,
):
    direct = shards == 16 and reps == 2
    cont = jnp.where(span_starts(lengths[0])[1], 0.0, 1.0).astype(F32).reshape(1, 1)
    hidden = tokens.astype(F32)
    shares = []
    earlier = ()
    for layer in range(LAYERS):
        for weight, width in ((weight_in[layer], WIDTH), (weight_out[layer], D)):
            weight, *earlier = lax.optimization_barrier((weight, *earlier))
            share = jnp.pad(weight.astype(BF), ((0, 0), (0, width - weight.shape[1])))
            shares.append(share)
            earlier = (share,)
    gathered = [lax.all_gather(share, "shard", axis=0, tiled=True) for share in shares]
    saved = []
    layer_outs = []
    for layer in range(LAYERS):
        full_in, full_out = gathered[2 * layer : 2 * layer + 2]
        normed, norm_pull = jax.vjp(prenorm, hidden, side_params[layer, :D])
        normed = normed.astype(BF)
        zx = jnp.dot(normed, full_in, preferred_element_type=F32)
        mixed, y, inverse = mixer_fwd(zx, cont, side_params[layer])
        left = left_rows(normed, mixed) if direct else None
        branch = jnp.dot(mixed, full_out, preferred_element_type=F32)
        hidden = hidden + branch
        layer_outs.append(hidden)
        saved.append((full_in, full_out, norm_pull, normed, zx, mixed, y, inverse, branch, left))
    gradient = cotangent.astype(F32)
    sums = [None] * LAYERS
    side_mixer = [None] * LAYERS
    side_norm = [None] * LAYERS
    for layer in reversed(range(LAYERS)):
        full_in, full_out, norm_pull, normed, zx, mixed, y, inverse, branch, left = saved[layer]
        side_row = side_params[layer]
        low = gradient.astype(BF)
        factor = jnp.sum(low.astype(F32) * branch, axis=1, keepdims=True) * (1.0 / INNER)
        rows = jnp.concatenate([inverse[:, :1], factor, jnp.zeros((TOK, 126), F32)], axis=1)
        dz, dy, dgain = gate_bwd(low, full_out, zx, side_row, y, rows)
        dx, dskip, dcw, dbc, dcwbc, dhp = scan_bwd(zx, cont, side_row, y, dy, 0, STEPS, None)
        side = mixer_side(dgain, [dskip], [dcw], dcwbc, dhp)
        count = side.shape[0]
        if layer < LAYERS - 1:
            side = jnp.concatenate([side, side_norm[layer + 1]])
        if direct:
            sum_in, sum_out, back, side = sums_direct(left, dz, [dx], dbc, low, full_in, side)
        else:
            sum_in, sum_out, back, side = sums_plain(normed, mixed, dz, [dx], dbc, low, full_in, side, reps)
        side_mixer[layer] = side[:count]
        if layer < LAYERS - 1:
            side_norm[layer + 1] = side[count : count + D]
        back_hidden, side_norm[layer] = norm_pull(back)
        sums[layer] = (sum_in, sum_out)
        gradient = gradient + back_hidden
    side_norm[0] = sum_everywhere(side_norm[0], reps, shards)
    grad_in = jnp.stack([s[0] for s in sums])
    grad_out = jnp.stack([s[1].reshape(weight_out.shape[1:]) for s in sums])
    grad_side = jnp.stack([jnp.concatenate(pair) for pair in zip(side_norm, side_mixer)])
    return (
        jnp.stack(layer_outs),
        gradient,
        *adamw_step(weight_in, moment_in, second_in, grad_in, RATE_MATRIX, DECAY_MATRIX),
        *adamw_step(weight_out, moment_out, second_out, grad_out, RATE_MATRIX, DECAY_MATRIX),
        *adamw_step(side_params, side_moment, side_second, grad_side, RATE_SIDE, 0.0),
    )


def solution(mesh):
    rows = P(("rep", "shard"), None)
    owned = P(None, "shard", None)
    body = partial(per_device, reps=mesh.shape["rep"], shards=mesh.shape["shard"])
    return jax.shard_map(
        body,
        mesh=mesh,
        in_specs=(rows, rows, rows) + (owned,) * 6 + (P(),) * 3,
        out_specs=(P(None, ("rep", "shard"), None), rows) + (owned,) * 6 + (P(),) * 3,
        check_vma=False,
    )
```

```python
from functools import partial

import jax
import jax.numpy as jnp
from jax import lax
from jax.experimental import pallas as pl
from jax.experimental.pallas import tpu as pltpu
from jax.sharding import PartitionSpec as P

LAYERS = 2
STEP = 10
BETA_ONE = 0.9
BETA_TWO = 0.95
ADAM_EPSILON = 1e-08
RATE_MATRIX = 0.05
RATE_SIDE = 0.5
DECAY_MATRIX = 0.1
D = 1536
INNER = 3072
HEAD_DIM = 64
STATE = 128
CONV = 4
SPAN = 256
HEADS = 48
XBC = 3328
TOK = 512
GROUP = 8
BC_WIDE = 512
N_SCAN_SCRATCH = 17
WIDE = GROUP * HEAD_DIM
STEPS = HEADS // GROUP
HALO = 8
EPSILON = 1e-05
HIGHEST = lax.Precision.HIGHEST
BF = jnp.bfloat16
F32 = jnp.float32


def dot(a, b, dims=((1,), (0,)), precision=None):
    return lax.dot_general(a, b, (dims, ((), ())), precision=precision, preferred_element_type=F32)


NT = ((1,), (1,))
TN = ((0,), (0,))


def sigmoid(v):
    return 1.0 / (1.0 + jnp.exp(-v))


def softplus(v):
    e = jnp.exp(-jnp.abs(v))
    u = 1.0 + e
    tail = jnp.where(u == 1.0, e, jnp.log(u) * (e / jnp.where(u == 1.0, 1.0, u - 1.0)))
    return jnp.maximum(v, 0.0) + tail


def load_halo(buf, xin, cont, width):
    buf[0:HALO, :width] = jnp.zeros((HALO, width), F32)
    buf[HALO : HALO + SPAN, :width] = xin[0:SPAN]
    buf[HALO + SPAN : 2 * HALO + SPAN, :width] = xin[SPAN - HALO : SPAN] * cont
    buf[2 * HALO + SPAN : 2 * (HALO + SPAN), :width] = xin[SPAN : 2 * SPAN]


def shifted(buf, k, span, width, lo=0, rows=SPAN):
    base = span * (HALO + SPAN) + HALO - k + lo
    return buf[base : base + rows, :width]


def conv_of(buf, cw, span, width, lo=0, rows=SPAN):
    total = cw[4:5, :] + cw[3:4, :] * shifted(buf, 0, span, width, lo, rows)
    for k in range(1, CONV):
        total = total + cw[3 - k : 4 - k, :] * shifted(buf, k, span, width, lo, rows)
    return total


def lower_tri():
    return (
        lax.broadcasted_iota(jnp.int32, (SPAN, SPAN), 0)
        >= lax.broadcasted_iota(jnp.int32, (SPAN, SPAN), 1)
    )


def setup(cont, bc_ref, dt_ref, cwbc_ref, hp_ref, buf, bct, scores, dts, cum, cumt):
    load_halo(buf, bc_ref[...], cont, 2 * STATE)
    for span in range(2):
        lo = span * SPAN
        s = conv_of(buf, cwbc_ref[...], span, 2 * STATE)
        bct[lo : lo + SPAN, :] = (s * sigmoid(s)).astype(BF)
        sc = dot(bct[lo : lo + SPAN, STATE:], bct[lo : lo + SPAN, :STATE], NT)
        scores[lo : lo + SPAN, :] = jnp.where(lower_tri(), sc, 0.0)
    lane = lax.broadcasted_iota(jnp.int32, (TOK, 128), 1)
    raw = jnp.where(lane < HEADS, dt_ref[...], 0.0) + hp_ref[0:1, :]
    step = jnp.where(lane < HEADS, softplus(raw), 0.0)
    dts[...] = step
    a = -jnp.exp(hp_ref[1:2, :]) * step
    tri = jnp.where(lower_tri(), 1.0, 0.0)
    for span in range(2):
        lo = span * SPAN
        cum[lo : lo + SPAN, :] = dot(tri, a[lo : lo + SPAN, :], precision=HIGHEST)
    cumt[...] = cum[...].T


def pair_lanes(col, j, rows):
    lane = lax.broadcasted_iota(jnp.int32, (rows, 2 * HEAD_DIM), 1)
    return jnp.where(lane < HEAD_DIM, col[:, j : j + 1], col[:, j + 1 : j + 2])


def fwd_kernel(
    cont_ref, z_ref, x_ref, bc_ref, dt_ref, cwx_ref, cwbc_ref, hp_ref, cp_ref, gain_ref,
    m_ref, y_ref, inv_ref,
    buf, bct, scores, dts, cum, cumt, mix, xt, g_s, ssq, grp, state,
):
    g = pl.program_id(0)
    cont = cont_ref[0, 0]

    @pl.when(g == 0)
    def _():
        setup(cont, bc_ref, dt_ref, cwbc_ref, hp_ref, buf, bct, scores, dts, cum, cumt)
        ssq[...] = jnp.zeros_like(ssq)

    shift = lax.rem(128 - GROUP * g, 128)
    grp[0] = pltpu.roll(dts[...], shift, 1)
    grp[1] = pltpu.roll(cum[...], shift, 1)
    rows8 = cumt[pl.ds(pl.multiple_of(g * GROUP, GROUP), GROUP), :]
    load_halo(buf, x_ref[...], cont, WIDE)
    for span in range(2):
        lo = span * SPAN
        s = conv_of(buf, cwx_ref[...], span, WIDE)
        x = s * sigmoid(s)
        y_ref[lo : lo + SPAN, :] = x * cp_ref[1:2, :]
        for j in range(0, GROUP, 2):
            c0 = j * HEAD_DIM
            xt[lo : lo + SPAN, c0 : c0 + 128] = x[:, c0 : c0 + 128] * pair_lanes(
                grp[0, lo : lo + SPAN, :], j, SPAN
            )
    last = grp[1, SPAN - 1 : SPAN, :]
    w0 = jnp.exp(last - grp[1, 0:SPAN, :])
    for j in range(0, GROUP, 2):
        c0 = j * HEAD_DIM
        xw = xt[0:SPAN, c0 : c0 + 128] * pair_lanes(w0, j, SPAN)
        st = dot(bct[0:SPAN, :STATE], xw.astype(BF), TN) * cont
        e1 = pair_lanes(jnp.exp(grp[1, SPAN:, :]), j, SPAN)
        y_ref[SPAN:, c0 : c0 + 128] += e1 * dot(bct[SPAN:, STATE:], st.astype(BF))
    for span in range(2):
        lo = span * SPAN
        for j in range(GROUP):
            c0 = j * HEAD_DIM
            slot = j % 2
            fill_mix(mix, slot, scores, grp, rows8, span, j)
            y_ref[lo : lo + SPAN, c0 : c0 + HEAD_DIM] += dot(
                mix[slot], xt[lo : lo + SPAN, c0 : c0 + HEAD_DIM].astype(BF)
            )
    z = z_ref[...]
    gated = y_ref[...] * (z * sigmoid(z))
    g_s[g] = gated
    ssq[...] += jnp.broadcast_to(jnp.sum(gated * gated, axis=1, keepdims=True), ssq.shape)

    @pl.when(g == STEPS - 1)
    def _():
        inv = lax.rsqrt(ssq[...] * (1.0 / INNER) + EPSILON)
        inv_ref[...] = inv
        col = inv[:, 0:1]
        for k in range(STEPS):
            m_ref[:, k * WIDE : (k + 1) * WIDE] = (
                g_s[k] * col * gain_ref[0:1, k * WIDE : (k + 1) * WIDE]
            ).astype(BF)


CHUNK = 64


def fill_mix(mix, slot, scores, grp, rows8, span, j):
    lo = span * SPAN
    for r in range(0, SPAN, CHUNK):
        wide = 128 if r + CHUNK <= 128 else 256
        gap = grp[1, lo + r : lo + r + CHUNK, j : j + 1] - rows8[j : j + 1, lo : lo + wide]
        val = scores[lo + r : lo + r + CHUNK, :wide] * jnp.exp(jnp.minimum(gap, 0.0))
        mix[slot, r : r + CHUNK, :wide] = val.astype(BF)
        if wide < 256:
            mix[slot, r : r + CHUNK, wide:] = jnp.zeros((CHUNK, 256 - wide), BF)


def head_rows(side_row):
    cur = D + INNER + CONV * XBC + XBC
    rows = side_row[cur : cur + 3 * HEADS].reshape(3, HEADS)
    return jnp.pad(rows, ((0, 5), (0, 128 - HEADS)))


def conv_rows(side_row):
    cur = D + INNER
    rows = side_row[cur : cur + (CONV + 1) * XBC].reshape(CONV + 1, XBC)
    return jnp.pad(rows, ((0, 3), (0, 0)))


def column_rows(side_row):
    gain = side_row[D : D + INNER]
    skip = jnp.repeat(side_row[-HEADS:], HEAD_DIM)
    return jnp.pad(jnp.stack([gain, skip]), ((0, 6), (0, 0)))


def mixer_fwd(zx, cont, side_row):
    hp, cw, cp = head_rows(side_row), conv_rows(side_row), column_rows(side_row)
    full = lambda shape: pl.BlockSpec(shape, lambda g: (0,) * len(shape))
    return pl.pallas_call(
        fwd_kernel,
        grid=(STEPS,),
        out_shape=(
            jax.ShapeDtypeStruct((TOK, INNER), BF),
            jax.ShapeDtypeStruct((TOK, INNER), F32),
            jax.ShapeDtypeStruct((TOK, 128), F32),
        ),
        in_specs=[
            pl.BlockSpec(memory_space=pltpu.SMEM),
            pl.BlockSpec((TOK, WIDE), lambda g: (0, g)),
            pl.BlockSpec((TOK, WIDE), lambda g: (0, STEPS + g)),
            pl.BlockSpec((TOK, 2 * STATE), lambda g: (0, 2 * INNER // (2 * STATE))),
            pl.BlockSpec((TOK, 128), lambda g: (0, (INNER + XBC) // 128)),
            pl.BlockSpec((8, WIDE), lambda g: (0, g)),
            pl.BlockSpec((8, 2 * STATE), lambda g: (0, INNER // (2 * STATE))),
            full((8, 128)),
            pl.BlockSpec((8, WIDE), lambda g: (0, g)),
            full((8, INNER)),
        ],
        out_specs=(
            full((TOK, INNER)),
            pl.BlockSpec((TOK, WIDE), lambda g: (0, g)),
            full((TOK, 128)),
        ),
        scratch_shapes=[
            pltpu.VMEM((2 * (HALO + SPAN), WIDE), F32),
            pltpu.VMEM((TOK, 2 * STATE), BF),
            pltpu.VMEM((TOK, SPAN), F32),
            pltpu.VMEM((TOK, 128), F32),
            pltpu.VMEM((TOK, 128), F32),
            pltpu.VMEM((128, TOK), F32),
            pltpu.VMEM((2, SPAN, SPAN), BF),
            pltpu.VMEM((TOK, WIDE), F32),
            pltpu.VMEM((STEPS, TOK, WIDE), F32),
            pltpu.VMEM((TOK, 128), F32),
            pltpu.VMEM((2, TOK, 128), F32),
            pltpu.VMEM((STATE, WIDE), F32),
        ],
        compiler_params=pltpu.CompilerParams(vmem_limit_bytes=48 * 2**20),
        cost_estimate=pl.CostEstimate(flops=6 * 10**9, bytes_accessed=25 * 2**20, transcendentals=10**7),
        name="mixer_fwd",
    )(cont, zx, zx, zx, zx, cw, cw, hp, cp, cp)


def gate_kernel(low_ref, w_ref, z_ref, cp_ref, y_ref, row_ref, dz_ref, dy_ref, dgain_ref):
    dm = dot(low_ref[...], w_ref[...], NT)
    z = z_ref[...]
    sz = sigmoid(z)
    gate = z * sz
    y = y_ref[...]
    inv = row_ref[:, 0:1]
    gn = y * gate * inv
    dgain_ref[...] = jnp.zeros_like(dgain_ref)
    dgain_ref[0:1, :] = jnp.sum(dm * gn, axis=0, keepdims=True)
    dg = inv * (dm * cp_ref[0:1, :] - gn * row_ref[:, 1:2])
    dz_ref[...] = (dg * y * (sz * (1.0 + z * (1.0 - sz)))).astype(BF)
    dy_ref[...] = dg * gate


def gate_bwd(low, full_out, zx, side_row, y, rows):
    cp = column_rows(side_row)
    by_g = lambda rows_: pl.BlockSpec((rows_, WIDE), lambda g: (0, g))
    full = lambda shape: pl.BlockSpec(shape, lambda g: (0,) * len(shape))
    return pl.pallas_call(
        gate_kernel,
        grid=(STEPS,),
        out_shape=(
            jax.ShapeDtypeStruct((TOK, INNER), BF),
            jax.ShapeDtypeStruct((TOK, INNER), F32),
            jax.ShapeDtypeStruct((8, INNER), F32),
        ),
        in_specs=[
            full((TOK, D)),
            pl.BlockSpec((WIDE, D), lambda g: (g, 0)),
            by_g(TOK),
            by_g(8),
            by_g(TOK),
            full((TOK, 128)),
        ],
        out_specs=(by_g(TOK), by_g(TOK), by_g(8)),
        compiler_params=pltpu.CompilerParams(vmem_limit_bytes=48 * 2**20),
        cost_estimate=pl.CostEstimate(flops=5 * 10**9, bytes_accessed=40 * 2**20, transcendentals=2 * 10**6),
        name="gate_bwd",
    )(low, full_out, zx, cp, y, rows)


def scan_kernel(
    engine_of, n_engine_in,
    cont_ref, x_ref, bc_ref, dt_ref, cwx_ref, cwbc_ref, hp_ref, cp_ref, y_ref, dy, *rest,
):
    engine_in, rest = rest[:n_engine_in], rest[n_engine_in:]
    (dx_ref, dskip_ref, dcw_ref, dbc_ref, dcwbc_ref, dhp_ref), rest = rest[:6], rest[6:]
    (buf, bct, scores, dts, cum, cumt, mix, decay, xt, xf, sig, dxt, dscore, dbcs, dcum, ddt, grp), rest = (
        rest[-N_SCAN_SCRATCH:], rest[:-N_SCAN_SCRATCH]
    )
    engine = engine_of(engine_in, rest)
    g = pl.program_id(0)
    cont = cont_ref[0, 0]

    @pl.when(g == 0)
    def _():
        engine.open()
        setup(cont, bc_ref, dt_ref, cwbc_ref, hp_ref, buf, bct, scores, dts, cum, cumt)
        for ref in (dscore, dbcs, dcum, ddt):
            ref[...] = jnp.zeros_like(ref)

    shift = lax.rem(128 - GROUP * g, 128)
    grp[0] = pltpu.roll(dts[...], shift, 1)
    grp[1] = pltpu.roll(cum[...], shift, 1)
    load_halo(buf, x_ref[...], cont, WIDE)
    skip = cp_ref[1:2, :]
    dskip_ref[...] = jnp.zeros_like(dskip_ref)
    pick = jnp.where(
        lax.broadcasted_iota(jnp.int32, (WIDE, 128), 0) // HEAD_DIM + GROUP * g
        == lax.broadcasted_iota(jnp.int32, (WIDE, 128), 1),
        1.0,
        0.0,
    )
    for span in range(2):
        lo = span * SPAN
        hi = lo + SPAN
        s = conv_of(buf, cwx_ref[...], span, WIDE)
        sg = sigmoid(s)
        x = s * sg
        xf[lo:hi, :] = x
        sig[lo:hi, :] = sg * (1.0 + s * (1.0 - sg))
        for j in range(0, GROUP, 2):
            c0 = j * HEAD_DIM
            xt[lo:hi, c0 : c0 + 128] = x[:, c0 : c0 + 128] * pair_lanes(grp[0, lo:hi, :], j, SPAN)
        dyv = dy[lo:hi, :]
        dskip_ref[0:1, :] += jnp.sum(dyv * x, axis=0, keepdims=True)
        yin = y_ref[lo:hi, :] - skip * x
        dcum[lo:hi, :] += dot(dyv.astype(BF).astype(F32) * yin, pick, precision=HIGHEST)

    last = grp[1, SPAN - 1 : SPAN, :]
    w0 = jnp.exp(last - grp[1, 0:SPAN, :])
    ecum1 = jnp.exp(grp[1, SPAN:, :])
    for j in range(0, GROUP, 2):
        cs = slice(j * HEAD_DIM, j * HEAD_DIM + 128)
        wl = pair_lanes(w0, j, SPAN)
        xw = (xt[0:SPAN, cs] * wl).astype(BF)
        prior = (dot(bct[0:SPAN, :STATE], xw, TN) * cont).astype(BF)
        dye = (dy[SPAN:, cs] * pair_lanes(ecum1, j, SPAN)).astype(BF)
        dprior = (dot(bct[SPAN:, STATE:], dye, TN) * cont).astype(BF)
        dbcs[SPAN:, STATE:] += dot(dye, prior, NT)
        dbcs[0:SPAN, :STATE] += dot(xw, dprior, NT)
        dxt[0:SPAN, cs] = dot(bct[0:SPAN, :STATE], dprior) * wl
        dxt[SPAN:, cs] = jnp.zeros((SPAN, 128), F32)
    through = dxt[0:SPAN, :] * xt[0:SPAN, :]
    dcum[SPAN - 1 : SPAN, :] += dot(jnp.sum(through, axis=0, keepdims=True), pick, precision=HIGHEST)

    def pair(i, _):
        lo = pl.multiple_of(i // 4 * SPAN, SPAN)
        j = i % 4
        here = pl.ds(lo, SPAN)
        cs = pl.ds(pl.multiple_of(j * 128, 128), 128)
        dyp = dy[here, cs]
        dyb = dyp.astype(BF)
        dyt = dyp.T.astype(BF)
        xtb = xt[here, cs].astype(BF)
        col = pltpu.roll(grp[1, here, :], lax.rem(128 - 2 * j, 128), 1)
        row = pltpu.roll(cumt[pl.ds(pl.multiple_of(g * GROUP, GROUP), GROUP), here], lax.rem(GROUP - 2 * j, GROUP), 0)
        parts = []
        for h in range(2):
            hs = slice(h * HEAD_DIM, (h + 1) * HEAD_DIM)
            for r in range(0, SPAN, CHUNK):
                wide = 128 if r + CHUNK <= 128 else 256
                gap = col[r : r + CHUNK, h : h + 1] - row[h : h + 1, :wide]
                e = jnp.exp(jnp.minimum(gap, 0.0))
                decay[r : r + CHUNK, :wide] = e
                score = scores[pl.ds(pl.multiple_of(lo + r, CHUNK), CHUNK), :wide]
                mix[h, r : r + CHUNK, :wide] = (score * e).astype(BF)
                if wide < 256:
                    mix[h, r : r + CHUNK, wide:] = jnp.zeros((CHUNK, 256 - wide), BF)
                    decay[r : r + CHUNK, wide:] = jnp.zeros((CHUNK, 256 - wide), F32)
            dscore[here, :] += dot(dyb[:, hs], xtb[:, hs], NT) * decay[...]
            parts.append(dot(dyt[hs, :], mix[h]))
        dxt[here, cs] += jnp.concatenate(parts, axis=0).T
        engine.pump(g * GROUP + i, STEPS * GROUP)
        return 0

    lax.fori_loop(0, GROUP, pair, 0)

    dcw_ref[...] = jnp.zeros_like(dcw_ref)
    for span in range(2):
        lo = span * SPAN
        hi = lo + SPAN
        x = xf[lo:hi, :]
        xtv = xt[lo:hi, :]
        dv = dxt[lo:hi, :]
        dcum[lo:hi, :] -= dot(dv * xtv.astype(BF).astype(F32), pick, precision=HIGHEST)
        ddt[lo:hi, :] += dot(dv * x, pick, precision=HIGHEST)
        for j in range(0, GROUP, 2):
            cs = slice(j * HEAD_DIM, j * HEAD_DIM + 128)
            dc = dxt[lo:hi, cs] * pair_lanes(grp[0, lo:hi, :], j, SPAN) + dy[lo:hi, cs] * skip[:, cs]
            dxt[lo:hi, cs] = dc * sig[lo:hi, cs]
        conv_weights(dcw_ref, buf, dxt[lo:hi, :], span, WIDE)
    back_halo(buf, dxt[...], cont, WIDE)
    for span in range(2):
        lo = span * SPAN
        dx_ref[lo : lo + SPAN, :] = conv_back(buf, cwx_ref[...], span, WIDE).astype(BF)

    @pl.when(g == STEPS - 1)
    def _():
        load_halo(buf, bc_ref[...], cont, 2 * STATE)
        dcwbc_ref[...] = jnp.zeros_like(dcwbc_ref)
        for span in range(2):
            lo = span * SPAN
            hi = lo + SPAN
            ds = jnp.where(lower_tri(), dscore[lo:hi, :], 0.0).astype(BF)
            dbcs[lo:hi, :STATE] += dot(ds, bct[lo:hi, STATE:], TN)
            dbcs[lo:hi, STATE:] += dot(ds, bct[lo:hi, :STATE])
            s = conv_of(buf, cwbc_ref[...], span, 2 * STATE)
            sg = sigmoid(s)
            dcv = dbcs[lo:hi, :] * (sg * (1.0 + s * (1.0 - sg)))
            dbcs[lo:hi, :] = dcv
            conv_weights(dcwbc_ref, buf, dcv, span, 2 * STATE)
        back_halo(buf, dbcs[...], cont, 2 * STATE)
        for span in range(2):
            lo = span * SPAN
            dbc_ref[lo : lo + SPAN, : 2 * STATE] = conv_back(buf, cwbc_ref[...], span, 2 * STATE).astype(BF)
        lane = lax.broadcasted_iota(jnp.int32, (TOK, 128), 1)
        raw = jnp.where(lane < HEADS, dt_ref[...], 0.0) + hp_ref[0:1, :]
        decay_rate = -jnp.exp(hp_ref[1:2, :])
        tri = jnp.where(lower_tri(), 1.0, 0.0)
        da = jnp.concatenate(
            [dot(tri, dcum[lo : lo + SPAN, :], TN, HIGHEST) for lo in (0, SPAN)], axis=0
        )
        draw = jnp.where(lane < HEADS, (ddt[...] + decay_rate * da) * sigmoid(raw), 0.0)
        dbc_ref[:, 2 * STATE : 2 * STATE + 128] = draw.astype(BF)
        dbc_ref[:, 2 * STATE + 128 :] = jnp.zeros((TOK, BC_WIDE - 2 * STATE - 128), BF)
        dhp_ref[...] = jnp.zeros_like(dhp_ref)
        dhp_ref[0:1, :] = jnp.sum(draw, axis=0, keepdims=True)
        dhp_ref[1:2, :] = jnp.sum(da * decay_rate * dts[...], axis=0, keepdims=True)
        engine.close(STEPS * GROUP)


def conv_weights(out, buf, dcv, span, width):
    for k in range(CONV):
        out[3 - k : 4 - k, :] += jnp.sum(dcv * shifted(buf, k, span, width), axis=0, keepdims=True)
    out[4:5, :] += jnp.sum(dcv, axis=0, keepdims=True)


def back_halo(buf, dcv, cont, width):
    buf[0:SPAN, :width] = dcv[0:SPAN]
    buf[SPAN : SPAN + HALO, :width] = dcv[SPAN : SPAN + HALO] * cont
    buf[SPAN + HALO : 2 * SPAN + HALO, :width] = dcv[SPAN:]
    buf[2 * SPAN + HALO : 2 * (SPAN + HALO), :width] = jnp.zeros((HALO, width), F32)


def conv_back(buf, cw, span, width):
    base = span * (SPAN + HALO)
    total = cw[3:4, :] * buf[base : base + SPAN, :width]
    for k in range(1, CONV):
        total = total + cw[3 - k : 4 - k, :] * buf[base + k : base + k + SPAN, :width]
    return total


def scan_bwd(zx, cont, side_row, y, dy, work):
    hp, cw, cp = head_rows(side_row), conv_rows(side_row), column_rows(side_row)
    full = lambda shape: pl.BlockSpec(shape, lambda g: (0,) * len(shape))
    by_g = lambda rows_: pl.BlockSpec((rows_, WIDE), lambda g: (0, g))
    shapes = (
        ((TOK, INNER), BF), ((8, INNER), F32), ((8, INNER), F32),
        ((TOK, BC_WIDE), BF), ((8, 2 * STATE), F32), ((8, 128), F32),
    )
    out = pl.pallas_call(
        partial(scan_kernel, work.engine, len(work.inputs)),
        grid=(STEPS,),
        out_shape=tuple(jax.ShapeDtypeStruct(*s) for s in shapes) + tuple(work.out_shapes),
        in_specs=[
            pl.BlockSpec(memory_space=pltpu.SMEM),
            pl.BlockSpec((TOK, WIDE), lambda g: (0, STEPS + g)),
            pl.BlockSpec((TOK, 2 * STATE), lambda g: (0, 2 * INNER // (2 * STATE))),
            pl.BlockSpec((TOK, 128), lambda g: (0, (INNER + XBC) // 128)),
            by_g(8),
            pl.BlockSpec((8, 2 * STATE), lambda g: (0, INNER // (2 * STATE))),
            full((8, 128)),
            by_g(8),
            by_g(TOK),
            by_g(TOK),
            *work.in_specs,
        ],
        out_specs=(by_g(TOK), by_g(8), by_g(8)) + tuple(full(s[0]) for s in shapes[3:]) + tuple(work.out_specs),
        scratch_shapes=[
            *work.scratch,
            pltpu.VMEM((2 * (HALO + SPAN), WIDE), F32),
            pltpu.VMEM((TOK, 2 * STATE), BF),
            pltpu.VMEM((TOK, SPAN), F32),
            pltpu.VMEM((TOK, 128), F32),
            pltpu.VMEM((TOK, 128), F32),
            pltpu.VMEM((128, TOK), F32),
            pltpu.VMEM((2, SPAN, SPAN), BF),
            pltpu.VMEM((SPAN, SPAN), F32),
            pltpu.VMEM((TOK, WIDE), F32),
            pltpu.VMEM((TOK, WIDE), F32),
            pltpu.VMEM((TOK, WIDE), F32),
            pltpu.VMEM((TOK, WIDE), F32),
            pltpu.VMEM((TOK, SPAN), F32),
            pltpu.VMEM((TOK, 2 * STATE), F32),
            pltpu.VMEM((TOK, 128), F32),
            pltpu.VMEM((TOK, 128), F32),
            pltpu.VMEM((2, TOK, 128), F32),
        ],
        compiler_params=work.params(),
        cost_estimate=pl.CostEstimate(flops=12 * 10**9, bytes_accessed=60 * 2**20, transcendentals=2 * 10**7),
        name=f"scan_bwd{work.name}",
    )(cont, zx, zx, zx, cw, cw, hp, cp, y, dy, *work.inputs)
    return out[:6], out[6:]


def mixer_side(dgain, dskip, dcw, dcwbc, dhp):
    return jnp.concatenate(
        [
            dgain[0],
            jnp.concatenate([dcw[: CONV + 1], dcwbc[: CONV + 1]], axis=1).reshape(-1),
            dhp[0, :HEADS],
            dhp[1, :HEADS],
            jnp.sum(dskip[0].reshape(HEADS, HEAD_DIM), axis=1),
        ]
    )


def back_kernel(dz_ref, dx_ref, dbc_ref, w_ref, out_ref):
    n = INNER
    total = dot(dz_ref[...], w_ref[:, :n], NT) + dot(dx_ref[...], w_ref[:, n : 2 * n], NT)
    out_ref[...] = total + dot(dbc_ref[...], w_ref[:, 2 * n :], NT)


def back_to_input(dz, dx, dbc, full_in):
    part = 256
    whole = lambda a: pl.BlockSpec(a.shape, lambda k: (0, 0), pipeline_mode=pl.Buffered(1))
    return pl.pallas_call(
        back_kernel,
        grid=(D // part,),
        out_shape=jax.ShapeDtypeStruct((TOK, D), F32),
        in_specs=[whole(dz), whole(dx), whole(dbc), pl.BlockSpec((part, full_in.shape[1]), lambda k: (k, 0))],
        out_specs=pl.BlockSpec((TOK, part), lambda k: (0, k)),
        compiler_params=pltpu.CompilerParams(vmem_limit_bytes=48 * 2**20),
        cost_estimate=pl.CostEstimate(flops=10**10, bytes_accessed=32 * 2**20, transcendentals=0),
        name="back_to_input",
    )(dz, dx, dbc, full_in)


ROWS = 96
COLS = 256
HALF = COLS // 2
LAG = 2
SLOTS = 2 * LAG
MESH = pl.DeviceIdType.MESH
STAGES_A = ("core", "y", "z", "far", "rep")
STAGES_B = ("core", "rep", "y", "z", "far", "rep")
SIZES_A = (8 * ROWS, 4 * ROWS, 2 * ROWS, ROWS, ROWS)
SIZES_B = (8 * ROWS, 4 * ROWS, 2 * ROWS, ROWS, ROWS // 2, ROWS // 2)
IN_BLOCKS = 26
WIDTH = IN_BLOCKS * COLS
OUT_BLOCKS = 6
SIDE_ROWS = 176
SIDE_LINKS = ("core", "rep", "y", "z", "far")


class Place:
    def __init__(self):
        self.me = lax.axis_index("shard")
        self.rep = lax.axis_index("rep")
        me = self.me
        self.bits = (me // 8 % 2, me // 4 % 2, me // 2 % 2, me % 2)
        flips = {"far": 0, "z": 1, "y": 2, "core": 3}
        self.targets = {
            name: (self.rep, self.owner(*(int(k == bit) for k in range(4)))) for name, bit in flips.items()
        }
        self.targets["rep"] = (1 - self.rep, me)

    def owner(self, far, z, y, core):
        bits = [1 - b if d else b for b, d in zip(self.bits, (far, z, y, core))]
        return bits[0] * 8 + bits[1] * 4 + bits[2] * 2 + bits[3]

    def greet(self):
        barrier = pltpu.get_barrier_semaphore()
        for target in self.targets.values():
            pl.semaphore_signal(barrier, inc=1, device_id=target, device_id_type=MESH)
        pl.semaphore_wait(barrier, len(self.targets))


class NoEngine:
    def open(self):
        pass

    def pump(self, now, pumps):
        pass

    def close(self, pumps):
        pass


class NoWork:
    name, inputs, in_specs, out_shapes, out_specs, scratch = "", [], [], [], [], []

    def engine(self, inputs, rest):
        return NoEngine()

    def params(self):
        return pltpu.CompilerParams(vmem_limit_bytes=48 * 2**20)


class Sums:
    def __init__(self, name, collective_id, segments, side=None):
        self.name, self.collective_id, self.has_side = name, collective_id, side is not None
        self.counts = [(left.shape[0], right.shape[1] // COLS) for left, right in segments]
        self.blocks = sum(k * n for k, n in self.counts)
        self.ticks = self.blocks + LAG * len(STAGES_B)
        self.inputs = [a for segment in segments for a in segment] + ([side] if self.has_side else [])
        once = lambda a: pl.BlockSpec(a.shape, lambda *_: (0,) * len(a.shape), pipeline_mode=pl.Buffered(1))
        self.in_specs = [once(a) for a in self.inputs]
        self.out_shapes = [jax.ShapeDtypeStruct((ROWS, self.blocks * COLS), F32)]
        if self.has_side:
            self.out_shapes.append(jax.ShapeDtypeStruct((len(SIDE_LINKS) + 1, SIDE_ROWS, 128), F32))
        self.out_specs = [once(a) for a in self.out_shapes]
        self.scratch = [pltpu.VMEM((16 * ROWS, COLS), F32)]
        for links, sizes in ((STAGES_A, SIZES_A), (STAGES_B, SIZES_B)):
            self.scratch += [pltpu.VMEM((SLOTS, r, HALF), BF) for r in sizes] * 2
            self.scratch += [pltpu.VMEM((SLOTS, r, HALF), F32) for r in sizes[:-1]]
            self.scratch += [pltpu.SemaphoreType.DMA((len(links), SLOTS))] * 2
        if self.has_side:
            self.scratch += [
                pltpu.VMEM((len(SIDE_LINKS), SIDE_ROWS, 128), F32),
                pltpu.SemaphoreType.DMA((2, len(SIDE_LINKS))),
            ]

    def params(self):
        return pltpu.CompilerParams(
            collective_id=self.collective_id, has_side_effects=True, vmem_limit_bytes=60 * 2**20
        )

    def engine(self, inputs, rest):
        return Engine(self, inputs, rest)


class Engine:
    def __init__(self, work, inputs, rest):
        self.work = work
        n_out = len(work.out_shapes)
        outs, rest = rest[:n_out], rest[n_out:]
        self.out_ref = outs[0]
        self.tmp, rest = rest[0], rest[1:]
        self.kinds = {}
        for kind, links in (("a", STAGES_A), ("b", STAGES_B)):
            n = len(links)
            src, rest = rest[:n], rest[n:]
            dst, rest = rest[:n], rest[n:]
            acc, rest = rest[: n - 1], rest[n - 1 :]
            self.kinds[kind] = (links, src, dst, acc, rest[0], rest[1])
            rest = rest[2:]
        if work.has_side:
            self.side_ref, self.side_out = inputs[-1], outs[1]
            self.side_in, self.side_sems = rest
        self.operands = [(inputs[2 * i], inputs[2 * i + 1]) for i in range(len(work.counts))]
        self.place = Place()

    def copy(self, kind, s, j):
        links, src, dst, _, ss, rs = self.kinds[kind]
        slot = j % SLOTS
        return pltpu.make_async_remote_copy(
            src_ref=src[s].at[slot],
            dst_ref=dst[s].at[slot],
            send_sem=ss.at[s, slot],
            recv_sem=rs.at[s, slot],
            device_id=self.place.targets[links[s]],
            device_id_type=MESH,
        )

    def multiply(self, j):
        first = 0
        for (left_ref, right_ref), (k, n) in zip(self.operands, self.work.counts):

            @pl.when((j >= first) & (j < first + k * n))
            def _():
                cols = pl.ds(pl.multiple_of((j - first) % n * COLS, COLS), COLS)
                self.tmp[...] = dot(left_ref[(j - first) // n], right_ref[:, cols])

            first += k * n

    def begin(self, j):
        slot = j % SLOTS
        self.multiply(j)
        place, rep = self.place, self.place.rep
        src_a, acc_a = self.kinds["a"][1][0], self.kinds["a"][3][0]
        src_b, acc_b = self.kinds["b"][1][0], self.kinds["b"][3][0]
        for d_core in range(2):
            for b in range(8):
                owner = place.owner(b & 1, b >> 1 & 1, b >> 2 & 1, d_core)
                block = self.tmp[pl.ds(pl.multiple_of(owner * ROWS, ROWS), ROWS), :HALF]
                to = slice(b * ROWS, (b + 1) * ROWS)
                if d_core:
                    src_a[slot, to, :] = block.astype(BF)
                else:
                    acc_a[slot, to, :] = block
                for d_rep in range(2):
                    top = owner * ROWS + (1 - rep if d_rep else rep) * (ROWS // 2)
                    block = self.tmp[pl.ds(pl.multiple_of(top, ROWS // 2), ROWS // 2), HALF:]
                    to = slice((d_rep * 8 + b) * (ROWS // 2), (d_rep * 8 + b + 1) * (ROWS // 2))
                    if d_core:
                        src_b[slot, to, :] = block.astype(BF)
                    else:
                        acc_b[slot, to, :] = block
        self.copy("a", 0, j).start()
        self.copy("b", 0, j).start()

    def go_on(self, kind, s, j):
        links, src, dst, acc, _, _ = self.kinds[kind]
        slot = j % SLOTS
        self.copy(kind, s - 1, j).wait()
        size = src[s].shape[1]
        if s == len(links) - 1:
            src[s][slot] = (acc[s - 1][slot] + dst[s - 1][slot].astype(F32)).astype(BF)
        else:
            src[s][slot] = (acc[s - 1][slot, size:, :] + dst[s - 1][slot, size:, :].astype(F32)).astype(BF)
            acc[s][slot] = acc[s - 1][slot, :size, :] + dst[s - 1][slot, :size, :].astype(F32)
        self.copy(kind, s, j).start()

    def finish(self, kind, j):
        links, src, dst, _, _, _ = self.kinds[kind]
        slot = j % SLOTS
        self.copy(kind, len(links) - 1, j).wait()
        rep = self.place.rep
        if kind == "a":
            cols = pl.ds(pl.multiple_of(j * COLS, HALF), HALF)
            self.out_ref[:, cols] = src[-1][slot].astype(F32) + dst[-1][slot].astype(F32)
        else:
            cols = pl.ds(pl.multiple_of(j * COLS + HALF, HALF), HALF)
            mine = pl.ds(pl.multiple_of(rep * (ROWS // 2), ROWS // 2), ROWS // 2)
            theirs = pl.ds(pl.multiple_of((1 - rep) * (ROWS // 2), ROWS // 2), ROWS // 2)
            self.out_ref[mine, cols] = src[-1][slot].astype(F32)
            self.out_ref[theirs, cols] = dst[-1][slot].astype(F32)

    def side_copy(self, k):
        return pltpu.make_async_remote_copy(
            src_ref=self.side_out.at[k],
            dst_ref=self.side_in.at[k],
            send_sem=self.side_sems.at[0, k],
            recv_sem=self.side_sems.at[1, k],
            device_id=self.place.targets[SIDE_LINKS[k]],
            device_id_type=MESH,
        )

    def open(self):
        self.place.greet()
        if self.work.has_side:
            self.side_out[0] = self.side_ref[...]
            self.side_copy(0).start()

    def tick(self, t):
        n_a, n_b = len(STAGES_A), len(STAGES_B)
        for s in range(n_b, -1, -1):
            j = t - LAG * s

            @pl.when((j >= 0) & (j < self.work.blocks))
            def _():
                if s == 0:
                    self.begin(j)
                    return
                if s < n_b:
                    self.go_on("b", s, j)
                else:
                    self.finish("b", j)
                if s < n_a:
                    self.go_on("a", s, j)
                elif s == n_a:
                    self.finish("a", j)

        if self.work.has_side:
            for k in range(len(SIDE_LINKS)):

                @pl.when(t == 4 * (k + 1))
                def _():
                    self.side_copy(k).wait()
                    self.side_out[k + 1] = self.side_out[k] + self.side_in[k]
                    if k + 1 < len(SIDE_LINKS):
                        self.side_copy(k + 1).start()

    def pump(self, now, pumps):
        ticks = min(self.work.ticks, pumps)
        t = now * ticks // pumps

        @pl.when((now + 1) * ticks // pumps > t)
        def _():
            self.tick(t)

    def close(self, pumps):
        if self.work.ticks > pumps:

            def more(t, _):
                self.tick(t)
                return 0

            lax.fori_loop(pumps, self.work.ticks, more, 0)


def last_kernel(work, dz_ref, w_ref, *rest):
    n = len(work.inputs)
    inputs, rest = rest[:n], rest[n:]
    dr_ref, rest = rest[0], rest[1:]
    wbuf, wsem = rest[-2:]
    engine = work.engine(inputs, rest[:-2])
    dx_ref, dbc_ref = inputs[1], inputs[3]

    def weights(k):
        cols = pl.ds(pl.multiple_of(k * COLS, COLS), COLS)
        return pltpu.make_async_copy(w_ref.at[:, cols], wbuf.at[k % 2], wsem.at[k % 2])

    weights(0).start()
    weights(1).start()
    engine.open()
    dr_ref[...] = jnp.zeros_like(dr_ref)
    bounds = ((dz_ref, 0, 2 * STEPS), (dx_ref, 2 * STEPS, 4 * STEPS), (dbc_ref, 4 * STEPS, IN_BLOCKS))

    def step(t, _):
        engine.tick(t)

        @pl.when(t < IN_BLOCKS)
        def _():
            weights(t).wait()
            for ref, lo, hi in bounds:

                @pl.when((t >= lo) & (t < hi))
                def _():
                    cols = pl.ds(pl.multiple_of((t - lo) * COLS, COLS), COLS)
                    dr_ref[...] += dot(ref[:, cols], wbuf[t % 2], NT)

            @pl.when(t + 2 < IN_BLOCKS)
            def _():
                weights(t + 2).start()

        return 0

    lax.fori_loop(0, max(work.ticks, IN_BLOCKS), step, 0)


def last_sums(dz, full_in, work):
    whole = lambda a: pl.BlockSpec(memory_space=pltpu.VMEM)
    out = pl.pallas_call(
        partial(last_kernel, work),
        out_shape=(jax.ShapeDtypeStruct((TOK, D), F32), *work.out_shapes),
        in_specs=[whole(dz), pl.BlockSpec(memory_space=pl.ANY), *map(whole, work.inputs)],
        out_specs=(whole(dz), *map(whole, work.out_shapes)),
        scratch_shapes=[*work.scratch, pltpu.VMEM((2, D, COLS), BF), pltpu.SemaphoreType.DMA((2,))],
        compiler_params=work.params(),
        cost_estimate=pl.CostEstimate(flops=2 * 10**10, bytes_accessed=50 * 2**20, transcendentals=0),
        name="last_sums",
    )(dz, full_in, *work.inputs)
    return out[0], out[1:]


def adamw_step(parameter, first_moment, second_moment, gradient, step_rate, decay_rate):
    first_new = BETA_ONE * first_moment + (1.0 - BETA_ONE) * gradient
    second_new = BETA_TWO * second_moment + (1.0 - BETA_TWO) * gradient * gradient
    correction_one = 1.0 - BETA_ONE**STEP
    correction_two = 1.0 - BETA_TWO**STEP
    update = first_new / correction_one / (jnp.sqrt(second_new / correction_two) + ADAM_EPSILON)
    return (parameter - step_rate * (update + decay_rate * parameter), first_new, second_new)


def adam_kernel(wi, mi, vi, wo, mo, vo, sums_1, sums_0, sums_last, *outs):
    layer = pl.program_id(0)
    n = INNER
    out = slice(0, 2 * D), slice(n + BC_WIDE, n + BC_WIDE + 2 * D)

    def update(refs, to, at, gradient):
        values = adamw_step(*(ref[at] for ref in refs), gradient, RATE_MATRIX, DECAY_MATRIX)
        for ref, value in zip(to, values):
            ref[at] = value

    def all_of(gates, rest, outputs):
        update((wi, mi, vi), outs[:3], (0, slice(None), slice(0, n)), gates[0][:, gates[1] : gates[1] + n])
        width = wi.shape[2] - n
        update((wi, mi, vi), outs[:3], (0, slice(None), slice(n, None)), rest[0][:, rest[1] : rest[1] + width])
        for q in range(2):
            lo = outputs[1] + q * D
            update((wo, mo, vo), outs[3:], (0, q), outputs[0][:, lo : lo + D])

    @pl.when(layer == 1)
    def _():
        all_of((sums_1, 2 * D), (sums_0, 0), (sums_1, 0))

    @pl.when(layer == 0)
    def _():
        all_of((sums_0, n + BC_WIDE + 2 * D), (sums_last, 0), (sums_0, n + BC_WIDE))


def adam(inputs, outputs, sums):
    part = 24
    outputs = [a.reshape(LAYERS, 2, ROWS, D) for a in outputs]
    width = inputs[0].shape[2]
    in_spec = pl.BlockSpec((1, part, width), lambda l, k: (l, k, 0))
    out_spec = pl.BlockSpec((1, 2, part, D), lambda l, k: (l, 0, k, 0))
    by_row = lambda l, k: (k, 0)
    only_0 = lambda l, k: (jnp.where(l == 0, k, ROWS // part - 1), 0)
    only_1 = lambda l, k: (jnp.where(l == 1, k, 0), 0)
    done = pl.pallas_call(
        adam_kernel,
        grid=(LAYERS, ROWS // part),
        out_shape=tuple(jax.ShapeDtypeStruct(a.shape, F32) for a in (*inputs, *outputs)),
        in_specs=[in_spec] * 3
        + [out_spec] * 3
        + [pl.BlockSpec((part, a.shape[1]), at) for a, at in zip(sums, (only_1, by_row, only_0))],
        out_specs=(in_spec,) * 3 + (out_spec,) * 3,
        compiler_params=pltpu.CompilerParams(vmem_limit_bytes=56 * 2**20),
        cost_estimate=pl.CostEstimate(flops=10**8, bytes_accessed=52 * 2**20, transcendentals=0),
        name="adam",
    )(*inputs, *outputs, *sums)
    return done[:3], [a.reshape(LAYERS, 2 * ROWS, D) for a in done[3:]]


GATHER_A = ("far", "z", "y", "core")
GATHER_B = ("far", "z", "y", "rep", "core")
GATHER_SLOTS = 6 * LAG


def gather_kernel(
    layer, blocks, w_in, w_out, r_ref, full_in, full_out, zx,
    own_in, own_out, buf_a, buf_b, natural, zbuf, local, flush, ss_a, rs_a, ss_b, rs_b,
):
    place = Place()
    rep = place.rep
    kinds = {"a": (GATHER_A, buf_a, ROWS, ss_a, rs_a), "b": (GATHER_B, buf_b, ROWS // 2, ss_b, rs_b)}
    valid = w_in.shape[2] - (IN_BLOCKS - 1) * COLS

    def copy(kind, s, j):
        links, buf, rows, ss, rs = kinds[kind]
        slot = j % GATHER_SLOTS
        size = rows << s
        return pltpu.make_async_remote_copy(
            src_ref=buf.at[slot, 0:size, :],
            dst_ref=buf.at[slot, size : 2 * size, :],
            send_sem=ss.at[s, slot],
            recv_sem=rs.at[s, slot],
            device_id=place.targets[links[s]],
            device_id_type=MESH,
        )

    def begin(j):
        slot = j % GATHER_SLOTS
        mine = pl.ds(pl.multiple_of(rep * (ROWS // 2), ROWS // 2), ROWS // 2)

        @pl.when(j < IN_BLOCKS - 1)
        def _():
            lo = pl.multiple_of(j * COLS, COLS)
            buf_a[slot, 0:ROWS, :] = own_in[:, pl.ds(lo, HALF)].astype(BF)
            buf_b[slot, 0 : ROWS // 2, :] = own_in[mine, pl.ds(pl.multiple_of(lo + HALF, HALF), HALF)].astype(BF)

        @pl.when(j == IN_BLOCKS - 1)
        def _():
            buf_a[slot, 0:ROWS, :] = jnp.zeros((ROWS, HALF), BF)
            buf_b[slot, 0 : ROWS // 2, :] = jnp.zeros((ROWS // 2, HALF), BF)
            buf_a[slot, 0:ROWS, 0:valid] = own_in[:, (IN_BLOCKS - 1) * COLS :].astype(BF)

        if blocks > IN_BLOCKS:

            @pl.when(j >= IN_BLOCKS)
            def _():
                k = j - IN_BLOCKS
                q = k // OUT_BLOCKS
                lo = pl.multiple_of(k % OUT_BLOCKS * COLS, COLS)
                top = pl.multiple_of(q * ROWS, ROWS)
                half = pl.ds(pl.multiple_of(q * ROWS + rep * (ROWS // 2), ROWS // 2), ROWS // 2)
                buf_a[slot, 0:ROWS, :] = own_out[pl.ds(top, ROWS), pl.ds(lo, HALF)].astype(BF)
                buf_b[slot, 0 : ROWS // 2, :] = own_out[half, pl.ds(pl.multiple_of(lo + HALF, HALF), HALF)].astype(BF)

        copy("a", 0, j).start()
        copy("b", 0, j).start()

    def out_copies(j):
        p = j % 2
        cols = pl.ds(pl.multiple_of(j * COLS, COLS), COLS)
        return (
            pltpu.make_async_copy(natural.at[p], full_in.at[:, :, cols], flush.at[0, p]),
            pltpu.make_async_copy(zbuf.at[p], zx.at[:, cols], flush.at[1, p]),
        )

    def row_copy(j):
        p = j % 2
        k = j - IN_BLOCKS
        cols = pl.ds(pl.multiple_of(k % OUT_BLOCKS * COLS, COLS), COLS)
        return pltpu.make_async_copy(natural.at[p], full_out.at[:, k // OUT_BLOCKS, :, cols], flush.at[0, p])

    def flushed(j):
        @pl.when((j >= 0) & (j < IN_BLOCKS))
        def _():
            for c in out_copies(j):
                c.wait()

        if blocks > IN_BLOCKS:

            @pl.when(j >= IN_BLOCKS)
            def _():
                row_copy(j).wait()

    def finish(j):
        slot = j % GATHER_SLOTS
        p = j % 2
        copy("b", len(GATHER_B) - 1, j).wait()
        flushed(j - 2)
        for k in range(16):
            owner = place.owner(k & 1, k >> 1 & 1, k >> 2 & 1, k >> 3)
            natural[p, owner, :, :HALF] = buf_a[slot, k * ROWS : (k + 1) * ROWS, :]
            for d_rep in range(2):
                at = (k & 7) + 8 * d_rep + 16 * (k >> 3)
                half = pl.ds(pl.multiple_of((1 - rep if d_rep else rep) * (ROWS // 2), ROWS // 2), ROWS // 2)
                natural[p, owner, half, HALF:] = buf_b[slot, at * (ROWS // 2) : (at + 1) * (ROWS // 2), :]

        @pl.when(j < IN_BLOCKS)
        def _():
            zbuf[p] = dot(r_ref[...], natural[p].reshape(16 * ROWS, COLS))
            for c in out_copies(j):
                c.start()

        if blocks > IN_BLOCKS:

            @pl.when(j >= IN_BLOCKS)
            def _():
                row_copy(j).start()

    loads = [pltpu.make_async_copy(w_in.at[layer], own_in, local.at[0])]
    loads.append(pltpu.make_async_copy(w_out.at[layer], own_out, local.at[1]))
    for load in loads:
        load.start()
    place.greet()
    for load in loads:
        load.wait()

    def tick(t, _):
        for s in range(len(GATHER_B), -1, -1):
            j = t - LAG * s

            @pl.when((j >= 0) & (j < blocks))
            def _():
                if s == 0:
                    begin(j)
                elif s == len(GATHER_B):
                    finish(j)
                else:
                    copy("b", s - 1, j).wait()
                    copy("b", s, j).start()
                    copy("a", s - 1, j).wait()
                    if s < len(GATHER_A):
                        copy("a", s, j).start()

        return 0

    lax.fori_loop(0, blocks + LAG * len(GATHER_B), tick, 0)
    flushed(jnp.int32(blocks - 2))
    flushed(jnp.int32(blocks - 1))


def gather_first(layer, weight_in, weight_out, normed):
    blocks = IN_BLOCKS + 2 * OUT_BLOCKS
    hbm = pl.BlockSpec(memory_space=pl.ANY)
    sems = pltpu.SemaphoreType.DMA
    full_in, full_out, zx = pl.pallas_call(
        partial(gather_kernel, layer, blocks),
        out_shape=(
            jax.ShapeDtypeStruct((16, ROWS, WIDTH), BF),
            jax.ShapeDtypeStruct((16, 2, ROWS, D), BF),
            jax.ShapeDtypeStruct((TOK, WIDTH), F32),
        ),
        in_specs=[hbm, hbm, pl.BlockSpec(memory_space=pltpu.VMEM)],
        out_specs=(hbm,) * 3,
        scratch_shapes=[
            pltpu.VMEM(weight_in.shape[1:], F32),
            pltpu.VMEM(weight_out.shape[1:], F32),
            pltpu.VMEM((GATHER_SLOTS, 16 * ROWS, HALF), BF),
            pltpu.VMEM((GATHER_SLOTS, 16 * ROWS, HALF), BF),
            pltpu.VMEM((2, 16, ROWS, COLS), BF),
            pltpu.VMEM((2, TOK, COLS), F32),
            sems((2,)),
            sems((2, 2)),
            sems((len(GATHER_A), GATHER_SLOTS)),
            sems((len(GATHER_A), GATHER_SLOTS)),
            sems((len(GATHER_B), GATHER_SLOTS)),
            sems((len(GATHER_B), GATHER_SLOTS)),
        ],
        compiler_params=pltpu.CompilerParams(
            collective_id=4, has_side_effects=True, vmem_limit_bytes=56 * 2**20
        ),
        cost_estimate=pl.CostEstimate(flops=10**10, bytes_accessed=50 * 2**20, transcendentals=0),
        name="gather_first",
    )(weight_in, weight_out, normed)
    return full_in.reshape(16 * ROWS, WIDTH), full_out.reshape(INNER, D), zx


def rows_kernel(normed_ref, mixed_ref, in_ref, out_ref):
    in_ref[0] = normed_ref[...].astype(F32).T.astype(BF)
    turned = mixed_ref[...].astype(F32).T.astype(BF)
    for i in range(turned.shape[0] // (2 * ROWS)):
        for q in range(2):
            lo = (2 * i + q) * ROWS
            out_ref[q, i * ROWS : (i + 1) * ROWS, :] = turned[lo : lo + ROWS]


def left_rows(normed, mixed):
    steps = 4
    wide = D // steps
    return pl.pallas_call(
        rows_kernel,
        grid=(steps,),
        out_shape=(
            jax.ShapeDtypeStruct((1, D, TOK), BF),
            jax.ShapeDtypeStruct((2, D, TOK), BF),
        ),
        in_specs=[
            pl.BlockSpec((TOK, wide), lambda k: (0, k)),
            pl.BlockSpec((TOK, 2 * wide), lambda k: (0, k)),
        ],
        out_specs=(
            pl.BlockSpec((1, wide, TOK), lambda k: (0, k, 0)),
            pl.BlockSpec((2, wide, TOK), lambda k: (0, k, 0)),
        ),
        compiler_params=pltpu.CompilerParams(vmem_limit_bytes=32 * 2**20),
        cost_estimate=pl.CostEstimate(flops=0, bytes_accessed=9 * 2**20, transcendentals=0),
        name="left_rows",
    )(normed, mixed)


def span_starts(seq_lengths):
    offsets = jnp.cumsum(seq_lengths) - seq_lengths
    places = jnp.arange(seq_lengths.shape[0], dtype=jnp.int32) * SPAN
    matches = (offsets[None, :] == places[:, None]) & (seq_lengths[None, :] > 0)
    return jnp.any(matches, axis=1)


def prenorm(hidden, gain):
    inverse = lax.rsqrt(jnp.mean(hidden * hidden, axis=-1, keepdims=True) + EPSILON)
    return hidden * inverse * gain


def swap(value, axis, count, bit):
    return lax.ppermute(value, axis, [(i, i ^ bit) for i in range(count)])


def plain_owner_sum(left, right, reps):
    mine = lax.psum_scatter(dot(left, right, TN).astype(BF), "shard", scatter_dimension=0, tiled=True)
    total = mine.astype(F32)
    for bit in [1 << k for k in range(reps.bit_length() - 1)]:
        total = total + swap(total.astype(BF), "rep", reps, bit).astype(F32)
    return total


def sum_everywhere(value, reps, shards):
    for axis, count in (("shard", shards), ("rep", reps)):
        bit = 1
        while bit < count:
            value = value + swap(value, axis, count, bit)
            bit *= 2
    return value


def side_block(*parts):
    flat = jnp.concatenate(parts)
    return jnp.pad(flat, (0, SIDE_ROWS * 128 - flat.shape[0])).reshape(SIDE_ROWS, 128)


def pad_cast(weight, width):
    return jnp.pad(weight.astype(BF), ((0, 0), (0, width - weight.shape[1])))


def sums_plain(normed, mixed, dz, dxs, dbc, low, full_in, side, reps):
    right = jnp.concatenate([dz, *dxs, dbc], axis=1)
    used = 2 * INNER + 2 * STATE + HEADS
    sum_in = plain_owner_sum(normed, right[:, :used], reps)
    sum_out = plain_owner_sum(mixed, low, reps)
    return sum_in, sum_out, dot(right, full_in, NT), lax.psum(side, ("rep", "shard"))


def per_device(
    tokens, cotangent, lengths,
    weight_in, moment_in, second_in,
    weight_out, moment_out, second_out,
    side_params, side_moment, side_second,
    *, reps, shards,
):
    direct = shards == 16 and reps == 2
    cont = jnp.where(span_starts(lengths[0])[1], 0.0, 1.0).astype(F32).reshape(1, 1)
    hidden = tokens.astype(F32)
    saved = []
    layer_outs = []
    shares = []
    for layer in range(LAYERS):
        normed, norm_pull = jax.vjp(prenorm, hidden, side_params[layer, :D])
        normed = normed.astype(BF)
        if direct and layer == 0:
            full_in, full_out, zx = gather_first(layer, weight_in, weight_out, normed)
            zx, later_in, later_out = lax.optimization_barrier((zx, weight_in[1], weight_out[1]))
            shares = [pad_cast(later_in, WIDTH)]
            shares += lax.optimization_barrier((later_out, shares[0]))[:1]
            shares = [lax.all_gather(w.astype(BF), "shard", axis=0, tiled=True) for w in shares]
        else:
            if direct:
                full_in, full_out = shares
            else:
                full_in = lax.all_gather(pad_cast(weight_in[layer], WIDTH), "shard", axis=0, tiled=True)
                full_out = lax.all_gather(weight_out[layer].astype(BF), "shard", axis=0, tiled=True)
            zx = jnp.dot(normed, full_in, preferred_element_type=F32)
        mixed, y, inverse = mixer_fwd(zx, cont, side_params[layer])
        left = None
        if direct:
            mixed, left = lax.optimization_barrier((mixed, left_rows(normed, mixed)))
        branch = jnp.dot(mixed, full_out, preferred_element_type=F32)
        hidden = hidden + branch
        layer_outs.append(hidden)
        saved.append((full_in, full_out, norm_pull, normed, zx, mixed, y, inverse, branch, left))
    gradient = cotangent.astype(F32)
    sums = [None] * LAYERS
    side_mixer = [None] * LAYERS
    side_norm = [None] * LAYERS
    held = []
    for layer in reversed(range(LAYERS)):
        full_in, full_out, norm_pull, normed, zx, mixed, y, inverse, branch, left = saved[layer]
        side_row = side_params[layer]
        low = gradient.astype(BF)
        factor = jnp.sum(low.astype(F32) * branch, axis=1, keepdims=True) * (1.0 / INNER)
        rows = jnp.concatenate([inverse[:, :1], factor, jnp.zeros((TOK, 126), F32)], axis=1)
        dz, dy, dgain = gate_bwd(low, full_out, zx, side_row, y, rows)
        work = NoWork()
        if direct and layer == 1:
            work = Sums("_1", 1, [(left[1], low), (left[0], dz)])
        elif direct:
            above = saved[1][-1]
            side = side_block(side_mixer[1], side_norm[1])
            work = Sums("_0", 2, [(above[0], held[0]), (above[0], held[1]), (left[1], low), (left[0], dz)], side)
        (dx, dskip, dcw, dbc, dcwbc, dhp), done = scan_bwd(zx, cont, side_row, y, dy, work)
        side_mixer[layer] = mixer_side(dgain, dskip, dcw, dcwbc, dhp)
        count = side_mixer[layer].shape[0]
        if not direct:
            sum_in, sum_out, back, side_mixer[layer] = sums_plain(
                normed, mixed, dz, [dx], dbc, low, full_in, side_mixer[layer], reps
            )
            sums[layer] = (sum_in, sum_out)
        elif layer == 1:
            sums_1 = done[0]
            held = [dx, dbc]
            back = back_to_input(dz, dx, dbc, full_in)
        else:
            sums_0, side = done
            side = side[-1].reshape(-1)
            side_mixer[1], side_norm[1] = side[:count], side[count : count + D]
            work = Sums("_last", 3, [(left[0], dx), (left[0], dbc)], side_block(side_mixer[0]))
            back, (sums_last, side) = last_sums(dz, full_in, work)
            side_mixer[0] = side[-1].reshape(-1)[:count]
        back_hidden, side_norm[layer] = norm_pull(back)
        gradient = gradient + back_hidden
    if direct:
        side_norm[0] = sum_everywhere(side_norm[0], reps, shards)
        new_in, new_out = adam(
            (weight_in, moment_in, second_in), (weight_out, moment_out, second_out), (sums_1, sums_0, sums_last)
        )
    else:
        side_norm = [lax.psum(s, ("rep", "shard")) for s in side_norm]
        grad_in = jnp.stack([s[0] for s in sums])
        grad_out = jnp.stack([s[1] for s in sums])
        new_in = adamw_step(weight_in, moment_in, second_in, grad_in, RATE_MATRIX, DECAY_MATRIX)
        new_out = adamw_step(weight_out, moment_out, second_out, grad_out, RATE_MATRIX, DECAY_MATRIX)
    grad_side = jnp.stack([jnp.concatenate(pair) for pair in zip(side_norm, side_mixer)])
    return (
        jnp.stack(layer_outs),
        gradient,
        *new_in,
        *new_out,
        *adamw_step(side_params, side_moment, side_second, grad_side, RATE_SIDE, 0.0),
    )


def solution(mesh):
    rows = P(("rep", "shard"), None)
    owned = P(None, "shard", None)
    body = partial(per_device, reps=mesh.shape["rep"], shards=mesh.shape["shard"])
    return jax.shard_map(
        body,
        mesh=mesh,
        in_specs=(rows, rows, rows) + (owned,) * 6 + (P(),) * 3,
        out_specs=(P(None, ("rep", "shard"), None), rows) + (owned,) * 6 + (P(),) * 3,
        check_vma=False,
    )
```

```python
from functools import partial

import jax
import jax.numpy as jnp
from jax import lax
from jax.experimental import pallas as pl
from jax.experimental.pallas import tpu as pltpu
from jax.sharding import PartitionSpec as P

LAYERS = 2
STEP = 10
BETA_ONE = 0.9
BETA_TWO = 0.95
ADAM_EPSILON = 1e-08
RATE_MATRIX = 0.05
RATE_SIDE = 0.5
DECAY_MATRIX = 0.1
D = 1536
INNER = 3072
HEAD_DIM = 64
STATE = 128
CONV = 4
SPAN = 256
HEADS = 48
XBC = 3328
TOK = 512
GROUP = 8
BC_WIDE = 512
N_SCAN_SCRATCH = 18
PUMPS = GROUP // 2 + 2
WIDE = GROUP * HEAD_DIM
STEPS = HEADS // GROUP
HALO = 8
LOG2_E = 1.4426950408889634
EPSILON = 1e-05
HIGHEST = lax.Precision.HIGHEST
BF = jnp.bfloat16
F32 = jnp.float32


def dot(a, b, dims=((1,), (0,)), precision=None):
    return lax.dot_general(a, b, (dims, ((), ())), precision=precision, preferred_element_type=F32)


NT = ((1,), (1,))
TN = ((0,), (0,))


def sigmoid(v):
    return 1.0 / (1.0 + jnp.exp(-v))


def softplus(v):
    e = jnp.exp(-jnp.abs(v))
    u = 1.0 + e
    tail = jnp.where(u == 1.0, e, jnp.log(u) * (e / jnp.where(u == 1.0, 1.0, u - 1.0)))
    return jnp.maximum(v, 0.0) + tail


def load_halo(buf, xin, cont, width):
    buf[0:HALO, :width] = jnp.zeros((HALO, width), F32)
    buf[HALO : HALO + SPAN, :width] = xin[0:SPAN]
    buf[HALO + SPAN : 2 * HALO + SPAN, :width] = xin[SPAN - HALO : SPAN] * cont
    buf[2 * HALO + SPAN : 2 * (HALO + SPAN), :width] = xin[SPAN : 2 * SPAN]


def shifted(buf, k, span, width, lo=0, rows=SPAN):
    base = span * (HALO + SPAN) + HALO - k + lo
    return buf[base : base + rows, :width]


def conv_of(buf, cw, span, width, lo=0, rows=SPAN):
    total = cw[4:5, :] + cw[3:4, :] * shifted(buf, 0, span, width, lo, rows)
    for k in range(1, CONV):
        total = total + cw[3 - k : 4 - k, :] * shifted(buf, k, span, width, lo, rows)
    return total


def lower_tri():
    return (
        lax.broadcasted_iota(jnp.int32, (SPAN, SPAN), 0)
        >= lax.broadcasted_iota(jnp.int32, (SPAN, SPAN), 1)
    )


def setup(cont, bc_ref, dt_ref, cwbc_ref, hp_ref, buf, bct, scores, dts, cum, cumt):
    load_halo(buf, bc_ref[...], cont, 2 * STATE)
    for span in range(2):
        lo = span * SPAN
        s = conv_of(buf, cwbc_ref[...], span, 2 * STATE)
        bct[lo : lo + SPAN, :] = (s * sigmoid(s)).astype(BF)
        sc = dot(bct[lo : lo + SPAN, STATE:], bct[lo : lo + SPAN, :STATE], NT)
        scores[lo : lo + SPAN, :] = jnp.where(lower_tri(), sc, 0.0)
    lane = lax.broadcasted_iota(jnp.int32, (TOK, 128), 1)
    raw = jnp.where(lane < HEADS, dt_ref[...], 0.0) + hp_ref[0:1, :]
    step = jnp.where(lane < HEADS, softplus(raw), 0.0)
    dts[...] = step
    a = (-LOG2_E * jnp.exp(hp_ref[1:2, :])) * step
    tri = jnp.where(lower_tri(), 1.0, 0.0)
    for span in range(2):
        lo = span * SPAN
        cum[lo : lo + SPAN, :] = dot(tri, a[lo : lo + SPAN, :], precision=HIGHEST)
    cumt[...] = cum[...].T


def head_sums(value, pick):
    total = None
    for _ in range(3):
        part = value.astype(BF)
        value = value - part.astype(F32)
        term = dot(part, pick)
        total = term if total is None else total + term
    return total


def pair_lanes(col, j, rows):
    lane = lax.broadcasted_iota(jnp.int32, (rows, 2 * HEAD_DIM), 1)
    return jnp.where(lane < HEAD_DIM, col[:, j : j + 1], col[:, j + 1 : j + 2])


def fwd_kernel(
    cont_ref, z_ref, x_ref, bc_ref, dt_ref, cwx_ref, cwbc_ref, hp_ref, cp_ref, gain_ref,
    m_ref, y_ref, inv_ref,
    buf, bct, scores, dts, cum, cumt, mix, xt, g_s, ssq, grp, state,
):
    g = pl.program_id(0)
    cont = cont_ref[0, 0]

    @pl.when(g == 0)
    def _():
        setup(cont, bc_ref, dt_ref, cwbc_ref, hp_ref, buf, bct, scores, dts, cum, cumt)
        ssq[...] = jnp.zeros_like(ssq)

    shift = lax.rem(128 - GROUP * g, 128)
    grp[0] = pltpu.roll(dts[...], shift, 1)
    grp[1] = pltpu.roll(cum[...], shift, 1)
    rows8 = cumt[pl.ds(pl.multiple_of(g * GROUP, GROUP), GROUP), :]
    load_halo(buf, x_ref[...], cont, WIDE)
    for span in range(2):
        lo = span * SPAN
        s = conv_of(buf, cwx_ref[...], span, WIDE)
        x = s * sigmoid(s)
        y_ref[lo : lo + SPAN, :] = x * cp_ref[1:2, :]
        for j in range(0, GROUP, 2):
            c0 = j * HEAD_DIM
            xt[lo : lo + SPAN, c0 : c0 + 128] = x[:, c0 : c0 + 128] * pair_lanes(
                grp[0, lo : lo + SPAN, :], j, SPAN
            )
    last = grp[1, SPAN - 1 : SPAN, :]
    w0 = jnp.exp2(last - grp[1, 0:SPAN, :])
    for j in range(0, GROUP, 2):
        c0 = j * HEAD_DIM
        xw = xt[0:SPAN, c0 : c0 + 128] * pair_lanes(w0, j, SPAN)
        st = dot(bct[0:SPAN, :STATE], xw.astype(BF), TN) * cont
        e1 = pair_lanes(jnp.exp2(grp[1, SPAN:, :]), j, SPAN)
        y_ref[SPAN:, c0 : c0 + 128] += e1 * dot(bct[SPAN:, STATE:], st.astype(BF))
    first = lax.broadcasted_iota(jnp.int32, (SPAN, 128), 1) < HEAD_DIM
    for span in range(2):
        lo = span * SPAN
        for j in range(0, GROUP, 2):
            slot = j // 2 % 2
            for h in range(2):
                fill_mix(mix, slot, h, scores, grp, rows8, span, j + h)
            cs = slice(j * HEAD_DIM, j * HEAD_DIM + 128)
            xp = xt[lo : lo + SPAN, cs]
            both = jnp.concatenate([jnp.where(first, xp, 0.0), jnp.where(first, 0.0, xp)], axis=0)
            y_ref[lo : lo + SPAN, cs] += dot(mix[slot], both.astype(BF))
    z = z_ref[...]
    gated = y_ref[...] * (z * sigmoid(z))
    g_s[g] = gated
    ssq[...] += jnp.broadcast_to(jnp.sum(gated * gated, axis=1, keepdims=True), ssq.shape)

    @pl.when(g == STEPS - 1)
    def _():
        inv = lax.rsqrt(ssq[...] * (1.0 / INNER) + EPSILON)
        inv_ref[...] = inv
        col = inv[:, 0:1]
        for k in range(STEPS):
            m_ref[:, k * WIDE : (k + 1) * WIDE] = (
                g_s[k] * col * gain_ref[0:1, k * WIDE : (k + 1) * WIDE]
            ).astype(BF)


CHUNK = 64


def fill_mix(mix, slot, h, scores, grp, rows8, span, j):
    lo = span * SPAN
    base = h * SPAN
    for r in range(0, SPAN, CHUNK):
        wide = 128 if r + CHUNK <= 128 else 256
        gap = grp[1, lo + r : lo + r + CHUNK, j : j + 1] - rows8[j : j + 1, lo : lo + wide]
        val = scores[lo + r : lo + r + CHUNK, :wide] * jnp.exp2(jnp.minimum(gap, 0.0))
        mix[slot, r : r + CHUNK, base : base + wide] = val.astype(BF)
        if wide < 256:
            mix[slot, r : r + CHUNK, base + wide : base + 256] = jnp.zeros((CHUNK, 256 - wide), BF)


def head_rows(side_row):
    cur = D + INNER + CONV * XBC + XBC
    rows = side_row[cur : cur + 3 * HEADS].reshape(3, HEADS)
    return jnp.pad(rows, ((0, 5), (0, 128 - HEADS)))


def conv_rows(side_row):
    cur = D + INNER
    rows = side_row[cur : cur + (CONV + 1) * XBC].reshape(CONV + 1, XBC)
    return jnp.pad(rows, ((0, 3), (0, 0)))


def column_rows(side_row):
    gain = side_row[D : D + INNER]
    skip = jnp.repeat(side_row[-HEADS:], HEAD_DIM)
    return jnp.pad(jnp.stack([gain, skip]), ((0, 6), (0, 0)))


def mixer_fwd(zx, cont, side_row):
    hp, cw, cp = head_rows(side_row), conv_rows(side_row), column_rows(side_row)
    full = lambda shape: pl.BlockSpec(shape, lambda g: (0,) * len(shape))
    return pl.pallas_call(
        fwd_kernel,
        grid=(STEPS,),
        out_shape=(
            jax.ShapeDtypeStruct((TOK, INNER), BF),
            jax.ShapeDtypeStruct((TOK, INNER), F32),
            jax.ShapeDtypeStruct((TOK, 128), F32),
        ),
        in_specs=[
            pl.BlockSpec(memory_space=pltpu.SMEM),
            pl.BlockSpec((TOK, WIDE), lambda g: (0, g)),
            pl.BlockSpec((TOK, WIDE), lambda g: (0, STEPS + g)),
            pl.BlockSpec((TOK, 2 * STATE), lambda g: (0, 2 * INNER // (2 * STATE))),
            pl.BlockSpec((TOK, 128), lambda g: (0, (INNER + XBC) // 128)),
            pl.BlockSpec((8, WIDE), lambda g: (0, g)),
            pl.BlockSpec((8, 2 * STATE), lambda g: (0, INNER // (2 * STATE))),
            full((8, 128)),
            pl.BlockSpec((8, WIDE), lambda g: (0, g)),
            full((8, INNER)),
        ],
        out_specs=(
            full((TOK, INNER)),
            pl.BlockSpec((TOK, WIDE), lambda g: (0, g)),
            full((TOK, 128)),
        ),
        scratch_shapes=[
            pltpu.VMEM((2 * (HALO + SPAN), WIDE), F32),
            pltpu.VMEM((TOK, 2 * STATE), BF),
            pltpu.VMEM((TOK, SPAN), F32),
            pltpu.VMEM((TOK, 128), F32),
            pltpu.VMEM((TOK, 128), F32),
            pltpu.VMEM((128, TOK), F32),
            pltpu.VMEM((2, SPAN, 2 * SPAN), BF),
            pltpu.VMEM((TOK, WIDE), F32),
            pltpu.VMEM((STEPS, TOK, WIDE), F32),
            pltpu.VMEM((TOK, 128), F32),
            pltpu.VMEM((2, TOK, 128), F32),
            pltpu.VMEM((STATE, WIDE), F32),
        ],
        compiler_params=pltpu.CompilerParams(vmem_limit_bytes=60 * 2**20),
        cost_estimate=pl.CostEstimate(flops=6 * 10**9, bytes_accessed=25 * 2**20, transcendentals=10**7),
        name="mixer_fwd",
    )(cont, zx, zx, zx, zx, cw, cw, hp, cp, cp)


def gate_kernel(low_ref, w_ref, z_ref, cp_ref, y_ref, row_ref, dz_ref, dy_ref, dgain_ref):
    dm = dot(low_ref[...], w_ref[...], NT)
    z = z_ref[...]
    sz = sigmoid(z)
    gate = z * sz
    y = y_ref[...]
    inv = row_ref[:, 0:1]
    gn = y * gate * inv
    dgain_ref[...] = jnp.zeros_like(dgain_ref)
    dgain_ref[0:1, :] = jnp.sum(dm * gn, axis=0, keepdims=True)
    dg = inv * (dm * cp_ref[0:1, :] - gn * row_ref[:, 1:2])
    dz_ref[...] = (dg * y * (sz * (1.0 + z * (1.0 - sz)))).astype(BF)
    dy_ref[...] = dg * gate


def gate_bwd(low, full_out, zx, side_row, y, rows):
    cp = column_rows(side_row)
    by_g = lambda rows_: pl.BlockSpec((rows_, WIDE), lambda g: (0, g))
    full = lambda shape: pl.BlockSpec(shape, lambda g: (0,) * len(shape))
    return pl.pallas_call(
        gate_kernel,
        grid=(STEPS,),
        out_shape=(
            jax.ShapeDtypeStruct((TOK, INNER), BF),
            jax.ShapeDtypeStruct((TOK, INNER), F32),
            jax.ShapeDtypeStruct((8, INNER), F32),
        ),
        in_specs=[
            full((TOK, D)),
            pl.BlockSpec((WIDE, D), lambda g: (g, 0)),
            by_g(TOK),
            by_g(8),
            by_g(TOK),
            full((TOK, 128)),
        ],
        out_specs=(by_g(TOK), by_g(TOK), by_g(8)),
        compiler_params=pltpu.CompilerParams(vmem_limit_bytes=60 * 2**20),
        cost_estimate=pl.CostEstimate(flops=5 * 10**9, bytes_accessed=40 * 2**20, transcendentals=2 * 10**6),
        name="gate_bwd",
    )(low, full_out, zx, cp, y, rows)


def scan_kernel(
    engine_of, n_engine_in,
    cont_ref, x_ref, bc_ref, dt_ref, cwx_ref, cwbc_ref, hp_ref, cp_ref, y_ref, dy, *rest,
):
    engine_in, rest = rest[:n_engine_in], rest[n_engine_in:]
    (dx_ref, dskip_ref, dcw_ref, dbc_ref, dcwbc_ref, dhp_ref), rest = rest[:6], rest[6:]
    (buf, bct, scores, dts, cum, cumt, mix, decay, xt, xf, sig, dsum, dxt, dscore, dbcs, dcum, ddt, grp), rest = (
        rest[-N_SCAN_SCRATCH:], rest[:-N_SCAN_SCRATCH]
    )
    engine = engine_of(engine_in, rest)
    g = pl.program_id(0)
    cont = cont_ref[0, 0]

    @pl.when(g == 0)
    def _():
        engine.open()

    engine.pump(g * PUMPS, STEPS * PUMPS)

    @pl.when(g == 0)
    def _():
        setup(cont, bc_ref, dt_ref, cwbc_ref, hp_ref, buf, bct, scores, dts, cum, cumt)
        for ref in (dscore, dbcs, dcum, ddt):
            ref[...] = jnp.zeros_like(ref)

    shift = lax.rem(128 - GROUP * g, 128)
    grp[0] = pltpu.roll(dts[...], shift, 1)
    grp[1] = pltpu.roll(cum[...], shift, 1)
    load_halo(buf, x_ref[...], cont, WIDE)
    skip = cp_ref[1:2, :]
    dskip_ref[...] = jnp.zeros_like(dskip_ref)
    pick = jnp.where(
        lax.broadcasted_iota(jnp.int32, (WIDE, 128), 0) // HEAD_DIM + GROUP * g
        == lax.broadcasted_iota(jnp.int32, (WIDE, 128), 1),
        1.0,
        0.0,
    ).astype(BF)
    for span in range(2):
        lo = span * SPAN
        hi = lo + SPAN
        s = conv_of(buf, cwx_ref[...], span, WIDE)
        sg = sigmoid(s)
        x = s * sg
        xf[lo:hi, :] = x
        sig[lo:hi, :] = sg * (1.0 + s * (1.0 - sg))
        for j in range(0, GROUP, 2):
            c0 = j * HEAD_DIM
            xt[lo:hi, c0 : c0 + 128] = x[:, c0 : c0 + 128] * pair_lanes(grp[0, lo:hi, :], j, SPAN)
        dyv = dy[lo:hi, :]
        dskip_ref[0:1, :] += jnp.sum(dyv * x, axis=0, keepdims=True)
        yin = y_ref[lo:hi, :] - skip * x
        dsum[lo:hi, :] = dyv.astype(BF).astype(F32) * yin

    last = grp[1, SPAN - 1 : SPAN, :]
    w0 = jnp.exp2(last - grp[1, 0:SPAN, :])
    ecum1 = jnp.exp2(grp[1, SPAN:, :])
    for j in range(0, GROUP, 2):
        cs = slice(j * HEAD_DIM, j * HEAD_DIM + 128)
        wl = pair_lanes(w0, j, SPAN)
        xw = (xt[0:SPAN, cs] * wl).astype(BF)
        prior = (dot(bct[0:SPAN, :STATE], xw, TN) * cont).astype(BF)
        dye = (dy[SPAN:, cs] * pair_lanes(ecum1, j, SPAN)).astype(BF)
        dprior = (dot(bct[SPAN:, STATE:], dye, TN) * cont).astype(BF)
        dbcs[SPAN:, STATE:] += dot(dye, prior, NT)
        dbcs[0:SPAN, :STATE] += dot(xw, dprior, NT)
        dxt[0:SPAN, cs] = dot(bct[0:SPAN, :STATE], dprior) * wl
        dxt[SPAN:, cs] = jnp.zeros((SPAN, 128), F32)
    through = dxt[0:SPAN, :] * xt[0:SPAN, :]
    dcum[SPAN - 1 : SPAN, :] += head_sums(jnp.sum(through, axis=0, keepdims=True), pick)

    first = lax.broadcasted_iota(jnp.int32, (SPAN, 128), 1) < HEAD_DIM

    def pair(j, _):
        cs = pl.ds(pl.multiple_of(j * 128, 128), 128)
        group_rows = cumt[pl.ds(pl.multiple_of(g * GROUP, GROUP), GROUP), :]
        row = pltpu.roll(group_rows, lax.rem(GROUP - 2 * j, GROUP), 0)
        cols = pltpu.roll(grp[1], lax.rem(128 - 2 * j, 128), 1)
        for span in range(2):
            lo = span * SPAN
            hi = lo + SPAN
            dyp = dy[lo:hi, cs]
            dyt = dyp.T.astype(BF)
            xtb = xt[lo:hi, cs].astype(BF)
            parts = []
            for h in range(2):
                k = 2 * span + h
                for r in range(0, SPAN, CHUNK):
                    wide = 128 if r + CHUNK <= 128 else 256
                    gap = cols[lo + r : lo + r + CHUNK, h : h + 1] - row[h : h + 1, lo : lo + wide]
                    e = jnp.exp2(jnp.minimum(gap, 0.0))
                    decay[k, r : r + CHUNK, :wide] = e
                    mix[k, r : r + CHUNK, :wide] = (scores[lo + r : lo + r + CHUNK, :wide] * e).astype(BF)
                    if wide < 256:
                        mix[k, r : r + CHUNK, wide:] = jnp.zeros((CHUNK, 256 - wide), BF)
                dmix = dot(jnp.where(first == (h == 0), dyp, 0.0).astype(BF), xtb, NT)
                top, low = dmix[:128, :128], dmix[128:, :]
                dscore[lo : lo + 128, :128] += top * decay[k, :128, :128]
                dscore[lo + 128 : hi, :] += low * decay[k, 128:, :]
                parts.append(dot(dyt[h * HEAD_DIM : (h + 1) * HEAD_DIM, :], mix[k]))
            dxt[lo:hi, cs] += jnp.concatenate(parts, axis=0).T
        engine.pump(g * PUMPS + 1 + j, STEPS * PUMPS)
        return 0

    lax.fori_loop(0, GROUP // 2, pair, 0)
    engine.pump(g * PUMPS + GROUP // 2 + 1, STEPS * PUMPS)

    dcw_ref[...] = jnp.zeros_like(dcw_ref)
    for span in range(2):
        lo = span * SPAN
        hi = lo + SPAN
        x = xf[lo:hi, :]
        xtv = xt[lo:hi, :]
        dv = dxt[lo:hi, :]
        dcum[lo:hi, :] += head_sums(dsum[lo:hi, :] - dv * xtv.astype(BF).astype(F32), pick)
        ddt[lo:hi, :] += head_sums(dv * x, pick)
        for j in range(0, GROUP, 2):
            cs = slice(j * HEAD_DIM, j * HEAD_DIM + 128)
            dc = dxt[lo:hi, cs] * pair_lanes(grp[0, lo:hi, :], j, SPAN) + dy[lo:hi, cs] * skip[:, cs]
            dxt[lo:hi, cs] = dc * sig[lo:hi, cs]
        conv_weights(dcw_ref, buf, dxt[lo:hi, :], span, WIDE)
    back_halo(buf, dxt[...], cont, WIDE)
    for span in range(2):
        lo = span * SPAN
        dx_ref[lo : lo + SPAN, :] = conv_back(buf, cwx_ref[...], span, WIDE).astype(BF)

    @pl.when(g == STEPS - 1)
    def _():
        load_halo(buf, bc_ref[...], cont, 2 * STATE)
        dcwbc_ref[...] = jnp.zeros_like(dcwbc_ref)
        for span in range(2):
            lo = span * SPAN
            hi = lo + SPAN
            ds = jnp.where(lower_tri(), dscore[lo:hi, :], 0.0).astype(BF)
            dbcs[lo:hi, :STATE] += dot(ds, bct[lo:hi, STATE:], TN)
            dbcs[lo:hi, STATE:] += dot(ds, bct[lo:hi, :STATE])
            s = conv_of(buf, cwbc_ref[...], span, 2 * STATE)
            sg = sigmoid(s)
            dcv = dbcs[lo:hi, :] * (sg * (1.0 + s * (1.0 - sg)))
            dbcs[lo:hi, :] = dcv
            conv_weights(dcwbc_ref, buf, dcv, span, 2 * STATE)
        back_halo(buf, dbcs[...], cont, 2 * STATE)
        for span in range(2):
            lo = span * SPAN
            dbc_ref[lo : lo + SPAN, : 2 * STATE] = conv_back(buf, cwbc_ref[...], span, 2 * STATE).astype(BF)
        lane = lax.broadcasted_iota(jnp.int32, (TOK, 128), 1)
        raw = jnp.where(lane < HEADS, dt_ref[...], 0.0) + hp_ref[0:1, :]
        decay_rate = -jnp.exp(hp_ref[1:2, :])
        tri = jnp.where(lower_tri(), 1.0, 0.0)
        da = jnp.concatenate(
            [dot(tri, dcum[lo : lo + SPAN, :], TN, HIGHEST) for lo in (0, SPAN)], axis=0
        )
        draw = jnp.where(lane < HEADS, (ddt[...] + decay_rate * da) * sigmoid(raw), 0.0)
        dbc_ref[:, 2 * STATE : 2 * STATE + 128] = draw.astype(BF)
        dbc_ref[:, 2 * STATE + 128 :] = jnp.zeros((TOK, BC_WIDE - 2 * STATE - 128), BF)
        dhp_ref[...] = jnp.zeros_like(dhp_ref)
        dhp_ref[0:1, :] = jnp.sum(draw, axis=0, keepdims=True)
        dhp_ref[1:2, :] = jnp.sum(da * decay_rate * dts[...], axis=0, keepdims=True)


def conv_weights(out, buf, dcv, span, width):
    for k in range(CONV):
        out[3 - k : 4 - k, :] += jnp.sum(dcv * shifted(buf, k, span, width), axis=0, keepdims=True)
    out[4:5, :] += jnp.sum(dcv, axis=0, keepdims=True)


def back_halo(buf, dcv, cont, width):
    buf[0:SPAN, :width] = dcv[0:SPAN]
    buf[SPAN : SPAN + HALO, :width] = dcv[SPAN : SPAN + HALO] * cont
    buf[SPAN + HALO : 2 * SPAN + HALO, :width] = dcv[SPAN:]
    buf[2 * SPAN + HALO : 2 * (SPAN + HALO), :width] = jnp.zeros((HALO, width), F32)


def conv_back(buf, cw, span, width):
    base = span * (SPAN + HALO)
    total = cw[3:4, :] * buf[base : base + SPAN, :width]
    for k in range(1, CONV):
        total = total + cw[3 - k : 4 - k, :] * buf[base + k : base + k + SPAN, :width]
    return total


def scan_bwd(zx, cont, side_row, y, dy, work):
    hp, cw, cp = head_rows(side_row), conv_rows(side_row), column_rows(side_row)
    full = lambda shape: pl.BlockSpec(shape, lambda g: (0,) * len(shape))
    by_g = lambda rows_: pl.BlockSpec((rows_, WIDE), lambda g: (0, g))
    shapes = (
        ((TOK, INNER), BF), ((8, INNER), F32), ((8, INNER), F32),
        ((TOK, BC_WIDE), BF), ((8, 2 * STATE), F32), ((8, 128), F32),
    )
    out = pl.pallas_call(
        partial(scan_kernel, work.engine, len(work.inputs)),
        grid=(STEPS,),
        out_shape=tuple(jax.ShapeDtypeStruct(*s) for s in shapes) + tuple(work.out_shapes),
        in_specs=[
            pl.BlockSpec(memory_space=pltpu.SMEM),
            pl.BlockSpec((TOK, WIDE), lambda g: (0, STEPS + g)),
            pl.BlockSpec((TOK, 2 * STATE), lambda g: (0, 2 * INNER // (2 * STATE))),
            pl.BlockSpec((TOK, 128), lambda g: (0, (INNER + XBC) // 128)),
            by_g(8),
            pl.BlockSpec((8, 2 * STATE), lambda g: (0, INNER // (2 * STATE))),
            full((8, 128)),
            by_g(8),
            by_g(TOK),
            by_g(TOK),
            *work.in_specs,
        ],
        out_specs=(by_g(TOK), by_g(8), by_g(8)) + tuple(full(s[0]) for s in shapes[3:]) + tuple(work.out_specs),
        scratch_shapes=[
            *work.scratch,
            pltpu.VMEM((2 * (HALO + SPAN), WIDE), F32),
            pltpu.VMEM((TOK, 2 * STATE), BF),
            pltpu.VMEM((TOK, SPAN), F32),
            pltpu.VMEM((TOK, 128), F32),
            pltpu.VMEM((TOK, 128), F32),
            pltpu.VMEM((128, TOK), F32),
            pltpu.VMEM((4, SPAN, SPAN), BF),
            pltpu.VMEM((4, SPAN, SPAN), F32),
            pltpu.VMEM((TOK, WIDE), F32),
            pltpu.VMEM((TOK, WIDE), F32),
            pltpu.VMEM((TOK, WIDE), F32),
            pltpu.VMEM((TOK, WIDE), F32),
            pltpu.VMEM((TOK, WIDE), F32),
            pltpu.VMEM((TOK, SPAN), F32),
            pltpu.VMEM((TOK, 2 * STATE), F32),
            pltpu.VMEM((TOK, 128), F32),
            pltpu.VMEM((TOK, 128), F32),
            pltpu.VMEM((2, TOK, 128), F32),
        ],
        compiler_params=work.params(),
        cost_estimate=pl.CostEstimate(flops=12 * 10**9, bytes_accessed=60 * 2**20, transcendentals=2 * 10**7),
        name=f"scan_bwd{work.name}",
    )(cont, zx, zx, zx, cw, cw, hp, cp, y, dy, *work.inputs)
    return out[:6], out[6:]


def mixer_side(dgain, dskip, dcw, dcwbc, dhp):
    return jnp.concatenate(
        [
            dgain[0],
            jnp.concatenate([dcw[: CONV + 1], dcwbc[: CONV + 1]], axis=1).reshape(-1),
            dhp[0, :HEADS],
            dhp[1, :HEADS],
            jnp.sum(dskip[0].reshape(HEADS, HEAD_DIM), axis=1),
        ]
    )


def back_kernel(dz_ref, dx_ref, dbc_ref, w_ref, out_ref):
    n = INNER
    total = dot(dz_ref[...], w_ref[:, :n], NT) + dot(dx_ref[...], w_ref[:, n : 2 * n], NT)
    out_ref[...] = total + dot(dbc_ref[...], w_ref[:, 2 * n :], NT)


def back_to_input(dz, dx, dbc, full_in):
    part = 256
    whole = lambda a: pl.BlockSpec(a.shape, lambda k: (0, 0), pipeline_mode=pl.Buffered(1))
    return pl.pallas_call(
        back_kernel,
        grid=(D // part,),
        out_shape=jax.ShapeDtypeStruct((TOK, D), F32),
        in_specs=[whole(dz), whole(dx), whole(dbc), pl.BlockSpec((part, full_in.shape[1]), lambda k: (k, 0))],
        out_specs=pl.BlockSpec((TOK, part), lambda k: (0, k)),
        compiler_params=pltpu.CompilerParams(vmem_limit_bytes=60 * 2**20),
        cost_estimate=pl.CostEstimate(flops=10**10, bytes_accessed=32 * 2**20, transcendentals=0),
        name="back_to_input",
    )(dz, dx, dbc, full_in)


ROWS = 96
COLS = 256
HALF = COLS // 2
LAG = 2
SLOTS = 2 * LAG
MESH = pl.DeviceIdType.MESH
STAGES_A = ("core", "y", "z", "far", "rep")
STAGES_B = ("core", "rep", "y", "z", "far", "rep")
STAGES_ODD = ("core", "rep", "z", "far", "y", "rep")
SIZES_A = (8 * ROWS, 4 * ROWS, 2 * ROWS, ROWS, ROWS)
SIZES_B = (8 * ROWS, 4 * ROWS, 2 * ROWS, ROWS, ROWS // 2, ROWS // 2)
IN_BLOCKS = 26
WIDTH = IN_BLOCKS * COLS
OUT_BLOCKS = 6
SIDE_ROWS = 176
SIDE_MIXER = 160
SIDE_LINKS = ("core", "rep", "y", "z", "far")


def choose(j, even, odd):
    return even + (odd - even) * (j % 2)


class Place:
    def __init__(self):
        self.me = lax.axis_index("shard")
        self.rep = lax.axis_index("rep")
        me = self.me
        self.bits = (me // 8 % 2, me // 4 % 2, me // 2 % 2, me % 2)
        flips = {"far": 0, "z": 1, "y": 2, "core": 3}
        self.targets = {
            name: (self.rep, self.owner(*(int(k == bit) for k in range(4)))) for name, bit in flips.items()
        }
        self.targets["rep"] = (1 - self.rep, me)

    def target(self, even, odd, j):
        if even == odd:
            return self.targets[even]
        return (self.rep, choose(j, self.targets[even][1], self.targets[odd][1]))

    def owner(self, far, z, y, core):
        bits = [1 - b if d else b for b, d in zip(self.bits, (far, z, y, core))]
        return bits[0] * 8 + bits[1] * 4 + bits[2] * 2 + bits[3]

    def greet(self):
        barrier = pltpu.get_barrier_semaphore()
        for target in self.targets.values():
            pl.semaphore_signal(barrier, inc=1, device_id=target, device_id_type=MESH)
        pl.semaphore_wait(barrier, len(self.targets))


class NoEngine:
    def open(self):
        pass

    def pump(self, now, pumps):
        pass


class NoWork:
    name, inputs, in_specs, out_shapes, out_specs, scratch = "", [], [], [], [], []

    def engine(self, inputs, rest):
        return NoEngine()

    def params(self):
        return pltpu.CompilerParams(vmem_limit_bytes=60 * 2**20)


class Sums:
    def __init__(self, name, collective_id, segments, side=None, late=None):
        self.late = late
        self.name, self.collective_id, self.has_side = name, collective_id, side is not None
        self.counts = [(left.shape[0], right.shape[1] // COLS) for left, right in segments]
        self.blocks = sum(k * n for k, n in self.counts)
        self.ticks = self.blocks + LAG * len(STAGES_B)
        self.inputs = [a for segment in segments for a in segment] + ([side] if self.has_side else [])
        once = lambda a: pl.BlockSpec(a.shape, lambda *_: (0,) * len(a.shape), pipeline_mode=pl.Buffered(1))
        self.in_specs = [once(a) for a in self.inputs]
        self.out_shapes = [jax.ShapeDtypeStruct((ROWS, self.blocks * COLS), F32)]
        if self.has_side:
            self.out_shapes.append(jax.ShapeDtypeStruct((len(SIDE_LINKS) + 1, SIDE_ROWS, 128), F32))
        self.out_specs = [once(a) for a in self.out_shapes]
        self.scratch = [pltpu.VMEM((16 * ROWS, COLS), F32)]
        for links, sizes in ((STAGES_A, SIZES_A), (STAGES_B, SIZES_B)):
            self.scratch += [pltpu.VMEM((SLOTS, r, HALF), BF) for r in sizes] * 2
            self.scratch += [pltpu.VMEM((SLOTS, r, HALF), F32) for r in sizes[:-1]]
            self.scratch += [pltpu.SemaphoreType.DMA((len(links), SLOTS))] * 2
        if self.has_side:
            self.scratch += [
                pltpu.VMEM((len(SIDE_LINKS), SIDE_ROWS, 128), F32),
                pltpu.SemaphoreType.DMA((2, len(SIDE_LINKS))),
            ]

    def params(self):
        return pltpu.CompilerParams(
            collective_id=self.collective_id, has_side_effects=True, vmem_limit_bytes=60 * 2**20
        )

    def engine(self, inputs, rest):
        return Engine(self, inputs, rest)


class Engine:
    def __init__(self, work, inputs, rest):
        self.work = work
        n_out = len(work.out_shapes)
        outs, rest = rest[:n_out], rest[n_out:]
        self.out_ref = outs[0]
        self.tmp, rest = rest[0], rest[1:]
        self.kinds = {}
        for kind, links in (("a", STAGES_A), ("b", STAGES_B)):
            n = len(links)
            src, rest = rest[:n], rest[n:]
            dst, rest = rest[:n], rest[n:]
            acc, rest = rest[: n - 1], rest[n - 1 :]
            self.kinds[kind] = (links, src, dst, acc, rest[0], rest[1])
            rest = rest[2:]
        if work.has_side:
            self.side_ref, self.side_out = inputs[-1], outs[1]
            self.side_in, self.side_sems = rest
        self.operands = [(inputs[2 * i], inputs[2 * i + 1]) for i in range(len(work.counts))]
        self.place = Place()

    def copy(self, kind, s, j):
        links, src, dst, _, ss, rs = self.kinds[kind]
        slot = j % SLOTS
        return pltpu.make_async_remote_copy(
            src_ref=src[s].at[slot],
            dst_ref=dst[s].at[slot],
            send_sem=ss.at[s, slot],
            recv_sem=rs.at[s, slot],
            device_id=self.place.target(links[s], STAGES_ODD[s] if kind == "b" else links[s], j),
            device_id_type=MESH,
        )

    def multiply(self, j):
        first = 0
        for (left_ref, right_ref), (k, n) in zip(self.operands, self.work.counts):

            @pl.when((j >= first) & (j < first + k * n))
            def _():
                cols = pl.ds(pl.multiple_of((j - first) % n * COLS, COLS), COLS)
                self.tmp[...] = dot(left_ref[(j - first) // n], right_ref[:, cols])

            first += k * n

    def begin(self, j):
        slot = j % SLOTS
        self.multiply(j)
        place, rep = self.place, self.place.rep
        src_a, acc_a = self.kinds["a"][1][0], self.kinds["a"][3][0]
        src_b, acc_b = self.kinds["b"][1][0], self.kinds["b"][3][0]
        for d_core in range(2):
            for b in range(8):
                owner = place.owner(b & 1, b >> 1 & 1, b >> 2 & 1, d_core)
                block = self.tmp[pl.ds(pl.multiple_of(owner * ROWS, ROWS), ROWS), :HALF]
                to = slice(b * ROWS, (b + 1) * ROWS)
                if d_core:
                    src_a[slot, to, :] = block.astype(BF)
                else:
                    acc_a[slot, to, :] = block
                owner = choose(j, owner, place.owner(b >> 1 & 1, b >> 2 & 1, b & 1, d_core))
                for d_rep in range(2):
                    top = owner * ROWS + (1 - rep if d_rep else rep) * (ROWS // 2)
                    block = self.tmp[pl.ds(pl.multiple_of(top, ROWS // 2), ROWS // 2), HALF:]
                    to = slice((d_rep * 8 + b) * (ROWS // 2), (d_rep * 8 + b + 1) * (ROWS // 2))
                    if d_core:
                        src_b[slot, to, :] = block.astype(BF)
                    else:
                        acc_b[slot, to, :] = block
        self.copy("a", 0, j).start()
        self.copy("b", 0, j).start()

    def go_on(self, kind, s, j):
        links, src, dst, acc, _, _ = self.kinds[kind]
        slot = j % SLOTS
        self.copy(kind, s - 1, j).wait()
        size = src[s].shape[1]
        if s == len(links) - 1:
            src[s][slot] = (acc[s - 1][slot] + dst[s - 1][slot].astype(F32)).astype(BF)
        else:
            src[s][slot] = (acc[s - 1][slot, size:, :] + dst[s - 1][slot, size:, :].astype(F32)).astype(BF)
            acc[s][slot] = acc[s - 1][slot, :size, :] + dst[s - 1][slot, :size, :].astype(F32)
        self.copy(kind, s, j).start()

    def finish(self, kind, j):
        links, src, dst, _, _, _ = self.kinds[kind]
        slot = j % SLOTS
        self.copy(kind, len(links) - 1, j).wait()
        rep = self.place.rep
        if kind == "a":
            cols = pl.ds(pl.multiple_of(j * COLS, HALF), HALF)
            self.out_ref[:, cols] = src[-1][slot].astype(F32) + dst[-1][slot].astype(F32)
        else:
            cols = pl.ds(pl.multiple_of(j * COLS + HALF, HALF), HALF)
            mine = pl.ds(pl.multiple_of(rep * (ROWS // 2), ROWS // 2), ROWS // 2)
            theirs = pl.ds(pl.multiple_of((1 - rep) * (ROWS // 2), ROWS // 2), ROWS // 2)
            self.out_ref[mine, cols] = src[-1][slot].astype(F32)
            self.out_ref[theirs, cols] = dst[-1][slot].astype(F32)

    def side_copy(self, k):
        return pltpu.make_async_remote_copy(
            src_ref=self.side_out.at[k],
            dst_ref=self.side_in.at[k],
            send_sem=self.side_sems.at[0, k],
            recv_sem=self.side_sems.at[1, k],
            device_id=self.place.targets[SIDE_LINKS[k]],
            device_id_type=MESH,
        )

    def open(self):
        self.place.greet()
        if self.work.has_side:
            self.side_out[0] = self.side_ref[...]
            if self.work.late is None:
                self.side_copy(0).start()

    def open_side(self, row):
        for k in range(D // 128):
            self.side_out[0, SIDE_MIXER + k : SIDE_MIXER + k + 1, :] = row[:, k * 128 : (k + 1) * 128]
        self.side_copy(0).start()

    def tick(self, t):
        n_a, n_b = len(STAGES_A), len(STAGES_B)
        for s in range(n_b, -1, -1):
            j = t - LAG * s

            @pl.when((j >= 0) & (j < self.work.blocks))
            def _():
                if s == 0:
                    self.begin(j)
                    return
                if s < n_b:
                    self.go_on("b", s, j)
                else:
                    self.finish("b", j)
                if s < n_a:
                    self.go_on("a", s, j)
                elif s == n_a:
                    self.finish("a", j)

        if self.work.has_side:
            for k in range(len(SIDE_LINKS)):

                @pl.when(t == (4 * (k + 1) if self.work.late is None else self.work.late + 2 * (k + 1)))
                def _():
                    self.side_copy(k).wait()
                    self.side_out[k + 1] = self.side_out[k] + self.side_in[k]
                    if k + 1 < len(SIDE_LINKS):
                        self.side_copy(k + 1).start()

    def pump(self, now, pumps):
        def more(t, _):
            self.tick(t)
            return 0

        ticks = self.work.ticks
        lax.fori_loop(now * ticks // pumps, (now + 1) * ticks // pumps, more, 0)


def last_kernel(work, dz_ref, h_ref, norm_ref, w_ref, *rest):
    n = len(work.inputs)
    inputs, rest = rest[:n], rest[n:]
    dr_ref, rest = rest[0], rest[1:]
    wbuf, wsem = rest[-2:]
    engine = work.engine(inputs, rest[:-2])
    dx_ref, dbc_ref = inputs[1], inputs[3]

    def weights(k):
        cols = pl.ds(pl.multiple_of(k * WIDE, WIDE), WIDE)
        return pltpu.make_async_copy(w_ref.at[:, cols], wbuf.at[k % 2], wsem.at[k % 2])

    weights(0).start()
    weights(1).start()
    engine.open()
    dr_ref[...] = jnp.zeros_like(dr_ref)
    count = 2 * STEPS + 1
    bounds = ((dz_ref, 0, STEPS), (dx_ref, STEPS, 2 * STEPS), (dbc_ref, 2 * STEPS, count))

    def step(t, _):
        engine.tick(t)

        @pl.when(t < count)
        def _():
            weights(t).wait()
            for ref, lo, hi in bounds:

                @pl.when((t >= lo) & (t < hi))
                def _():
                    cols = pl.ds(pl.multiple_of((t - lo) * WIDE, WIDE), WIDE)
                    dr_ref[...] += dot(ref[:, cols], wbuf[t % 2], NT)

            @pl.when(t + 2 < count)
            def _():
                weights(t + 2).start()

        @pl.when(t == count)
        def _():
            scaled = h_ref[...] * norm_ref[:, 0:1]
            engine.open_side(jnp.sum(dr_ref[...] * scaled, axis=0, keepdims=True))

        return 0

    lax.fori_loop(0, work.ticks, step, 0)
    dr_ref[...] = norm_gradient(dr_ref[...], h_ref[...], norm_ref[:, 0:1], norm_ref[0:1, 128:])


def norm_gradient(dr, h, inverse, gain):
    scaled = h * inverse
    dn = dr * gain
    return inverse * (dn - scaled * (jnp.sum(dn * scaled, axis=1, keepdims=True) * (1.0 / D)))


def last_sums(dz, hidden, norm_rows, full_in, work):
    whole = lambda a: pl.BlockSpec(memory_space=pltpu.VMEM)
    out = pl.pallas_call(
        partial(last_kernel, work),
        out_shape=(jax.ShapeDtypeStruct((TOK, D), F32), *work.out_shapes),
        in_specs=[whole(dz)] * 3 + [pl.BlockSpec(memory_space=pl.ANY), *map(whole, work.inputs)],
        out_specs=(whole(dz), *map(whole, work.out_shapes)),
        scratch_shapes=[*work.scratch, pltpu.VMEM((2, D, WIDE), BF), pltpu.SemaphoreType.DMA((2,))],
        compiler_params=work.params(),
        cost_estimate=pl.CostEstimate(flops=2 * 10**10, bytes_accessed=50 * 2**20, transcendentals=0),
        name="last_sums",
    )(dz, hidden, norm_rows, full_in, *work.inputs)
    return out[0], out[1:]


def norm_kernel(dr_ref, h_ref, norm_ref, e_ref, branch_ref, e_out, low_out, factor_out, dgain_out):
    @pl.when(pl.program_id(0) == 0)
    def _():
        dgain_out[...] = jnp.zeros_like(dgain_out)

    dr, h, inverse = dr_ref[...], h_ref[...], norm_ref[:, 0:1]
    dgain_out[0:1, :] += jnp.sum(dr * (h * inverse), axis=0, keepdims=True)
    e = e_ref[...] + norm_gradient(dr, h, inverse, norm_ref[0:1, 128:])
    low = e.astype(BF)
    e_out[...] = e
    low_out[...] = low
    factor = jnp.sum(low.astype(F32) * branch_ref[...], axis=1, keepdims=True) * (1.0 / INNER)
    factor_out[...] = jnp.broadcast_to(factor, factor_out.shape)


def norm_back(dr, hidden, norm_rows, gradient, branch):
    part = 128
    rows = lambda a: pl.BlockSpec((part, a), lambda k: (k, 0))
    shape = lambda a, t: jax.ShapeDtypeStruct(a, t)
    return pl.pallas_call(
        norm_kernel,
        grid=(TOK // part,),
        out_shape=(shape((TOK, D), F32), shape((TOK, D), BF), shape((TOK, 128), F32), shape((8, D), F32)),
        in_specs=[rows(D), rows(D), rows(128 + D), rows(D), rows(D)],
        out_specs=(rows(D), rows(D), rows(128), pl.BlockSpec((8, D), lambda k: (0, 0))),
        compiler_params=pltpu.CompilerParams(vmem_limit_bytes=60 * 2**20),
        cost_estimate=pl.CostEstimate(flops=10**7, bytes_accessed=18 * 2**20, transcendentals=0),
        name="norm_back",
    )(dr, hidden, norm_rows, gradient, branch)


def adamw_step(parameter, first_moment, second_moment, gradient, step_rate, decay_rate):
    first_new = BETA_ONE * first_moment + (1.0 - BETA_ONE) * gradient
    second_new = BETA_TWO * second_moment + (1.0 - BETA_TWO) * gradient * gradient
    correction_one = 1.0 - BETA_ONE**STEP
    correction_two = 1.0 - BETA_TWO**STEP
    update = first_new / correction_one / (jnp.sqrt(second_new / correction_two) + ADAM_EPSILON)
    return (parameter - step_rate * (update + decay_rate * parameter), first_new, second_new)


def adam_kernel(wi, mi, vi, wo, mo, vo, sums_1, sums_0, sums_last, *outs):
    layer = pl.program_id(0)
    n = INNER
    out = slice(0, 2 * D), slice(n + BC_WIDE, n + BC_WIDE + 2 * D)

    def update(refs, to, at, gradient):
        values = adamw_step(*(ref[at] for ref in refs), gradient, RATE_MATRIX, DECAY_MATRIX)
        for ref, value in zip(to, values):
            ref[at] = value

    def all_of(gates, rest, outputs):
        update((wi, mi, vi), outs[:3], (0, slice(None), slice(0, n)), gates[0][:, gates[1] : gates[1] + n])
        width = wi.shape[2] - n
        update((wi, mi, vi), outs[:3], (0, slice(None), slice(n, None)), rest[0][:, rest[1] : rest[1] + width])
        for q in range(2):
            lo = outputs[1] + q * D
            update((wo, mo, vo), outs[3:], (0, q), outputs[0][:, lo : lo + D])

    @pl.when(layer == 1)
    def _():
        all_of((sums_1, 2 * D), (sums_0, 0), (sums_1, 0))

    @pl.when(layer == 0)
    def _():
        all_of((sums_0, n + BC_WIDE + 2 * D), (sums_last, 0), (sums_0, n + BC_WIDE))


def adam(inputs, outputs, sums):
    part = 24
    outputs = [a.reshape(LAYERS, 2, ROWS, D) for a in outputs]
    width = inputs[0].shape[2]
    in_spec = pl.BlockSpec((1, part, width), lambda l, k: (l, k, 0))
    out_spec = pl.BlockSpec((1, 2, part, D), lambda l, k: (l, 0, k, 0))
    by_row = lambda l, k: (k, 0)
    only_0 = lambda l, k: (jnp.where(l == 0, k, ROWS // part - 1), 0)
    only_1 = lambda l, k: (jnp.where(l == 1, k, 0), 0)
    done = pl.pallas_call(
        adam_kernel,
        grid=(LAYERS, ROWS // part),
        out_shape=tuple(jax.ShapeDtypeStruct(a.shape, F32) for a in (*inputs, *outputs)),
        in_specs=[in_spec] * 3
        + [out_spec] * 3
        + [pl.BlockSpec((part, a.shape[1]), at) for a, at in zip(sums, (only_1, by_row, only_0))],
        out_specs=(in_spec,) * 3 + (out_spec,) * 3,
        compiler_params=pltpu.CompilerParams(vmem_limit_bytes=60 * 2**20),
        cost_estimate=pl.CostEstimate(flops=10**8, bytes_accessed=52 * 2**20, transcendentals=0),
        name="adam",
    )(*inputs, *outputs, *sums)
    return done[:3], [a.reshape(LAYERS, 2 * ROWS, D) for a in done[3:]]


GATHER_A = ("far", "z", "y", "core")
GATHER_B = ("far", "z", "y", "rep", "core")
GATHER_ODD = ("y", "far", "z", "rep", "core")
GATHER_SLOTS = 6 * LAG


def gather_kernel(
    blocks, w_in, w_out, r_ref, full_in, full_out, zx,
    own_in, own_out, buf_a, buf_b, natural, zbuf, local, flush, ss_a, rs_a, ss_b, rs_b,
):
    place = Place()
    rep = place.rep
    kinds = {"a": (GATHER_A, buf_a, ROWS, ss_a, rs_a), "b": (GATHER_B, buf_b, ROWS // 2, ss_b, rs_b)}
    valid = w_in.shape[2] - (IN_BLOCKS - 1) * COLS

    def copy(kind, s, j):
        links, buf, rows, ss, rs = kinds[kind]
        slot = j % GATHER_SLOTS
        size = rows << s
        return pltpu.make_async_remote_copy(
            src_ref=buf.at[slot, 0:size, :],
            dst_ref=buf.at[slot, size : 2 * size, :],
            send_sem=ss.at[s, slot],
            recv_sem=rs.at[s, slot],
            device_id=place.target(links[s], GATHER_ODD[s] if kind == "b" else links[s], j),
            device_id_type=MESH,
        )

    def begin(j):
        slot = j % GATHER_SLOTS
        mine = pl.ds(pl.multiple_of(rep * (ROWS // 2), ROWS // 2), ROWS // 2)

        @pl.when(j < IN_BLOCKS - 1)
        def _():
            lo = pl.multiple_of(j * COLS, COLS)
            buf_a[slot, 0:ROWS, :] = own_in[:, pl.ds(lo, HALF)].astype(BF)
            buf_b[slot, 0 : ROWS // 2, :] = own_in[mine, pl.ds(pl.multiple_of(lo + HALF, HALF), HALF)].astype(BF)

        @pl.when(j == IN_BLOCKS - 1)
        def _():
            buf_a[slot, 0:ROWS, :] = jnp.zeros((ROWS, HALF), BF)
            buf_b[slot, 0 : ROWS // 2, :] = jnp.zeros((ROWS // 2, HALF), BF)
            buf_a[slot, 0:ROWS, 0:valid] = own_in[:, (IN_BLOCKS - 1) * COLS :].astype(BF)

        if blocks > IN_BLOCKS:

            @pl.when(j >= IN_BLOCKS)
            def _():
                k = j - IN_BLOCKS
                q = k // OUT_BLOCKS
                lo = pl.multiple_of(k % OUT_BLOCKS * COLS, COLS)
                buf_a[slot, 0:ROWS, :] = own_out[q, :, pl.ds(lo, HALF)].astype(BF)
                buf_b[slot, 0 : ROWS // 2, :] = own_out[q, mine, pl.ds(pl.multiple_of(lo + HALF, HALF), HALF)].astype(BF)

        copy("a", 0, j).start()
        copy("b", 0, j).start()

    def out_copies(j):
        p = j % 2
        cols = pl.ds(pl.multiple_of(j * COLS, COLS), COLS)
        return (
            pltpu.make_async_copy(natural.at[p], full_in.at[:, :, cols], flush.at[0, p]),
            pltpu.make_async_copy(zbuf.at[p], zx.at[:, cols], flush.at[1, p]),
        )

    def row_copy(j):
        p = j % 2
        k = j - IN_BLOCKS
        cols = pl.ds(pl.multiple_of(k % OUT_BLOCKS * COLS, COLS), COLS)
        q = k // OUT_BLOCKS
        return pltpu.make_async_copy(natural.at[p], full_out.at[q // 2, :, q % 2, :, cols], flush.at[0, p])

    def flushed(j):
        @pl.when((j >= 0) & (j < IN_BLOCKS))
        def _():
            for c in out_copies(j):
                c.wait()

        if blocks > IN_BLOCKS:

            @pl.when(j >= IN_BLOCKS)
            def _():
                row_copy(j).wait()

    def finish(j):
        slot = j % GATHER_SLOTS
        p = j % 2
        copy("b", len(GATHER_B) - 1, j).wait()
        flushed(j - 2)
        for k in range(16):
            owner = place.owner(k & 1, k >> 1 & 1, k >> 2 & 1, k >> 3)
            natural[p, owner, :, :HALF] = buf_a[slot, k * ROWS : (k + 1) * ROWS, :]
            owner = choose(j, owner, place.owner(k >> 1 & 1, k >> 2 & 1, k & 1, k >> 3))
            for d_rep in range(2):
                at = (k & 7) + 8 * d_rep + 16 * (k >> 3)
                half = pl.ds(pl.multiple_of((1 - rep if d_rep else rep) * (ROWS // 2), ROWS // 2), ROWS // 2)
                natural[p, owner, half, HALF:] = buf_b[slot, at * (ROWS // 2) : (at + 1) * (ROWS // 2), :]

        @pl.when(j < IN_BLOCKS)
        def _():
            zbuf[p] = dot(r_ref[...], natural[p].reshape(16 * ROWS, COLS))
            for c in out_copies(j):
                c.start()

        if blocks > IN_BLOCKS:

            @pl.when(j >= IN_BLOCKS)
            def _():
                row_copy(j).start()

    loads = [pltpu.make_async_copy(w_in.at[0], own_in, local.at[0])]
    loads.append(pltpu.make_async_copy(w_out, own_out, local.at[1]))
    for load in loads:
        load.start()
    place.greet()
    for load in loads:
        load.wait()

    def tick(t, _):
        for s in range(len(GATHER_B), -1, -1):
            j = t - LAG * s

            @pl.when((j >= 0) & (j < blocks))
            def _():
                if s == 0:
                    begin(j)
                elif s == len(GATHER_B):
                    finish(j)
                else:
                    copy("b", s - 1, j).wait()
                    copy("b", s, j).start()
                    copy("a", s - 1, j).wait()
                    if s < len(GATHER_A):
                        copy("a", s, j).start()

        return 0

    lax.fori_loop(0, blocks + LAG * len(GATHER_B), tick, 0)
    flushed(jnp.int32(blocks - 2))
    flushed(jnp.int32(blocks - 1))


def gather_first(weight_in, weight_out, normed):
    outs = weight_out.reshape(2 * LAYERS, ROWS, D)
    blocks = IN_BLOCKS + outs.shape[0] * OUT_BLOCKS
    hbm = pl.BlockSpec(memory_space=pl.ANY)
    sems = pltpu.SemaphoreType.DMA
    full_in, full_out, zx = pl.pallas_call(
        partial(gather_kernel, blocks),
        out_shape=(
            jax.ShapeDtypeStruct((16, ROWS, WIDTH), BF),
            jax.ShapeDtypeStruct((LAYERS, 16, 2, ROWS, D), BF),
            jax.ShapeDtypeStruct((TOK, WIDTH), F32),
        ),
        in_specs=[hbm, hbm, pl.BlockSpec(memory_space=pltpu.VMEM)],
        out_specs=(hbm,) * 3,
        scratch_shapes=[
            pltpu.VMEM(weight_in.shape[1:], F32),
            pltpu.VMEM(outs.shape, F32),
            pltpu.VMEM((GATHER_SLOTS, 16 * ROWS, HALF), BF),
            pltpu.VMEM((GATHER_SLOTS, 16 * ROWS, HALF), BF),
            pltpu.VMEM((2, 16, ROWS, COLS), BF),
            pltpu.VMEM((2, TOK, COLS), F32),
            sems((2,)),
            sems((2, 2)),
            sems((len(GATHER_A), GATHER_SLOTS)),
            sems((len(GATHER_A), GATHER_SLOTS)),
            sems((len(GATHER_B), GATHER_SLOTS)),
            sems((len(GATHER_B), GATHER_SLOTS)),
        ],
        compiler_params=pltpu.CompilerParams(
            collective_id=4, has_side_effects=True, vmem_limit_bytes=60 * 2**20
        ),
        cost_estimate=pl.CostEstimate(flops=10**10, bytes_accessed=50 * 2**20, transcendentals=0),
        name="gather_first",
    )(weight_in, outs, normed)
    return full_in.reshape(16 * ROWS, WIDTH), full_out.reshape(LAYERS, INNER, D), zx


def project_kernel(r_ref, w_ref, out_ref):
    out_ref[...] = dot(r_ref[...], w_ref[...])


def project(normed, full_in):
    return pl.pallas_call(
        project_kernel,
        grid=(2 * STEPS + 1,),
        out_shape=jax.ShapeDtypeStruct((TOK, WIDTH), F32),
        in_specs=[
            pl.BlockSpec((TOK, D), lambda k: (0, 0), pipeline_mode=pl.Buffered(1)),
            pl.BlockSpec((D, WIDE), lambda k: (0, k)),
        ],
        out_specs=pl.BlockSpec((TOK, WIDE), lambda k: (0, k)),
        compiler_params=pltpu.CompilerParams(vmem_limit_bytes=60 * 2**20),
        cost_estimate=pl.CostEstimate(flops=10**10, bytes_accessed=36 * 2**20, transcendentals=0),
        name="project",
    )(normed, full_in)


def rows_kernel(normed_ref, mixed_ref, in_ref, out_ref):
    in_ref[0] = normed_ref[...].astype(F32).T.astype(BF)
    turned = mixed_ref[...].astype(F32).T.astype(BF)
    for i in range(turned.shape[0] // (2 * ROWS)):
        for q in range(2):
            lo = (2 * i + q) * ROWS
            out_ref[q, i * ROWS : (i + 1) * ROWS, :] = turned[lo : lo + ROWS]


def left_rows(normed, mixed):
    steps = 4
    wide = D // steps
    return pl.pallas_call(
        rows_kernel,
        grid=(steps,),
        out_shape=(
            jax.ShapeDtypeStruct((1, D, TOK), BF),
            jax.ShapeDtypeStruct((2, D, TOK), BF),
        ),
        in_specs=[
            pl.BlockSpec((TOK, wide), lambda k: (0, k)),
            pl.BlockSpec((TOK, 2 * wide), lambda k: (0, k)),
        ],
        out_specs=(
            pl.BlockSpec((1, wide, TOK), lambda k: (0, k, 0)),
            pl.BlockSpec((2, wide, TOK), lambda k: (0, k, 0)),
        ),
        compiler_params=pltpu.CompilerParams(vmem_limit_bytes=60 * 2**20),
        cost_estimate=pl.CostEstimate(flops=0, bytes_accessed=9 * 2**20, transcendentals=0),
        name="left_rows",
    )(normed, mixed)


def span_starts(seq_lengths):
    offsets = jnp.cumsum(seq_lengths) - seq_lengths
    places = jnp.arange(seq_lengths.shape[0], dtype=jnp.int32) * SPAN
    matches = (offsets[None, :] == places[:, None]) & (seq_lengths[None, :] > 0)
    return jnp.any(matches, axis=1)


def swap(value, axis, count, bit):
    return lax.ppermute(value, axis, [(i, i ^ bit) for i in range(count)])


def plain_owner_sum(left, right, reps):
    mine = lax.psum_scatter(dot(left, right, TN).astype(BF), "shard", scatter_dimension=0, tiled=True)
    total = mine.astype(F32)
    for bit in [1 << k for k in range(reps.bit_length() - 1)]:
        total = total + swap(total.astype(BF), "rep", reps, bit).astype(F32)
    return total


def side_block(mixer, norm=None):
    norm = jnp.zeros((D,), F32) if norm is None else norm
    rest = SIDE_ROWS * 128 - SIDE_MIXER * 128 - D
    flat = jnp.concatenate([jnp.pad(mixer, (0, SIDE_MIXER * 128 - mixer.shape[0])), norm, jnp.zeros((rest,), F32)])
    return flat.reshape(SIDE_ROWS, 128)


def side_parts(block, count):
    flat = block.reshape(-1)
    return flat[:count], flat[SIDE_MIXER * 128 : SIDE_MIXER * 128 + D]


def pad_cast(weight, width):
    return jnp.pad(weight.astype(BF), ((0, 0), (0, width - weight.shape[1])))


def sums_plain(normed, mixed, dz, dxs, dbc, low, full_in, side, reps):
    right = jnp.concatenate([dz, *dxs, dbc], axis=1)
    used = 2 * INNER + 2 * STATE + HEADS
    sum_in = plain_owner_sum(normed, right[:, :used], reps)
    sum_out = plain_owner_sum(mixed, low, reps)
    return sum_in, sum_out, dot(right, full_in, NT), lax.psum(side, ("rep", "shard"))


def per_device(
    tokens, cotangent, lengths,
    weight_in, moment_in, second_in,
    weight_out, moment_out, second_out,
    side_params, side_moment, side_second,
    *, reps, shards,
):
    direct = shards == 16 and reps == 2
    cont = jnp.where(span_starts(lengths[0])[1], 0.0, 1.0).astype(F32).reshape(1, 1)
    hidden = tokens.astype(F32)
    saved = []
    layer_outs = []
    for layer in range(LAYERS):
        gain = side_params[layer, :D]
        inverse_in = lax.rsqrt(jnp.mean(hidden * hidden, axis=-1, keepdims=True) + EPSILON)
        normed = (hidden * inverse_in * gain).astype(BF)
        norm_rows = jnp.concatenate(
            [jnp.broadcast_to(inverse_in, (TOK, 128)), jnp.broadcast_to(gain, (TOK, D))], axis=1
        )
        if direct and layer == 0:
            first_in, both_out, zx = gather_first(weight_in, weight_out, normed)
            zx, later_in = lax.optimization_barrier((zx, weight_in[1]))
            second_in_full = lax.all_gather(pad_cast(later_in, WIDTH), "shard", axis=0, tiled=True)
            full_in, full_out = first_in, both_out[0]
        elif direct:
            full_in, full_out = second_in_full, both_out[1]
            zx = project(normed, full_in)
        else:
            full_in = lax.all_gather(pad_cast(weight_in[layer], WIDTH), "shard", axis=0, tiled=True)
            full_out = lax.all_gather(weight_out[layer].astype(BF), "shard", axis=0, tiled=True)
            zx = jnp.dot(normed, full_in, preferred_element_type=F32)
        mixed, y, inverse = mixer_fwd(zx, cont, side_params[layer])
        left = None
        if direct:
            mixed, left = lax.optimization_barrier((mixed, left_rows(normed, mixed)))
        branch = jnp.dot(mixed, full_out, preferred_element_type=F32)
        saved.append((full_in, full_out, hidden, norm_rows, normed, zx, mixed, y, inverse, branch, left))
        hidden = hidden + branch
        layer_outs.append(hidden)
    gradient = cotangent.astype(F32)
    low = cotangent
    factor = jnp.sum(gradient * saved[-1][-2], axis=1, keepdims=True) * (1.0 / INNER)
    sums = [None] * LAYERS
    side_mixer = [None] * LAYERS
    side_norm = [None] * LAYERS
    held = []
    for layer in reversed(range(LAYERS)):
        full_in, full_out, hidden, norm_rows, normed, zx, mixed, y, inverse, branch, left = saved[layer]
        side_row = side_params[layer]
        rows = jnp.concatenate([inverse[:, :1], factor[:, :1], jnp.zeros((TOK, 126), F32)], axis=1)
        dz, dy, dgain = gate_bwd(low, full_out, zx, side_row, y, rows)
        work = NoWork()
        if direct and layer == 1:
            work = Sums("_1", 1, [(left[1], low), (left[0], dz)])
        elif direct:
            above = saved[1][-1]
            side = side_block(side_mixer[1], side_norm[1])
            work = Sums("_0", 2, [(above[0], held[0]), (above[0], held[1]), (left[1], low), (left[0], dz)], side)
        (dx, dskip, dcw, dbc, dcwbc, dhp), done = scan_bwd(zx, cont, side_row, y, dy, work)
        side_mixer[layer] = mixer_side(dgain, dskip, dcw, dcwbc, dhp)
        count = side_mixer[layer].shape[0]
        if not direct:
            sum_in, sum_out, back, side_mixer[layer] = sums_plain(
                normed, mixed, dz, [dx], dbc, low, full_in, side_mixer[layer], reps
            )
            sums[layer] = (sum_in, sum_out)
        elif layer == 1:
            sums_1 = done[0]
            held = [dx, dbc]
            back = back_to_input(dz, dx, dbc, full_in)
        else:
            sums_0, side = done
            side_mixer[1], side_norm[1] = side_parts(side[-1], count)
            work = Sums("_last", 3, [(left[0], dx), (left[0], dbc)], side_block(side_mixer[0]), 2 * STEPS + 1)
            back, (sums_last, side) = last_sums(dz, hidden, norm_rows, full_in, work)
            side_mixer[0], side_norm[0] = side_parts(side[-1], count)
            gradient = gradient + back
            continue
        branch_below = saved[layer - 1][-2] if layer else branch
        gradient, low, factor, dgain_in = norm_back(back, hidden, norm_rows, gradient, branch_below)
        side_norm[layer] = dgain_in[0]
    if direct:
        new_in, new_out = adam(
            (weight_in, moment_in, second_in), (weight_out, moment_out, second_out), (sums_1, sums_0, sums_last)
        )
    else:
        side_norm = [lax.psum(v, ("rep", "shard")) for v in side_norm]
        grad_in = jnp.stack([v[0] for v in sums])
        grad_out = jnp.stack([v[1] for v in sums])
        new_in = adamw_step(weight_in, moment_in, second_in, grad_in, RATE_MATRIX, DECAY_MATRIX)
        new_out = adamw_step(weight_out, moment_out, second_out, grad_out, RATE_MATRIX, DECAY_MATRIX)
    grad_side = jnp.stack([jnp.concatenate(pair) for pair in zip(side_norm, side_mixer)])
    return (
        jnp.stack(layer_outs),
        gradient,
        *new_in,
        *new_out,
        *adamw_step(side_params, side_moment, side_second, grad_side, RATE_SIDE, 0.0),
    )


def solution(mesh):
    rows = P(("rep", "shard"), None)
    owned = P(None, "shard", None)
    body = partial(per_device, reps=mesh.shape["rep"], shards=mesh.shape["shard"])
    return jax.shard_map(
        body,
        mesh=mesh,
        in_specs=(rows, rows, rows) + (owned,) * 6 + (P(),) * 3,
        out_specs=(P(None, ("rep", "shard"), None), rows) + (owned,) * 6 + (P(),) * 3,
        check_vma=False,
    )
```

```python
from functools import partial

import jax
import jax.numpy as jnp
from jax import lax
from jax.experimental import pallas as pl
from jax.experimental.pallas import tpu as pltpu
from jax.sharding import PartitionSpec as P

LAYERS = 2
STEP = 10
BETA_ONE = 0.9
BETA_TWO = 0.95
ADAM_EPSILON = 1e-08
RATE_MATRIX = 0.05
RATE_SIDE = 0.5
DECAY_MATRIX = 0.1
D = 1536
INNER = 3072
HEAD_DIM = 64
STATE = 128
CONV = 4
SPAN = 256
HEADS = 48
XBC = 3328
TOK = 512
GROUP = 8
BC_WIDE = 512
N_SCAN_SCRATCH = 19
PUMPS = GROUP // 2 + 1
WIDE = GROUP * HEAD_DIM
STEPS = HEADS // GROUP
HALO = 8
LOG2_E = 1.4426950408889634
EPSILON = 1e-05
HIGHEST = lax.Precision.HIGHEST
BF = jnp.bfloat16
F32 = jnp.float32


def dot(a, b, dims=((1,), (0,)), precision=None):
    return lax.dot_general(a, b, (dims, ((), ())), precision=precision, preferred_element_type=F32)


NT = ((1,), (1,))
TN = ((0,), (0,))


def sigmoid(v):
    return 1.0 / (1.0 + jnp.exp(-v))


def softplus(v):
    e = jnp.exp(-jnp.abs(v))
    u = 1.0 + e
    tail = jnp.where(u == 1.0, e, jnp.log(u) * (e / jnp.where(u == 1.0, 1.0, u - 1.0)))
    return jnp.maximum(v, 0.0) + tail


def load_halo(buf, xin, cont, width):
    buf[0:HALO, :width] = jnp.zeros((HALO, width), F32)
    buf[HALO : HALO + SPAN, :width] = xin[0:SPAN]
    buf[HALO + SPAN : 2 * HALO + SPAN, :width] = xin[SPAN - HALO : SPAN] * cont
    buf[2 * HALO + SPAN : 2 * (HALO + SPAN), :width] = xin[SPAN : 2 * SPAN]


def shifted(buf, k, span, width, lo=0, rows=SPAN):
    base = span * (HALO + SPAN) + HALO - k + lo
    return buf[base : base + rows, :width]


def conv_of(buf, cw, span, width, lo=0, rows=SPAN):
    total = cw[4:5, :] + cw[3:4, :] * shifted(buf, 0, span, width, lo, rows)
    for k in range(1, CONV):
        total = total + cw[3 - k : 4 - k, :] * shifted(buf, k, span, width, lo, rows)
    return total


def lower_tri():
    return (
        lax.broadcasted_iota(jnp.int32, (SPAN, SPAN), 0)
        >= lax.broadcasted_iota(jnp.int32, (SPAN, SPAN), 1)
    )


def setup(cont, bc_ref, dt_ref, cwbc_ref, hp_ref, buf, bct, scores, dts, cum, cumt):
    load_halo(buf, bc_ref[...], cont, 2 * STATE)
    for span in range(2):
        lo = span * SPAN
        s = conv_of(buf, cwbc_ref[...], span, 2 * STATE)
        bct[lo : lo + SPAN, :] = (s * sigmoid(s)).astype(BF)
        sc = dot(bct[lo : lo + SPAN, STATE:], bct[lo : lo + SPAN, :STATE], NT)
        scores[lo : lo + SPAN, :] = jnp.where(lower_tri(), sc, 0.0)
    lane = lax.broadcasted_iota(jnp.int32, (TOK, 128), 1)
    raw = jnp.where(lane < HEADS, dt_ref[...], 0.0) + hp_ref[0:1, :]
    step = jnp.where(lane < HEADS, softplus(raw), 0.0)
    dts[...] = step
    a = (-LOG2_E * jnp.exp(hp_ref[1:2, :])) * step
    tri = jnp.where(lower_tri(), 1.0, 0.0)
    for span in range(2):
        lo = span * SPAN
        cum[lo : lo + SPAN, :] = dot(tri, a[lo : lo + SPAN, :], precision=HIGHEST)
    cumt[...] = cum[...].T


def split_dot(value, ones):
    high = value.astype(BF)
    low = (value - high.astype(F32)).astype(BF)
    return dot(high, ones) + dot(low, ones)


def spread_of():
    lane = lax.broadcasted_iota(jnp.int32, (128, WIDE), 0)
    column = lax.broadcasted_iota(jnp.int32, (128, WIDE), 1)
    return jnp.where(lane == column // HEAD_DIM, 1.0, 0.0).astype(BF)


def fwd_kernel(
    cont_ref, z_ref, x_ref, bc_ref, dt_ref, cwx_ref, cwbc_ref, hp_ref, cp_ref, gain_ref,
    m_ref, y_ref, inv_ref,
    buf, bct, scores, dts, cum, cumt, mix, xt, g_s, ssq, grp, state,
):
    g = pl.program_id(0)
    cont = cont_ref[0, 0]

    @pl.when(g == 0)
    def _():
        setup(cont, bc_ref, dt_ref, cwbc_ref, hp_ref, buf, bct, scores, dts, cum, cumt)
        ssq[...] = jnp.zeros_like(ssq)

    shift = lax.rem(128 - GROUP * g, 128)
    grp[0] = pltpu.roll(dts[...], shift, 1)
    grp[1] = pltpu.roll(cum[...], shift, 1)
    rows8 = cumt[pl.ds(pl.multiple_of(g * GROUP, GROUP), GROUP), :]
    load_halo(buf, x_ref[...], cont, WIDE)
    spread = spread_of()
    for span in range(2):
        lo = span * SPAN
        s = conv_of(buf, cwx_ref[...], span, WIDE)
        x = s * sigmoid(s)
        y_ref[lo : lo + SPAN, :] = x * cp_ref[1:2, :]
        xt[lo : lo + SPAN, :] = x * split_dot(grp[0, lo : lo + SPAN, :], spread)
    last = grp[1, SPAN - 1 : SPAN, :]
    xw = xt[0:SPAN, :] * split_dot(jnp.exp2(last - grp[1, 0:SPAN, :]), spread)
    st = dot(bct[0:SPAN, :STATE], xw.astype(BF), TN) * cont
    y_ref[SPAN:, :] += split_dot(jnp.exp2(grp[1, SPAN:, :]), spread) * dot(bct[SPAN:, STATE:], st.astype(BF))
    first = lax.broadcasted_iota(jnp.int32, (SPAN, 128), 1) < HEAD_DIM
    for span in range(2):
        lo = span * SPAN
        for j in range(0, GROUP, 2):
            slot = j // 2 % 2
            for h in range(2):
                fill_mix(mix, slot, h, scores, grp, rows8, span, j + h)
            cs = slice(j * HEAD_DIM, j * HEAD_DIM + 128)
            xp = xt[lo : lo + SPAN, cs]
            both = jnp.concatenate([jnp.where(first, xp, 0.0), jnp.where(first, 0.0, xp)], axis=0)
            y_ref[lo : lo + SPAN, cs] += dot(mix[slot], both.astype(BF))
    z = z_ref[...]
    gated = y_ref[...] * (z * sigmoid(z))
    g_s[g] = gated
    ssq[...] += jnp.broadcast_to(jnp.sum(gated * gated, axis=1, keepdims=True), ssq.shape)

    @pl.when(g == STEPS - 1)
    def _():
        inv = lax.rsqrt(ssq[...] * (1.0 / INNER) + EPSILON)
        inv_ref[...] = inv
        col = inv[:, 0:1]
        for k in range(STEPS):
            m_ref[:, k * WIDE : (k + 1) * WIDE] = (
                g_s[k] * col * gain_ref[0:1, k * WIDE : (k + 1) * WIDE]
            ).astype(BF)


CHUNK = 64


def fill_mix(mix, slot, h, scores, grp, rows8, span, j):
    lo = span * SPAN
    base = h * SPAN
    for r in range(0, SPAN, CHUNK):
        wide = 128 if r + CHUNK <= 128 else 256
        gap = grp[1, lo + r : lo + r + CHUNK, j : j + 1] - rows8[j : j + 1, lo : lo + wide]
        val = scores[lo + r : lo + r + CHUNK, :wide] * jnp.exp2(jnp.minimum(gap, 0.0))
        mix[slot, r : r + CHUNK, base : base + wide] = val.astype(BF)
        if wide < 256:
            mix[slot, r : r + CHUNK, base + wide : base + 256] = jnp.zeros((CHUNK, 256 - wide), BF)


def head_rows(side_row):
    cur = D + INNER + CONV * XBC + XBC
    rows = side_row[cur : cur + 3 * HEADS].reshape(3, HEADS)
    return jnp.pad(rows, ((0, 5), (0, 128 - HEADS)))


def conv_rows(side_row):
    cur = D + INNER
    rows = side_row[cur : cur + (CONV + 1) * XBC].reshape(CONV + 1, XBC)
    return jnp.pad(rows, ((0, 3), (0, 0)))


def column_rows(side_row):
    gain = side_row[D : D + INNER]
    skip = jnp.repeat(side_row[-HEADS:], HEAD_DIM)
    return jnp.pad(jnp.stack([gain, skip]), ((0, 6), (0, 0)))


def mixer_fwd(zx, cont, side_row):
    hp, cw, cp = head_rows(side_row), conv_rows(side_row), column_rows(side_row)
    full = lambda shape: pl.BlockSpec(shape, lambda g: (0,) * len(shape))
    return pl.pallas_call(
        fwd_kernel,
        grid=(STEPS,),
        out_shape=(
            jax.ShapeDtypeStruct((TOK, INNER), BF),
            jax.ShapeDtypeStruct((TOK, INNER), F32),
            jax.ShapeDtypeStruct((TOK, 128), F32),
        ),
        in_specs=[
            pl.BlockSpec(memory_space=pltpu.SMEM),
            pl.BlockSpec((TOK, WIDE), lambda g: (0, g)),
            pl.BlockSpec((TOK, WIDE), lambda g: (0, STEPS + g)),
            pl.BlockSpec((TOK, 2 * STATE), lambda g: (0, 2 * INNER // (2 * STATE))),
            pl.BlockSpec((TOK, 128), lambda g: (0, (INNER + XBC) // 128)),
            pl.BlockSpec((8, WIDE), lambda g: (0, g)),
            pl.BlockSpec((8, 2 * STATE), lambda g: (0, INNER // (2 * STATE))),
            full((8, 128)),
            pl.BlockSpec((8, WIDE), lambda g: (0, g)),
            full((8, INNER)),
        ],
        out_specs=(
            full((TOK, INNER)),
            pl.BlockSpec((TOK, WIDE), lambda g: (0, g)),
            full((TOK, 128)),
        ),
        scratch_shapes=[
            pltpu.VMEM((2 * (HALO + SPAN), WIDE), F32),
            pltpu.VMEM((TOK, 2 * STATE), BF),
            pltpu.VMEM((TOK, SPAN), F32),
            pltpu.VMEM((TOK, 128), F32),
            pltpu.VMEM((TOK, 128), F32),
            pltpu.VMEM((128, TOK), F32),
            pltpu.VMEM((2, SPAN, 2 * SPAN), BF),
            pltpu.VMEM((TOK, WIDE), F32),
            pltpu.VMEM((STEPS, TOK, WIDE), F32),
            pltpu.VMEM((TOK, 128), F32),
            pltpu.VMEM((2, TOK, 128), F32),
            pltpu.VMEM((STATE, WIDE), F32),
        ],
        compiler_params=pltpu.CompilerParams(vmem_limit_bytes=60 * 2**20),
        cost_estimate=pl.CostEstimate(flops=6 * 10**9, bytes_accessed=25 * 2**20, transcendentals=10**7),
        name="mixer_fwd",
    )(cont, zx, zx, zx, zx, cw, cw, hp, cp, cp)


def gate_kernel(low_ref, w_ref, z_ref, cp_ref, y_ref, row_ref, dz_ref, dy_ref, dgain_ref):
    dm = dot(low_ref[...], w_ref[...], NT)
    z = z_ref[...]
    sz = sigmoid(z)
    gate = z * sz
    y = y_ref[...]
    inv = row_ref[:, 0:1]
    gn = y * gate * inv
    dgain_ref[...] = jnp.zeros_like(dgain_ref)
    dgain_ref[0:1, :] = jnp.sum(dm * gn, axis=0, keepdims=True)
    dg = inv * (dm * cp_ref[0:1, :] - gn * row_ref[:, 1:2])
    dz_ref[...] = (dg * y * (sz * (1.0 + z * (1.0 - sz)))).astype(BF)
    dy_ref[...] = dg * gate


def gate_bwd(low, full_out, zx, side_row, y, rows):
    cp = column_rows(side_row)
    by_g = lambda rows_: pl.BlockSpec((rows_, WIDE), lambda g: (0, g))
    full = lambda shape: pl.BlockSpec(shape, lambda g: (0,) * len(shape))
    return pl.pallas_call(
        gate_kernel,
        grid=(STEPS,),
        out_shape=(
            jax.ShapeDtypeStruct((TOK, INNER), BF),
            jax.ShapeDtypeStruct((TOK, INNER), F32),
            jax.ShapeDtypeStruct((8, INNER), F32),
        ),
        in_specs=[
            full((TOK, D)),
            pl.BlockSpec((WIDE, D), lambda g: (g, 0)),
            by_g(TOK),
            by_g(8),
            by_g(TOK),
            full((TOK, 128)),
        ],
        out_specs=(by_g(TOK), by_g(TOK), by_g(8)),
        compiler_params=pltpu.CompilerParams(vmem_limit_bytes=60 * 2**20),
        cost_estimate=pl.CostEstimate(flops=5 * 10**9, bytes_accessed=40 * 2**20, transcendentals=2 * 10**6),
        name="gate_bwd",
    )(low, full_out, zx, cp, y, rows)


def scan_kernel(
    work, cont_ref, x_ref, bc_ref, dt_ref, cwx_ref, cwbc_ref, hp_ref, cp_ref, y_ref, dy, *rest,
):
    g = pl.program_id(0)
    scratch = rest[-N_SCAN_SCRATCH:]
    buf, bct, scores, dts, cum, cumt, mix, decay, xt, xf, sig, dsum, dtx, dxt, dscore, dbcs, dcum, ddt, grp = scratch
    engine = work.engine(rest[:-N_SCAN_SCRATCH], (xt, xf, sig))
    dx_ref, dskip_ref, dcw_ref, dbc_ref, dcwbc_ref, dhp_ref = engine.outputs(g)
    cont = cont_ref[0, 0]

    @pl.when(g == 0)
    def _():
        engine.open()

    @pl.when(g == 0)
    def _():
        setup(cont, bc_ref, dt_ref, cwbc_ref, hp_ref, buf, bct, scores, dts, cum, cumt)
        for ref in (dscore, dbcs, dcum, ddt):
            ref[...] = jnp.zeros_like(ref)

    shift = lax.rem(128 - GROUP * g, 128)
    grp[0] = pltpu.roll(dts[...], shift, 1)
    grp[1] = pltpu.roll(cum[...], shift, 1)
    load_halo(buf, x_ref[...], cont, WIDE)
    spread = spread_of()
    skip = cp_ref[1:2, :]
    dskip_ref[...] = jnp.zeros_like(dskip_ref)
    pick = jnp.where(
        lax.broadcasted_iota(jnp.int32, (WIDE, 128), 0) // HEAD_DIM + GROUP * g
        == lax.broadcasted_iota(jnp.int32, (WIDE, 128), 1),
        1.0,
        0.0,
    ).astype(BF)
    for span in range(2):
        lo = span * SPAN
        hi = lo + SPAN
        s = conv_of(buf, cwx_ref[...], span, WIDE)
        sg = sigmoid(s)
        x = s * sg
        xf[lo:hi, :] = x
        sig[lo:hi, :] = sg * (1.0 + s * (1.0 - sg))
        dtx[lo:hi, :] = split_dot(grp[0, lo:hi, :], spread)
        xt[lo:hi, :] = x * dtx[lo:hi, :]
        dyv = dy[lo:hi, :]
        dskip_ref[0:1, :] += jnp.sum(dyv * x, axis=0, keepdims=True)
        yin = y_ref[lo:hi, :] - skip * x
        dsum[lo:hi, :] = dyv.astype(BF).astype(F32) * yin

    last = grp[1, SPAN - 1 : SPAN, :]
    wl = split_dot(jnp.exp2(last - grp[1, 0:SPAN, :]), spread)
    xw = (xt[0:SPAN, :] * wl).astype(BF)
    prior = (dot(bct[0:SPAN, :STATE], xw, TN) * cont).astype(BF)
    dye = (dy[SPAN:, :] * split_dot(jnp.exp2(grp[1, SPAN:, :]), spread)).astype(BF)
    dprior = (dot(bct[SPAN:, STATE:], dye, TN) * cont).astype(BF)
    dbcs[SPAN:, STATE:] += dot(dye, prior, NT)
    dbcs[0:SPAN, :STATE] += dot(xw, dprior, NT)
    dxt[0:SPAN, :] = dot(bct[0:SPAN, :STATE], dprior) * wl
    dxt[SPAN:, :] = jnp.zeros((SPAN, WIDE), F32)
    through = dxt[0:SPAN, :] * xt[0:SPAN, :]
    dcum[SPAN - 1 : SPAN, :] += split_dot(jnp.sum(through, axis=0, keepdims=True), pick)

    first = lax.broadcasted_iota(jnp.int32, (SPAN, 128), 1) < HEAD_DIM

    def pair(j):
        cs = pl.ds(pl.multiple_of(j * 128, 128), 128)
        group_rows = cumt[pl.ds(pl.multiple_of(g * GROUP, GROUP), GROUP), :]
        row = pltpu.roll(group_rows, lax.rem(GROUP - 2 * j, GROUP), 0)
        cols = pltpu.roll(grp[1], lax.rem(128 - 2 * j, 128), 1)
        for span in range(2):
            lo = span * SPAN
            hi = lo + SPAN
            dyp = dy[lo:hi, cs]
            dyt = dyp.T.astype(BF)
            xtb = xt[lo:hi, cs].astype(BF)
            parts = []
            for h in range(2):
                k = 2 * span + h
                for r in range(0, SPAN, CHUNK):
                    wide = 128 if r + CHUNK <= 128 else 256
                    gap = cols[lo + r : lo + r + CHUNK, h : h + 1] - row[h : h + 1, lo : lo + wide]
                    e = jnp.exp2(jnp.minimum(gap, 0.0))
                    decay[k, r : r + CHUNK, :wide] = e.astype(BF)
                    mix[k, r : r + CHUNK, :wide] = (scores[lo + r : lo + r + CHUNK, :wide] * e).astype(BF)
                    if wide < 256:
                        mix[k, r : r + CHUNK, wide:] = jnp.zeros((CHUNK, 256 - wide), BF)
                dmix = dot(jnp.where(first == (h == 0), dyp, 0.0).astype(BF), xtb, NT)
                top, low = dmix[:128, :128], dmix[128:, :]
                dscore[lo : lo + 128, :128] += top * decay[k, :128, :128].astype(F32)
                dscore[lo + 128 : hi, :] += low * decay[k, 128:, :].astype(F32)
                parts.append(dot(dyt[h * HEAD_DIM : (h + 1) * HEAD_DIM, :], mix[k]))
            dxt[lo:hi, cs] += jnp.concatenate(parts, axis=0).T

    def place(i, _):
        engine.pump(g * PUMPS + i, STEPS * PUMPS)

        @pl.when(i < GROUP // 2)
        def _():
            pair(i)

        return 0

    lax.fori_loop(0, PUMPS, place, 0)

    dcw_ref[...] = jnp.zeros_like(dcw_ref)
    for span in range(2):
        lo = span * SPAN
        hi = lo + SPAN
        x = xf[lo:hi, :]
        xtv = xt[lo:hi, :]
        dv = dxt[lo:hi, :]
        dcum[lo:hi, :] += split_dot(dsum[lo:hi, :] - dv * xtv.astype(BF).astype(F32), pick)
        ddt[lo:hi, :] += split_dot(dv * x, pick)
        dxt[lo:hi, :] = (dv * dtx[lo:hi, :] + dy[lo:hi, :] * skip) * sig[lo:hi, :]
        conv_weights(dcw_ref, buf, dxt[lo:hi, :], span, WIDE)
    back_halo(buf, dxt[...], cont, WIDE)
    for span in range(2):
        lo = span * SPAN
        dx_ref[lo : lo + SPAN, :] = conv_back(buf, cwx_ref[...], span, WIDE).astype(BF)

    engine.group_done(g)

    @pl.when(g == STEPS - 1)
    def _():
        load_halo(buf, bc_ref[...], cont, 2 * STATE)
        dcwbc_ref[...] = jnp.zeros_like(dcwbc_ref)
        for span in range(2):
            lo = span * SPAN
            hi = lo + SPAN
            ds = jnp.where(lower_tri(), dscore[lo:hi, :], 0.0).astype(BF)
            dbcs[lo:hi, :STATE] += dot(ds, bct[lo:hi, STATE:], TN)
            dbcs[lo:hi, STATE:] += dot(ds, bct[lo:hi, :STATE])
            s = conv_of(buf, cwbc_ref[...], span, 2 * STATE)
            sg = sigmoid(s)
            dcv = dbcs[lo:hi, :] * (sg * (1.0 + s * (1.0 - sg)))
            dbcs[lo:hi, :] = dcv
            conv_weights(dcwbc_ref, buf, dcv, span, 2 * STATE)
        back_halo(buf, dbcs[...], cont, 2 * STATE)
        for span in range(2):
            lo = span * SPAN
            dbc_ref[lo : lo + SPAN, : 2 * STATE] = conv_back(buf, cwbc_ref[...], span, 2 * STATE).astype(BF)
        lane = lax.broadcasted_iota(jnp.int32, (TOK, 128), 1)
        raw = jnp.where(lane < HEADS, dt_ref[...], 0.0) + hp_ref[0:1, :]
        decay_rate = -jnp.exp(hp_ref[1:2, :])
        tri = jnp.where(lower_tri(), 1.0, 0.0)
        da = jnp.concatenate(
            [dot(tri, dcum[lo : lo + SPAN, :], TN, HIGHEST) for lo in (0, SPAN)], axis=0
        )
        draw = jnp.where(lane < HEADS, (ddt[...] + decay_rate * da) * sigmoid(raw), 0.0)
        dbc_ref[:, 2 * STATE : 2 * STATE + 128] = draw.astype(BF)
        dbc_ref[:, 2 * STATE + 128 :] = jnp.zeros((TOK, BC_WIDE - 2 * STATE - 128), BF)
        dhp_ref[...] = jnp.zeros_like(dhp_ref)
        dhp_ref[0:1, :] = jnp.sum(draw, axis=0, keepdims=True)
        dhp_ref[1:2, :] = jnp.sum(da * decay_rate * dts[...], axis=0, keepdims=True)
        engine.close()


def conv_weights(out, buf, dcv, span, width):
    for k in range(CONV):
        out[3 - k : 4 - k, :] += jnp.sum(dcv * shifted(buf, k, span, width), axis=0, keepdims=True)
    out[4:5, :] += jnp.sum(dcv, axis=0, keepdims=True)


def back_halo(buf, dcv, cont, width):
    buf[0:SPAN, :width] = dcv[0:SPAN]
    buf[SPAN : SPAN + HALO, :width] = dcv[SPAN : SPAN + HALO] * cont
    buf[SPAN + HALO : 2 * SPAN + HALO, :width] = dcv[SPAN:]
    buf[2 * SPAN + HALO : 2 * (SPAN + HALO), :width] = jnp.zeros((HALO, width), F32)


def conv_back(buf, cw, span, width):
    base = span * (SPAN + HALO)
    total = cw[3:4, :] * buf[base : base + SPAN, :width]
    for k in range(1, CONV):
        total = total + cw[3 - k : 4 - k, :] * buf[base + k : base + k + SPAN, :width]
    return total


def scan_bwd(zx, cont, side_row, y, dy, work):
    hp, cw, cp = head_rows(side_row), conv_rows(side_row), column_rows(side_row)
    full = lambda shape: pl.BlockSpec(shape, lambda g: (0,) * len(shape))
    by_g = lambda rows_: pl.BlockSpec((rows_, WIDE), lambda g: (0, g))
    vmem = lambda *shape: pltpu.VMEM(shape, F32)
    return pl.pallas_call(
        partial(scan_kernel, work),
        grid=(STEPS,),
        out_shape=tuple(work.out_shapes),
        in_specs=[
            pl.BlockSpec(memory_space=pltpu.SMEM),
            pl.BlockSpec((TOK, WIDE), lambda g: (0, STEPS + g)),
            pl.BlockSpec((TOK, 2 * STATE), lambda g: (0, 2 * INNER // (2 * STATE))),
            pl.BlockSpec((TOK, 128), lambda g: (0, (INNER + XBC) // 128)),
            by_g(8),
            pl.BlockSpec((8, 2 * STATE), lambda g: (0, INNER // (2 * STATE))),
            full((8, 128)),
            by_g(8),
            by_g(TOK),
            by_g(TOK),
            *work.in_specs,
        ],
        out_specs=tuple(work.out_specs),
        scratch_shapes=[
            *work.scratch,
            vmem(2 * (HALO + SPAN), WIDE),
            pltpu.VMEM((TOK, 2 * STATE), BF),
            vmem(TOK, SPAN),
            vmem(TOK, 128),
            vmem(TOK, 128),
            vmem(128, TOK),
            pltpu.VMEM((4, SPAN, SPAN), BF),
            pltpu.VMEM((4, SPAN, SPAN), BF),
            vmem(TOK, WIDE),
            vmem(TOK, WIDE),
            vmem(TOK, WIDE),
            vmem(TOK, WIDE),
            vmem(TOK, WIDE),
            vmem(TOK, WIDE),
            vmem(TOK, SPAN),
            vmem(TOK, 2 * STATE),
            vmem(TOK, 128),
            vmem(TOK, 128),
            vmem(2, TOK, 128),
        ],
        compiler_params=work.params(),
        cost_estimate=pl.CostEstimate(flops=4 * 10**10, bytes_accessed=60 * 2**20, transcendentals=2 * 10**7),
        name=f"scan_bwd{work.name}",
    )(cont, zx, zx, zx, cw, cw, hp, cp, y, dy, *work.inputs)


def mixer_side(dgain, dskip, dcw, dcwbc, dhp):
    return jnp.concatenate(
        [
            dgain[0],
            jnp.concatenate([dcw[: CONV + 1], dcwbc[: CONV + 1]], axis=1).reshape(-1),
            dhp[0, :HEADS],
            dhp[1, :HEADS],
            jnp.sum(dskip[0].reshape(HEADS, HEAD_DIM), axis=1),
        ]
    )


ROWS = 96
COLS = 256
HALF = COLS // 2
LAG = 2
SLOTS = 2 * LAG
OWN_SLOTS = LAG + 1
MESH = pl.DeviceIdType.MESH
STAGES_A = ("core", "y", "z", "far", "rep")
STAGES_B = ("core", "rep", "y", "z", "far", "rep")
STAGES_ODD = ("core", "rep", "z", "far", "y", "rep")
SIZES_A = (8 * ROWS, 4 * ROWS, 2 * ROWS, ROWS, ROWS)
SIZES_B = (8 * ROWS, 4 * ROWS, 2 * ROWS, ROWS, ROWS // 2, ROWS // 2)
IN_BLOCKS = 26
WIDTH = IN_BLOCKS * COLS
OUT_BLOCKS = 6
SIDE_WIDE = 3584
SIDE_STEPS = INNER + 2 * STATE
SCAN_TICKS = 28
SIDE_LINKS = ("core", "rep", "y", "z", "far")


def choose(j, even, odd):
    return even + (odd - even) * (j % 2)


class Place:
    def __init__(self):
        self.me = lax.axis_index("shard")
        self.rep = lax.axis_index("rep")
        me = self.me
        self.bits = (me // 8 % 2, me // 4 % 2, me // 2 % 2, me % 2)
        flips = {"far": 0, "z": 1, "y": 2, "core": 3}
        self.targets = {
            name: (self.rep, self.owner(*(int(k == bit) for k in range(4)))) for name, bit in flips.items()
        }
        self.targets["rep"] = (1 - self.rep, me)

    def target(self, even, odd, j):
        if even == odd:
            return self.targets[even]
        return (self.rep, choose(j, self.targets[even][1], self.targets[odd][1]))

    def owner(self, far, z, y, core):
        bits = [1 - b if d else b for b, d in zip(self.bits, (far, z, y, core))]
        return bits[0] * 8 + bits[1] * 4 + bits[2] * 2 + bits[3]

    def greet(self):
        barrier = pltpu.get_barrier_semaphore()
        for target in self.targets.values():
            pl.semaphore_signal(barrier, inc=1, device_id=target, device_id_type=MESH)
        pl.semaphore_wait(barrier, len(self.targets))


class NoEngine:
    def __init__(self, refs):
        self.refs = refs

    def outputs(self, g):
        return self.refs

    def open(self):
        pass

    def pump(self, now, pumps):
        pass

    def group_done(self, g):
        pass

    def close(self):
        pass


class NoWork:
    name, inputs, in_specs, scratch = "", [], [], []

    def __init__(self):
        shapes = (
            ((TOK, INNER), BF), ((8, INNER), F32), ((8, INNER), F32),
            ((TOK, BC_WIDE), BF), ((8, 2 * STATE), F32), ((8, 128), F32),
        )
        self.out_shapes = [jax.ShapeDtypeStruct(*s) for s in shapes]
        by_g = [pl.BlockSpec((a.shape[0], WIDE), lambda g: (0, g)) for a in self.out_shapes[:3]]
        self.out_specs = by_g + [pl.BlockSpec(a.shape, lambda g: (0, 0)) for a in self.out_shapes[3:]]

    def engine(self, refs, free):
        return NoEngine(refs)

    def params(self):
        return pltpu.CompilerParams(vmem_limit_bytes=60 * 2**20)


class Sums:
    name = "_sums"
    blocks = 2 * OUT_BLOCKS + IN_BLOCKS
    ticks = blocks + LAG * len(STAGES_B)

    def __init__(self, left, low, dz, dgain, hidden, inverse, gain, full_in):
        self.inputs = [left, low, dz, dgain, inverse, gain, hidden, full_in]
        once = lambda a: pl.BlockSpec(a.shape, lambda *_: (0,) * len(a.shape), pipeline_mode=pl.Buffered(1))
        self.in_specs = [once(a) for a in self.inputs[:-2]] + [pl.BlockSpec(memory_space=pl.ANY)] * 2
        self.out_shapes = [
            jax.ShapeDtypeStruct((TOK, D), F32),
            jax.ShapeDtypeStruct((ROWS, self.blocks * COLS), F32),
            jax.ShapeDtypeStruct((len(SIDE_LINKS) + 1, 8, SIDE_WIDE), F32),
        ]
        self.out_specs = [once(a) for a in self.out_shapes]
        self.out_specs[1] = pl.BlockSpec(memory_space=pl.ANY)
        self.scratch = [
            pltpu.VMEM((TOK, INNER), BF),
            pltpu.VMEM((8, WIDE), F32),
            pltpu.VMEM((8, WIDE), F32),
            pltpu.VMEM((TOK, BC_WIDE), BF),
            pltpu.VMEM((8, 2 * STATE), F32),
            pltpu.VMEM((8, 128), F32),
            pltpu.VMEM((2, D, COLS), BF),
            pltpu.SemaphoreType.DMA((5,)),
            pltpu.VMEM((len(SIDE_LINKS), 8, SIDE_WIDE), F32),
            pltpu.SemaphoreType.DMA((2, len(SIDE_LINKS))),
            pltpu.VMEM((16 * ROWS, COLS), F32),
            pltpu.VMEM((TOK, COLS), BF),
            pltpu.VMEM((SLOTS, ROWS, COLS), F32),
            pltpu.SemaphoreType.DMA((SLOTS,)),
        ]
        for links, sizes in ((STAGES_A, SIZES_A), (STAGES_B, SIZES_B)):
            self.scratch += [pltpu.VMEM((OWN_SLOTS, r, HALF), BF) for r in sizes]
            self.scratch += [pltpu.VMEM((SLOTS, r, HALF), BF) for r in sizes]
            self.scratch += [pltpu.VMEM((OWN_SLOTS, r, HALF), F32) for r in sizes[:-1]]
            self.scratch += [pltpu.SemaphoreType.DMA((len(links), SLOTS))] * 2

    def params(self):
        return pltpu.CompilerParams(collective_id=1, has_side_effects=True, vmem_limit_bytes=58 * 2**20)

    def engine(self, refs, free):
        return Engine(self, refs, free)


class Engine:
    def __init__(self, work, refs, free):
        self.work, self.free = work, free
        n = len(work.inputs)
        self.left, low, self.dz, self.dgain, self.inverse, self.gain, self.h, self.w = refs[:n]
        self.dr, self.out_ref, self.side_out = refs[n : n + 3]
        rest = refs[n + 3 :]
        self.dx, self.dskip, self.dcw, self.dbc, self.dcwbc, self.dhp = rest[:6]
        self.wbuf, self.wsem, self.side_in, self.side_sems, self.tmp, self.right, self.stage, self.out_sem = rest[6:14]
        rest = rest[14:]
        self.kinds = {}
        for kind, links in (("a", STAGES_A), ("b", STAGES_B)):
            n = len(links)
            src, rest = rest[:n], rest[n:]
            dst, rest = rest[:n], rest[n:]
            acc, rest = rest[: n - 1], rest[n - 1 :]
            self.kinds[kind] = (links, src, dst, acc, rest[0], rest[1])
            rest = rest[2:]
        self.operands = [(low, 2, OUT_BLOCKS), (self.dz, 1, 12), (self.dx, 1, 12), (self.dbc, 1, 2)]
        self.place = Place()

    def outputs(self, g):
        dx = self.dx.at[:, pl.ds(pl.multiple_of(g * WIDE, WIDE), WIDE)]
        return dx, self.dskip, self.dcw, self.dbc, self.dcwbc, self.dhp

    def group_done(self, g):
        cols = pl.ds(pl.multiple_of(g * WIDE, WIDE), WIDE)
        self.side_out[0, 0 : CONV + 1, cols] = self.dcw[0 : CONV + 1, :]
        self.side_out[0, 5:6, cols] = self.dskip[0:1, :]

    def weights(self, k):
        cols = pl.ds(pl.multiple_of(k * COLS, COLS), COLS)
        return pltpu.make_async_copy(self.w.at[:, cols], self.wbuf.at[k % 2], self.wsem.at[k % 2])

    def hidden(self, c):
        return pltpu.make_async_copy(self.h.at[:, c * WIDE : (c + 1) * WIDE], self.free[c], self.wsem.at[2 + c])

    def close(self):
        count = IN_BLOCKS
        side_tick = SCAN_TICKS + (count + 3) // 4
        self.weights(0).start()
        self.weights(1).start()
        for c in range(3):
            self.hidden(c).start()
        self.side_out[0, 6:7, 0:INNER] = self.dgain[0:1, :]
        self.side_out[0, 0 : CONV + 1, INNER:SIDE_STEPS] = self.dcwbc[0 : CONV + 1, :]
        self.side_out[0, 0:2, SIDE_STEPS : SIDE_STEPS + 128] = self.dhp[0:2, :]
        self.dr[...] = jnp.zeros_like(self.dr)
        bounds = ((self.dz, 0, 12), (self.dx, 12, 24), (self.dbc, 24, count))

        def product(k, _):
            self.weights(k).wait()
            for ref, lo, hi in bounds:

                @pl.when((k >= lo) & (k < hi))
                def _():
                    cols = pl.ds(pl.multiple_of((k - lo) * COLS, COLS), COLS)
                    self.right[...] = ref[:, cols]

            self.dr[...] += dot(self.right[...], self.wbuf[k % 2], NT)

            @pl.when(k + 2 < count)
            def _():
                self.weights(k + 2).start()

            return 0

        def step(t, _):
            self.tick(t)
            done = 4 * (t - SCAN_TICKS)
            lax.fori_loop(jnp.minimum(done, count), jnp.minimum(done + 4, count), product, 0)

            @pl.when(t == side_tick)
            def _():
                for c in range(3):
                    self.hidden(c).wait()
                    cols = slice(c * WIDE, (c + 1) * WIDE)
                    scaled = self.free[c][...] * self.inverse[:, 0:1]
                    self.side_out[0, 7:8, cols] = jnp.sum(self.dr[:, cols] * scaled, axis=0, keepdims=True)
                self.side_copy(0).start()

            for k in range(len(SIDE_LINKS)):

                @pl.when(t == side_tick + 2 * (k + 1))
                def _():
                    self.side_copy(k).wait()
                    self.side_out[k + 1] = self.side_out[k] + self.side_in[k]
                    if k + 1 < len(SIDE_LINKS):
                        self.side_copy(k + 1).start()

            return 0

        lax.fori_loop(SCAN_TICKS, self.work.ticks, step, 0)
        for j in range(self.work.blocks - SLOTS, self.work.blocks):
            self.leave(j).wait()
        inverse = self.inverse[:, 0:1]
        mean = 0.0
        for c in range(3):
            cols = slice(c * WIDE, (c + 1) * WIDE)
            scaled = self.free[c][...] * inverse
            dn = self.dr[:, cols] * self.gain[0:1, cols]
            self.free[c][...] = scaled
            self.dr[:, cols] = dn
            mean = mean + jnp.sum(dn * scaled, axis=1, keepdims=True)
        mean = mean * (1.0 / D)
        for c in range(3):
            cols = slice(c * WIDE, (c + 1) * WIDE)
            self.dr[:, cols] = inverse * (self.dr[:, cols] - self.free[c][...] * mean)

    def copy(self, kind, s, j):
        links, src, dst, _, ss, rs = self.kinds[kind]
        slot = j % SLOTS
        return pltpu.make_async_remote_copy(
            src_ref=src[s].at[j % OWN_SLOTS],
            dst_ref=dst[s].at[slot],
            send_sem=ss.at[s, slot],
            recv_sem=rs.at[s, slot],
            device_id=self.place.target(links[s], STAGES_ODD[s] if kind == "b" else links[s], j),
            device_id_type=MESH,
        )

    def multiply(self, j):
        first = 0
        for right_ref, k, n in self.operands:

            @pl.when((j >= first) & (j < first + k * n))
            def _():
                cols = pl.ds(pl.multiple_of((j - first) % n * COLS, COLS), COLS)
                self.right[...] = right_ref[:, cols]

            first += k * n
        left = jnp.where(j < 2 * OUT_BLOCKS, 1 + j // OUT_BLOCKS, 0)
        self.tmp[...] = dot(self.left[left], self.right[...])

    def begin(self, j):
        slot = j % OWN_SLOTS
        self.multiply(j)
        place, rep = self.place, self.place.rep
        src_a, acc_a = self.kinds["a"][1][0], self.kinds["a"][3][0]
        src_b, acc_b = self.kinds["b"][1][0], self.kinds["b"][3][0]
        for d_core in range(2):
            for b in range(8):
                owner = place.owner(b & 1, b >> 1 & 1, b >> 2 & 1, d_core)
                block = self.tmp[pl.ds(pl.multiple_of(owner * ROWS, ROWS), ROWS), :HALF]
                to = slice(b * ROWS, (b + 1) * ROWS)
                if d_core:
                    src_a[slot, to, :] = block.astype(BF)
                else:
                    acc_a[slot, to, :] = block
                owner = choose(j, owner, place.owner(b >> 1 & 1, b >> 2 & 1, b & 1, d_core))
                for d_rep in range(2):
                    top = owner * ROWS + (1 - rep if d_rep else rep) * (ROWS // 2)
                    block = self.tmp[pl.ds(pl.multiple_of(top, ROWS // 2), ROWS // 2), HALF:]
                    to = slice((d_rep * 8 + b) * (ROWS // 2), (d_rep * 8 + b + 1) * (ROWS // 2))
                    if d_core:
                        src_b[slot, to, :] = block.astype(BF)
                    else:
                        acc_b[slot, to, :] = block
        self.copy("a", 0, j).start()
        self.copy("b", 0, j).start()

    def go_on(self, kind, s, j):
        links, src, dst, acc, _, _ = self.kinds[kind]
        slot, own = j % SLOTS, j % OWN_SLOTS
        self.copy(kind, s - 1, j).wait()
        size = src[s].shape[1]
        if s == len(links) - 1:
            src[s][own] = (acc[s - 1][own] + dst[s - 1][slot].astype(F32)).astype(BF)
        else:
            src[s][own] = (acc[s - 1][own, size:, :] + dst[s - 1][slot, size:, :].astype(F32)).astype(BF)
            acc[s][own] = acc[s - 1][own, :size, :] + dst[s - 1][slot, :size, :].astype(F32)
        self.copy(kind, s, j).start()

    def leave(self, j):
        cols = pl.ds(pl.multiple_of(j * COLS, COLS), COLS)
        slot = j % SLOTS
        return pltpu.make_async_copy(self.stage.at[slot], self.out_ref.at[:, cols], self.out_sem.at[slot])

    def finish(self, kind, j):
        links, src, dst, _, _, _ = self.kinds[kind]
        slot, own = j % SLOTS, j % OWN_SLOTS
        self.copy(kind, len(links) - 1, j).wait()
        rep = self.place.rep
        if kind == "a":

            @pl.when(j >= SLOTS)
            def _():
                self.leave(j - SLOTS).wait()

            self.stage[slot, :, :HALF] = src[-1][own].astype(F32) + dst[-1][slot].astype(F32)
        else:
            mine = pl.ds(pl.multiple_of(rep * (ROWS // 2), ROWS // 2), ROWS // 2)
            theirs = pl.ds(pl.multiple_of((1 - rep) * (ROWS // 2), ROWS // 2), ROWS // 2)
            self.stage[slot, mine, HALF:] = src[-1][own].astype(F32)
            self.stage[slot, theirs, HALF:] = dst[-1][slot].astype(F32)
            self.leave(j).start()

    def side_copy(self, k):
        return pltpu.make_async_remote_copy(
            src_ref=self.side_out.at[k],
            dst_ref=self.side_in.at[k],
            send_sem=self.side_sems.at[0, k],
            recv_sem=self.side_sems.at[1, k],
            device_id=self.place.targets[SIDE_LINKS[k]],
            device_id_type=MESH,
        )

    def open(self):
        self.place.greet()
        self.side_out[0] = jnp.zeros((8, SIDE_WIDE), F32)

    def tick(self, t):
        n_a, n_b = len(STAGES_A), len(STAGES_B)
        for s in range(n_b, -1, -1):
            j = t - LAG * s

            @pl.when((j >= 0) & (j < self.work.blocks))
            def _():
                if s == 0:
                    self.begin(j)
                    return
                if s < n_b:
                    self.go_on("b", s, j)
                else:
                    self.finish("b", j)
                if s < n_a:
                    self.go_on("a", s, j)
                elif s == n_a:
                    self.finish("a", j)

    def pump(self, now, pumps):
        def more(t, _):
            self.tick(t)
            return 0

        lax.fori_loop(now * SCAN_TICKS // pumps, (now + 1) * SCAN_TICKS // pumps, more, 0)


def join_kernel(dh_ref, e_ref, branch_ref, e_out, low_out, factor_out):
    e = e_ref[...].astype(F32) + dh_ref[...]
    low = e.astype(BF)
    e_out[...] = e
    low_out[...] = low
    factor = jnp.sum(low.astype(F32) * branch_ref[...], axis=1, keepdims=True) * (1.0 / INNER)
    factor_out[...] = jnp.broadcast_to(factor, factor_out.shape)


def join(dh, gradient, branch):
    part = 128
    rows = lambda a: pl.BlockSpec((part, a), lambda k: (k, 0))
    shape = lambda a, t: jax.ShapeDtypeStruct(a, t)
    return pl.pallas_call(
        join_kernel,
        grid=(TOK // part,),
        out_shape=(shape((TOK, D), F32), shape((TOK, D), BF), shape((TOK, 128), F32)),
        in_specs=[rows(D), rows(D), rows(D)],
        out_specs=(rows(D), rows(D), rows(128)),
        compiler_params=pltpu.CompilerParams(vmem_limit_bytes=60 * 2**20),
        cost_estimate=pl.CostEstimate(flops=10**7, bytes_accessed=15 * 2**20, transcendentals=0),
        name="join",
    )(dh, gradient, branch)


def adamw_step(parameter, first_moment, second_moment, gradient, step_rate, decay_rate):
    first_new = BETA_ONE * first_moment + (1.0 - BETA_ONE) * gradient
    second_new = BETA_TWO * second_moment + (1.0 - BETA_TWO) * gradient * gradient
    correction_one = 1.0 - BETA_ONE**STEP
    correction_two = 1.0 - BETA_TWO**STEP
    update = first_new / correction_one / (jnp.sqrt(second_new / correction_two) + ADAM_EPSILON)
    return (parameter - step_rate * (update + decay_rate * parameter), first_new, second_new)


def adam_kernel(wi, mi, vi, wo, mo, vo, sums_0, sums_1, e_ref, dh_ref, *outs):
    outs[-1][...] = e_ref[...] + dh_ref[...]
    for layer, sums in enumerate((sums_0, sums_1)):

        @pl.when(pl.program_id(0) == layer)
        def _():
            width = wi.shape[2]
            todo = [((wi, mi, vi), outs[:3], 0, sums[:, 2 * D : 2 * D + width])]
            todo += [((wo, mo, vo), outs[3:6], (0, q), sums[:, q * D : (q + 1) * D]) for q in range(2)]
            for refs, to, at, gradient in todo:
                values = adamw_step(*(ref[at] for ref in refs), gradient, RATE_MATRIX, DECAY_MATRIX)
                for ref, value in zip(to, values):
                    ref[at] = value


def adam(inputs, outputs, sums, gradient, dh):
    part = 24
    outputs = [a.reshape(LAYERS, 2, ROWS, D) for a in outputs]
    width = inputs[0].shape[2]
    in_spec = pl.BlockSpec((1, part, width), lambda l, k: (l, k, 0))
    out_spec = pl.BlockSpec((1, 2, part, D), lambda l, k: (l, 0, k, 0))
    steps = ROWS // part
    row_spec = pl.BlockSpec((TOK // (LAYERS * steps), D), lambda l, k: (l * steps + k, 0))
    only_0 = lambda l, k: (jnp.where(l == 0, k, ROWS // part - 1), 0)
    only_1 = lambda l, k: (jnp.where(l == 1, k, 0), 0)
    done = pl.pallas_call(
        adam_kernel,
        grid=(LAYERS, ROWS // part),
        out_shape=tuple(jax.ShapeDtypeStruct(a.shape, F32) for a in (*inputs, *outputs, gradient)),
        in_specs=[in_spec] * 3
        + [out_spec] * 3
        + [pl.BlockSpec((part, a.shape[1]), at) for a, at in zip(sums, (only_0, only_1))]
        + [row_spec] * 2,
        out_specs=(in_spec,) * 3 + (out_spec,) * 3 + (row_spec,),
        compiler_params=pltpu.CompilerParams(vmem_limit_bytes=60 * 2**20),
        cost_estimate=pl.CostEstimate(flops=10**8, bytes_accessed=52 * 2**20, transcendentals=0),
        name="adam",
    )(*inputs, *outputs, *sums, gradient, dh)
    return done[:3], [a.reshape(LAYERS, 2 * ROWS, D) for a in done[3:6]], done[6]


GATHER_A = ("far", "z", "y", "core")
GATHER_B = ("far", "z", "y", "rep", "core")
GATHER_ODD = ("y", "far", "z", "rep", "core")
GATHER_SLOTS = 6 * LAG


def gather_kernel(
    blocks, w_in, w_out, r_ref, full_in, full_out, zx,
    own_in, own_out, buf_a, buf_b, natural, zbuf, local, flush, ss_a, rs_a, ss_b, rs_b,
):
    place = Place()
    rep = place.rep
    kinds = {"a": (GATHER_A, buf_a, ROWS, ss_a, rs_a), "b": (GATHER_B, buf_b, ROWS // 2, ss_b, rs_b)}
    valid = w_in.shape[2] - (IN_BLOCKS - 1) * COLS

    def copy(kind, s, j):
        links, buf, rows, ss, rs = kinds[kind]
        slot = j % GATHER_SLOTS
        size = rows << s
        return pltpu.make_async_remote_copy(
            src_ref=buf.at[slot, 0:size, :],
            dst_ref=buf.at[slot, size : 2 * size, :],
            send_sem=ss.at[s, slot],
            recv_sem=rs.at[s, slot],
            device_id=place.target(links[s], GATHER_ODD[s] if kind == "b" else links[s], j),
            device_id_type=MESH,
        )

    def begin(j):
        slot = j % GATHER_SLOTS
        mine = pl.ds(pl.multiple_of(rep * (ROWS // 2), ROWS // 2), ROWS // 2)

        @pl.when(j < IN_BLOCKS - 1)
        def _():
            lo = pl.multiple_of(j * COLS, COLS)
            buf_a[slot, 0:ROWS, :] = own_in[:, pl.ds(lo, HALF)].astype(BF)
            buf_b[slot, 0 : ROWS // 2, :] = own_in[mine, pl.ds(pl.multiple_of(lo + HALF, HALF), HALF)].astype(BF)

        @pl.when(j == IN_BLOCKS - 1)
        def _():
            buf_a[slot, 0:ROWS, :] = jnp.zeros((ROWS, HALF), BF)
            buf_b[slot, 0 : ROWS // 2, :] = jnp.zeros((ROWS // 2, HALF), BF)
            buf_a[slot, 0:ROWS, 0:valid] = own_in[:, (IN_BLOCKS - 1) * COLS :].astype(BF)

        if blocks > IN_BLOCKS:

            @pl.when(j >= IN_BLOCKS)
            def _():
                k = j - IN_BLOCKS
                q = k // OUT_BLOCKS
                lo = pl.multiple_of(k % OUT_BLOCKS * COLS, COLS)
                buf_a[slot, 0:ROWS, :] = own_out[q, :, pl.ds(lo, HALF)].astype(BF)
                buf_b[slot, 0 : ROWS // 2, :] = own_out[q, mine, pl.ds(pl.multiple_of(lo + HALF, HALF), HALF)].astype(BF)

        copy("a", 0, j).start()
        copy("b", 0, j).start()

    def out_copies(j):
        p = j % 2
        cols = pl.ds(pl.multiple_of(j * COLS, COLS), COLS)
        return (
            pltpu.make_async_copy(natural.at[p], full_in.at[:, :, cols], flush.at[0, p]),
            pltpu.make_async_copy(zbuf.at[p], zx.at[:, cols], flush.at[1, p]),
        )

    def row_copy(j):
        p = j % 2
        k = j - IN_BLOCKS
        cols = pl.ds(pl.multiple_of(k % OUT_BLOCKS * COLS, COLS), COLS)
        q = k // OUT_BLOCKS
        return pltpu.make_async_copy(natural.at[p], full_out.at[q // 2, :, q % 2, :, cols], flush.at[0, p])

    def flushed(j):
        @pl.when((j >= 0) & (j < IN_BLOCKS))
        def _():
            for c in out_copies(j):
                c.wait()

        if blocks > IN_BLOCKS:

            @pl.when(j >= IN_BLOCKS)
            def _():
                row_copy(j).wait()

    def finish(j):
        slot = j % GATHER_SLOTS
        p = j % 2
        copy("b", len(GATHER_B) - 1, j).wait()
        flushed(j - 2)
        for k in range(16):
            owner = place.owner(k & 1, k >> 1 & 1, k >> 2 & 1, k >> 3)
            natural[p, owner, :, :HALF] = buf_a[slot, k * ROWS : (k + 1) * ROWS, :]
            owner = choose(j, owner, place.owner(k >> 1 & 1, k >> 2 & 1, k & 1, k >> 3))
            for d_rep in range(2):
                at = (k & 7) + 8 * d_rep + 16 * (k >> 3)
                half = pl.ds(pl.multiple_of((1 - rep if d_rep else rep) * (ROWS // 2), ROWS // 2), ROWS // 2)
                natural[p, owner, half, HALF:] = buf_b[slot, at * (ROWS // 2) : (at + 1) * (ROWS // 2), :]

        @pl.when(j < IN_BLOCKS)
        def _():
            zbuf[p] = dot(r_ref[...], natural[p].reshape(16 * ROWS, COLS))
            for c in out_copies(j):
                c.start()

        if blocks > IN_BLOCKS:

            @pl.when(j >= IN_BLOCKS)
            def _():
                row_copy(j).start()

    loads = [pltpu.make_async_copy(w_in.at[0], own_in, local.at[0])]
    loads.append(pltpu.make_async_copy(w_out, own_out, local.at[1]))
    for load in loads:
        load.start()
    place.greet()
    for load in loads:
        load.wait()

    def tick(t, _):
        for s in range(len(GATHER_B), -1, -1):
            j = t - LAG * s

            @pl.when((j >= 0) & (j < blocks))
            def _():
                if s == 0:
                    begin(j)
                elif s == len(GATHER_B):
                    finish(j)
                else:
                    copy("b", s - 1, j).wait()
                    copy("b", s, j).start()
                    copy("a", s - 1, j).wait()
                    if s < len(GATHER_A):
                        copy("a", s, j).start()

        return 0

    lax.fori_loop(0, blocks + LAG * len(GATHER_B), tick, 0)
    flushed(jnp.int32(blocks - 2))
    flushed(jnp.int32(blocks - 1))


def gather_first(weight_in, weight_out, normed):
    outs = weight_out.reshape(2 * LAYERS, ROWS, D)
    blocks = IN_BLOCKS + outs.shape[0] * OUT_BLOCKS
    hbm = pl.BlockSpec(memory_space=pl.ANY)
    sems = pltpu.SemaphoreType.DMA
    full_in, full_out, zx = pl.pallas_call(
        partial(gather_kernel, blocks),
        out_shape=(
            jax.ShapeDtypeStruct((16, ROWS, WIDTH), BF),
            jax.ShapeDtypeStruct((LAYERS, 16, 2, ROWS, D), BF),
            jax.ShapeDtypeStruct((TOK, WIDTH), F32),
        ),
        in_specs=[hbm, hbm, pl.BlockSpec(memory_space=pltpu.VMEM)],
        out_specs=(hbm,) * 3,
        scratch_shapes=[
            pltpu.VMEM(weight_in.shape[1:], F32),
            pltpu.VMEM(outs.shape, F32),
            pltpu.VMEM((GATHER_SLOTS, 16 * ROWS, HALF), BF),
            pltpu.VMEM((GATHER_SLOTS, 16 * ROWS, HALF), BF),
            pltpu.VMEM((2, 16, ROWS, COLS), BF),
            pltpu.VMEM((2, TOK, COLS), F32),
            sems((2,)),
            sems((2, 2)),
            sems((len(GATHER_A), GATHER_SLOTS)),
            sems((len(GATHER_A), GATHER_SLOTS)),
            sems((len(GATHER_B), GATHER_SLOTS)),
            sems((len(GATHER_B), GATHER_SLOTS)),
        ],
        compiler_params=pltpu.CompilerParams(
            collective_id=4, has_side_effects=True, vmem_limit_bytes=60 * 2**20
        ),
        cost_estimate=pl.CostEstimate(flops=10**10, bytes_accessed=50 * 2**20, transcendentals=0),
        name="gather_first",
    )(weight_in, outs, normed)
    return full_in.reshape(16 * ROWS, WIDTH), full_out.reshape(LAYERS, INNER, D), zx


def project_kernel(r_ref, w_ref, out_ref):
    out_ref[...] = dot(r_ref[...], w_ref[...])


def project(normed, full_in):
    part = WIDTH // 4
    return pl.pallas_call(
        project_kernel,
        grid=(WIDTH // part,),
        out_shape=jax.ShapeDtypeStruct((TOK, WIDTH), F32),
        in_specs=[
            pl.BlockSpec((TOK, D), lambda k: (0, 0), pipeline_mode=pl.Buffered(1)),
            pl.BlockSpec((D, part), lambda k: (0, k)),
        ],
        out_specs=pl.BlockSpec((TOK, part), lambda k: (0, k)),
        compiler_params=pltpu.CompilerParams(vmem_limit_bytes=60 * 2**20),
        cost_estimate=pl.CostEstimate(flops=10**10, bytes_accessed=36 * 2**20, transcendentals=0),
        name="project",
    )(normed, full_in)


def rows_kernel(normed_ref, mixed_ref, out_ref):
    out_ref[0] = normed_ref[...].astype(F32).T.astype(BF)
    turned = mixed_ref[...].astype(F32).T.astype(BF)
    for i in range(turned.shape[0] // (2 * ROWS)):
        for q in range(2):
            lo = (2 * i + q) * ROWS
            out_ref[1 + q, i * ROWS : (i + 1) * ROWS, :] = turned[lo : lo + ROWS]


def left_rows(normed, mixed):
    steps = 4
    wide = D // steps
    return pl.pallas_call(
        rows_kernel,
        grid=(steps,),
        out_shape=jax.ShapeDtypeStruct((3, D, TOK), BF),
        in_specs=[
            pl.BlockSpec((TOK, wide), lambda k: (0, k)),
            pl.BlockSpec((TOK, 2 * wide), lambda k: (0, k)),
        ],
        out_specs=pl.BlockSpec((3, wide, TOK), lambda k: (0, k, 0)),
        compiler_params=pltpu.CompilerParams(vmem_limit_bytes=60 * 2**20),
        cost_estimate=pl.CostEstimate(flops=0, bytes_accessed=9 * 2**20, transcendentals=0),
        name="left_rows",
    )(normed, mixed)


def span_starts(seq_lengths):
    offsets = jnp.cumsum(seq_lengths) - seq_lengths
    places = jnp.arange(seq_lengths.shape[0], dtype=jnp.int32) * SPAN
    matches = (offsets[None, :] == places[:, None]) & (seq_lengths[None, :] > 0)
    return jnp.any(matches, axis=1)


def swap(value, axis, count, bit):
    return lax.ppermute(value, axis, [(i, i ^ bit) for i in range(count)])


def plain_owner_sum(left, right, reps):
    mine = lax.psum_scatter(dot(left, right, TN).astype(BF), "shard", scatter_dimension=0, tiled=True)
    total = mine.astype(F32)
    for bit in [1 << k for k in range(reps.bit_length() - 1)]:
        total = total + swap(total.astype(BF), "rep", reps, bit).astype(F32)
    return total


def side_gradient(block):
    conv = block[: CONV + 1, :SIDE_STEPS].reshape(-1)
    steps = block[:2, SIDE_STEPS : SIDE_STEPS + HEADS].reshape(-1)
    skip = jnp.sum(block[5, :INNER].reshape(HEADS, HEAD_DIM), axis=1)
    return jnp.concatenate([block[7, :D], block[6, :INNER], conv, steps, skip])


def pad_cast(weight, width):
    return jnp.pad(weight.astype(BF), ((0, 0), (0, width - weight.shape[1])))


def sums_plain(normed, mixed, dz, dxs, dbc, low, full_in, reps):
    right = jnp.concatenate([dz, *dxs, dbc], axis=1)
    used = 2 * INNER + 2 * STATE + HEADS
    sum_in = plain_owner_sum(normed, right[:, :used], reps)
    sum_out = plain_owner_sum(mixed, low, reps)
    return sum_in, sum_out, dot(right, full_in, NT)


def per_device(
    tokens, cotangent, lengths,
    weight_in, moment_in, second_in,
    weight_out, moment_out, second_out,
    side_params, side_moment, side_second,
    *, reps, shards,
):
    direct = shards == 16 and reps == 2
    cont = jnp.where(span_starts(lengths[0])[1], 0.0, 1.0).astype(F32).reshape(1, 1)
    hidden = tokens.astype(F32)
    saved = []
    layer_outs = []
    for layer in range(LAYERS):
        gain = side_params[layer, :D]
        inverse_in = lax.rsqrt(jnp.mean(hidden * hidden, axis=-1, keepdims=True) + EPSILON)
        normed = (hidden * inverse_in * gain).astype(BF)
        if direct and layer == 0:
            normed, later = lax.optimization_barrier((normed, pad_cast(weight_in[1], WIDTH)))
            first_in, both_out, zx = gather_first(weight_in, weight_out, normed)
            zx, later = lax.optimization_barrier((zx, later))
            second_in_full = lax.all_gather(later, "shard", axis=0, tiled=True)
            full_in, full_out = first_in, both_out[0]
        elif direct:
            full_in, full_out = second_in_full, both_out[1]
            zx = project(normed, full_in)
        else:
            full_in = lax.all_gather(pad_cast(weight_in[layer], WIDTH), "shard", axis=0, tiled=True)
            full_out = lax.all_gather(weight_out[layer].astype(BF), "shard", axis=0, tiled=True)
            zx = jnp.dot(normed, full_in, preferred_element_type=F32)
        mixed, y, inverse = mixer_fwd(zx, cont, side_params[layer])
        left = None
        if direct:
            mixed, left = lax.optimization_barrier((mixed, left_rows(normed, mixed)))
        branch = jnp.dot(mixed, full_out, preferred_element_type=F32)
        saved.append((full_in, full_out, hidden, inverse_in, normed, zx, mixed, y, inverse, branch, left))
        hidden = hidden + branch
        layer_outs.append(hidden)
    gradient = cotangent.astype(F32)
    low = cotangent
    factor = jnp.sum(gradient * saved[-1][-2], axis=1, keepdims=True) * (1.0 / INNER)
    sums = [None] * LAYERS
    sides = [None] * LAYERS
    for layer in reversed(range(LAYERS)):
        full_in, full_out, hidden, inverse_in, normed, zx, mixed, y, inverse, branch, left = saved[layer]
        side_row = side_params[layer]
        gain = side_row[:D]
        rows = jnp.concatenate([inverse[:, :1], factor[:, :1], jnp.zeros((TOK, 126), F32)], axis=1)
        dz, dy, dgain = gate_bwd(low, full_out, zx, side_row, y, rows)
        if direct:
            inverse_rows = jnp.broadcast_to(inverse_in, (TOK, 128))
            gain_rows = jnp.broadcast_to(gain, (8, D))
            work = Sums(left, low, dz, dgain, hidden, inverse_rows, gain_rows, full_in)
            back, sums[layer], side = scan_bwd(zx, cont, side_row, y, dy, work)
            sides[layer] = side_gradient(side[-1])
        else:
            dx, dskip, dcw, dbc, dcwbc, dhp = scan_bwd(zx, cont, side_row, y, dy, NoWork())
            side = mixer_side(dgain, dskip, dcw, dcwbc, dhp)
            sum_in, sum_out, back = sums_plain(normed, mixed, dz, [dx], dbc, low, full_in, reps)
            sums[layer] = (sum_in, sum_out)
            scaled = hidden * inverse_in
            side = jnp.concatenate([jnp.sum(back * scaled, axis=0), side])
            sides[layer] = lax.psum(side, ("rep", "shard"))
            dn = back * gain
            back = inverse_in * (dn - scaled * jnp.mean(dn * scaled, axis=1, keepdims=True))
        if layer:
            gradient, low, factor = join(back, gradient, saved[layer - 1][-2])
    if direct:
        new_in, new_out, gradient = adam(
            (weight_in, moment_in, second_in), (weight_out, moment_out, second_out), sums, gradient, back
        )
    else:
        gradient = gradient + back
        grad_in = jnp.stack([v[0] for v in sums])
        grad_out = jnp.stack([v[1] for v in sums])
        new_in = adamw_step(weight_in, moment_in, second_in, grad_in, RATE_MATRIX, DECAY_MATRIX)
        new_out = adamw_step(weight_out, moment_out, second_out, grad_out, RATE_MATRIX, DECAY_MATRIX)
    grad_side = jnp.stack(sides)
    return (
        jnp.stack(layer_outs),
        gradient,
        *new_in,
        *new_out,
        *adamw_step(side_params, side_moment, side_second, grad_side, RATE_SIDE, 0.0),
    )


def solution(mesh):
    rows = P(("rep", "shard"), None)
    owned = P(None, "shard", None)
    body = partial(per_device, reps=mesh.shape["rep"], shards=mesh.shape["shard"])
    return jax.shard_map(
        body,
        mesh=mesh,
        in_specs=(rows, rows, rows) + (owned,) * 6 + (P(),) * 3,
        out_specs=(P(None, ("rep", "shard"), None), rows) + (owned,) * 6 + (P(),) * 3,
        check_vma=False,
    )
```

```python
from functools import partial

import jax
import jax.numpy as jnp
from jax import lax
from jax.experimental import pallas as pl
from jax.experimental.pallas import tpu as pltpu
from jax.sharding import PartitionSpec as P

LAYERS = 2
STEP = 10
BETA_ONE = 0.9
BETA_TWO = 0.95
ADAM_EPSILON = 1e-08
RATE_MATRIX = 0.05
RATE_SIDE = 0.5
DECAY_MATRIX = 0.1
D = 1536
INNER = 3072
HEAD_DIM = 64
STATE = 128
CONV = 4
SPAN = 256
HEADS = 48
XBC = 3328
TOK = 512
GROUP = 8
BC_WIDE = 512
N_SCAN_SCRATCH = 19
PUMPS = GROUP // 2 + 1
WIDE = GROUP * HEAD_DIM
STEPS = HEADS // GROUP
HALO = 8
LOG2_E = 1.4426950408889634
EPSILON = 1e-05
HIGHEST = lax.Precision.HIGHEST
BF = jnp.bfloat16
F32 = jnp.float32


def dot(a, b, dims=((1,), (0,)), precision=None):
    return lax.dot_general(a, b, (dims, ((), ())), precision=precision, preferred_element_type=F32)


NT = ((1,), (1,))
TN = ((0,), (0,))


def sigmoid(v):
    return 1.0 / (1.0 + jnp.exp(-v))


def softplus(v):
    e = jnp.exp(-jnp.abs(v))
    u = 1.0 + e
    tail = jnp.where(u == 1.0, e, jnp.log(u) * (e / jnp.where(u == 1.0, 1.0, u - 1.0)))
    return jnp.maximum(v, 0.0) + tail


def load_halo(buf, xin, cont, width):
    buf[0:HALO, :width] = jnp.zeros((HALO, width), F32)
    buf[HALO : HALO + SPAN, :width] = xin[0:SPAN]
    buf[HALO + SPAN : 2 * HALO + SPAN, :width] = xin[SPAN - HALO : SPAN] * cont
    buf[2 * HALO + SPAN : 2 * (HALO + SPAN), :width] = xin[SPAN : 2 * SPAN]


def shifted(buf, k, span, width, lo=0, rows=SPAN):
    base = span * (HALO + SPAN) + HALO - k + lo
    return buf[base : base + rows, :width]


def conv_of(buf, cw, span, width, lo=0, rows=SPAN):
    total = cw[4:5, :] + cw[3:4, :] * shifted(buf, 0, span, width, lo, rows)
    for k in range(1, CONV):
        total = total + cw[3 - k : 4 - k, :] * shifted(buf, k, span, width, lo, rows)
    return total


def lower_tri():
    return (
        lax.broadcasted_iota(jnp.int32, (SPAN, SPAN), 0)
        >= lax.broadcasted_iota(jnp.int32, (SPAN, SPAN), 1)
    )


def setup(cont, bc_ref, dt_ref, cwbc_ref, hp_ref, buf, bct, scores, dts, cum, cumt):
    load_halo(buf, bc_ref[...], cont, 2 * STATE)
    for span in range(2):
        lo = span * SPAN
        s = conv_of(buf, cwbc_ref[...], span, 2 * STATE)
        bct[lo : lo + SPAN, :] = (s * sigmoid(s)).astype(BF)
        sc = dot(bct[lo : lo + SPAN, STATE:], bct[lo : lo + SPAN, :STATE], NT)
        scores[lo : lo + SPAN, :] = jnp.where(lower_tri(), sc, 0.0)
    lane = lax.broadcasted_iota(jnp.int32, (TOK, 128), 1)
    raw = jnp.where(lane < HEADS, dt_ref[...], 0.0) + hp_ref[0:1, :]
    step = jnp.where(lane < HEADS, softplus(raw), 0.0)
    dts[...] = step
    a = (-LOG2_E * jnp.exp(hp_ref[1:2, :])) * step
    tri = jnp.where(lower_tri(), 1.0, 0.0)
    for span in range(2):
        lo = span * SPAN
        cum[lo : lo + SPAN, :] = dot(tri, a[lo : lo + SPAN, :], precision=HIGHEST)
    cumt[...] = cum[...].T


def split_dot(value, ones):
    high = value.astype(BF)
    low = (value - high.astype(F32)).astype(BF)
    return dot(high, ones) + dot(low, ones)


def spread_of():
    lane = lax.broadcasted_iota(jnp.int32, (128, WIDE), 0)
    column = lax.broadcasted_iota(jnp.int32, (128, WIDE), 1)
    return jnp.where(lane == column // HEAD_DIM, 1.0, 0.0).astype(BF)


def fwd_kernel(
    cont_ref, z_ref, x_ref, bc_ref, dt_ref, cwx_ref, cwbc_ref, hp_ref, cp_ref, gain_ref,
    m_ref, y_ref, inv_ref,
    buf, bct, scores, dts, cum, cumt, mix, xt, g_s, ssq, grp, state,
):
    g = pl.program_id(0)
    cont = cont_ref[0, 0]

    @pl.when(g == 0)
    def _():
        setup(cont, bc_ref, dt_ref, cwbc_ref, hp_ref, buf, bct, scores, dts, cum, cumt)
        ssq[...] = jnp.zeros_like(ssq)

    shift = lax.rem(128 - GROUP * g, 128)
    grp[0] = pltpu.roll(dts[...], shift, 1)
    grp[1] = pltpu.roll(cum[...], shift, 1)
    rows8 = cumt[pl.ds(pl.multiple_of(g * GROUP, GROUP), GROUP), :]
    load_halo(buf, x_ref[...], cont, WIDE)
    spread = spread_of()
    for span in range(2):
        lo = span * SPAN
        s = conv_of(buf, cwx_ref[...], span, WIDE)
        x = s * sigmoid(s)
        y_ref[lo : lo + SPAN, :] = x * cp_ref[1:2, :]
        xt[lo : lo + SPAN, :] = x * split_dot(grp[0, lo : lo + SPAN, :], spread)
    last = grp[1, SPAN - 1 : SPAN, :]
    xw = xt[0:SPAN, :] * split_dot(jnp.exp2(last - grp[1, 0:SPAN, :]), spread)
    st = dot(bct[0:SPAN, :STATE], xw.astype(BF), TN) * cont
    y_ref[SPAN:, :] += split_dot(jnp.exp2(grp[1, SPAN:, :]), spread) * dot(bct[SPAN:, STATE:], st.astype(BF))
    first = lax.broadcasted_iota(jnp.int32, (SPAN, 128), 1) < HEAD_DIM
    for span in range(2):
        lo = span * SPAN
        for j in range(0, GROUP, 2):
            slot = j // 2 % 2
            for h in range(2):
                fill_mix(mix, slot, h, scores, grp, rows8, span, j + h)
            cs = slice(j * HEAD_DIM, j * HEAD_DIM + 128)
            xp = xt[lo : lo + SPAN, cs]
            both = jnp.concatenate([jnp.where(first, xp, 0.0), jnp.where(first, 0.0, xp)], axis=0)
            y_ref[lo : lo + SPAN, cs] += dot(mix[slot], both.astype(BF))
    z = z_ref[...]
    gated = y_ref[...] * (z * sigmoid(z))
    g_s[g] = gated
    ssq[...] += jnp.broadcast_to(jnp.sum(gated * gated, axis=1, keepdims=True), ssq.shape)

    @pl.when(g == STEPS - 1)
    def _():
        inv = lax.rsqrt(ssq[...] * (1.0 / INNER) + EPSILON)
        inv_ref[...] = inv
        col = inv[:, 0:1]
        for k in range(STEPS):
            m_ref[:, k * WIDE : (k + 1) * WIDE] = (
                g_s[k] * col * gain_ref[0:1, k * WIDE : (k + 1) * WIDE]
            ).astype(BF)


CHUNK = 64


def fill_mix(mix, slot, h, scores, grp, rows8, span, j):
    lo = span * SPAN
    base = h * SPAN
    for r in range(0, SPAN, CHUNK):
        wide = 128 if r + CHUNK <= 128 else 256
        gap = grp[1, lo + r : lo + r + CHUNK, j : j + 1] - rows8[j : j + 1, lo : lo + wide]
        val = scores[lo + r : lo + r + CHUNK, :wide] * jnp.exp2(jnp.minimum(gap, 0.0))
        mix[slot, r : r + CHUNK, base : base + wide] = val.astype(BF)
        if wide < 256:
            mix[slot, r : r + CHUNK, base + wide : base + 256] = jnp.zeros((CHUNK, 256 - wide), BF)


def head_rows(side_row):
    cur = D + INNER + CONV * XBC + XBC
    rows = side_row[cur : cur + 3 * HEADS].reshape(3, HEADS)
    return jnp.pad(rows, ((0, 5), (0, 128 - HEADS)))


def conv_rows(side_row):
    cur = D + INNER
    rows = side_row[cur : cur + (CONV + 1) * XBC].reshape(CONV + 1, XBC)
    return jnp.pad(rows, ((0, 3), (0, 0)))


def column_rows(side_row):
    gain = side_row[D : D + INNER]
    skip = jnp.repeat(side_row[-HEADS:], HEAD_DIM)
    return jnp.pad(jnp.stack([gain, skip]), ((0, 6), (0, 0)))


def mixer_fwd(zx, cont, side_row):
    hp, cw, cp = head_rows(side_row), conv_rows(side_row), column_rows(side_row)
    full = lambda shape: pl.BlockSpec(shape, lambda g: (0,) * len(shape))
    return pl.pallas_call(
        fwd_kernel,
        grid=(STEPS,),
        out_shape=(
            jax.ShapeDtypeStruct((TOK, INNER), BF),
            jax.ShapeDtypeStruct((TOK, INNER), F32),
            jax.ShapeDtypeStruct((TOK, 128), F32),
        ),
        in_specs=[
            pl.BlockSpec(memory_space=pltpu.SMEM),
            pl.BlockSpec((TOK, WIDE), lambda g: (0, g)),
            pl.BlockSpec((TOK, WIDE), lambda g: (0, STEPS + g)),
            pl.BlockSpec((TOK, 2 * STATE), lambda g: (0, 2 * INNER // (2 * STATE))),
            pl.BlockSpec((TOK, 128), lambda g: (0, (INNER + XBC) // 128)),
            pl.BlockSpec((8, WIDE), lambda g: (0, g)),
            pl.BlockSpec((8, 2 * STATE), lambda g: (0, INNER // (2 * STATE))),
            full((8, 128)),
            pl.BlockSpec((8, WIDE), lambda g: (0, g)),
            full((8, INNER)),
        ],
        out_specs=(
            full((TOK, INNER)),
            pl.BlockSpec((TOK, WIDE), lambda g: (0, g)),
            full((TOK, 128)),
        ),
        scratch_shapes=[
            pltpu.VMEM((2 * (HALO + SPAN), WIDE), F32),
            pltpu.VMEM((TOK, 2 * STATE), BF),
            pltpu.VMEM((TOK, SPAN), F32),
            pltpu.VMEM((TOK, 128), F32),
            pltpu.VMEM((TOK, 128), F32),
            pltpu.VMEM((128, TOK), F32),
            pltpu.VMEM((2, SPAN, 2 * SPAN), BF),
            pltpu.VMEM((TOK, WIDE), F32),
            pltpu.VMEM((STEPS, TOK, WIDE), F32),
            pltpu.VMEM((TOK, 128), F32),
            pltpu.VMEM((2, TOK, 128), F32),
            pltpu.VMEM((STATE, WIDE), F32),
        ],
        compiler_params=pltpu.CompilerParams(vmem_limit_bytes=60 * 2**20),
        cost_estimate=pl.CostEstimate(flops=6 * 10**9, bytes_accessed=25 * 2**20, transcendentals=10**7),
        name="mixer_fwd",
    )(cont, zx, zx, zx, zx, cw, cw, hp, cp, cp)


def gate_kernel(low_ref, w_ref, z_ref, cp_ref, y_ref, row_ref, dz_ref, dy_ref, dgain_ref):
    dm = dot(low_ref[...], w_ref[...], NT)
    z = z_ref[...]
    sz = sigmoid(z)
    gate = z * sz
    y = y_ref[...]
    inv = row_ref[:, 0:1]
    gn = y * gate * inv
    dgain_ref[...] = jnp.zeros_like(dgain_ref)
    dgain_ref[0:1, :] = jnp.sum(dm * gn, axis=0, keepdims=True)
    dg = inv * (dm * cp_ref[0:1, :] - gn * row_ref[:, 1:2])
    dz_ref[...] = (dg * y * (sz * (1.0 + z * (1.0 - sz)))).astype(BF)
    dy_ref[...] = (dg * gate).astype(BF)


def gate_bwd(low, full_out, zx, side_row, y, rows):
    cp = column_rows(side_row)
    by_g = lambda rows_: pl.BlockSpec((rows_, WIDE), lambda g: (0, g))
    full = lambda shape: pl.BlockSpec(shape, lambda g: (0,) * len(shape))
    return pl.pallas_call(
        gate_kernel,
        grid=(STEPS,),
        out_shape=(
            jax.ShapeDtypeStruct((TOK, INNER), BF),
            jax.ShapeDtypeStruct((TOK, INNER), BF),
            jax.ShapeDtypeStruct((8, INNER), F32),
        ),
        in_specs=[
            full((TOK, D)),
            pl.BlockSpec((WIDE, D), lambda g: (g, 0)),
            by_g(TOK),
            by_g(8),
            by_g(TOK),
            full((TOK, 128)),
        ],
        out_specs=(by_g(TOK), by_g(TOK), by_g(8)),
        compiler_params=pltpu.CompilerParams(vmem_limit_bytes=60 * 2**20),
        cost_estimate=pl.CostEstimate(flops=5 * 10**9, bytes_accessed=40 * 2**20, transcendentals=2 * 10**6),
        name="gate_bwd",
    )(low, full_out, zx, cp, y, rows)


def scan_kernel(
    work, cont_ref, x_ref, bc_ref, dt_ref, cwx_ref, cwbc_ref, hp_ref, cp_ref, y_ref, dy, *rest,
):
    g = pl.program_id(0)
    scratch = rest[-N_SCAN_SCRATCH:]
    buf, bct, scores, dts, cum, cumt, mix, decay, xt, xf, sig, dsum, dtx, dxt, dscore, dbcs, dcum, ddt, grp = scratch
    engine = work.engine(rest[:-N_SCAN_SCRATCH], (xt, xf, sig))
    dx_ref, dskip_ref, dcw_ref, dbc_ref, dcwbc_ref, dhp_ref = engine.outputs(g)
    cont = cont_ref[0, 0]

    @pl.when(g == 0)
    def _():
        engine.open()

    @pl.when(g == 0)
    def _():
        setup(cont, bc_ref, dt_ref, cwbc_ref, hp_ref, buf, bct, scores, dts, cum, cumt)
        for ref in (dscore, dbcs, dcum, ddt):
            ref[...] = jnp.zeros_like(ref)

    shift = lax.rem(128 - GROUP * g, 128)
    grp[0] = pltpu.roll(dts[...], shift, 1)
    grp[1] = pltpu.roll(cum[...], shift, 1)
    load_halo(buf, x_ref[...], cont, WIDE)
    spread = spread_of()
    skip = cp_ref[1:2, :]
    dskip_ref[...] = jnp.zeros_like(dskip_ref)
    pick = jnp.where(
        lax.broadcasted_iota(jnp.int32, (WIDE, 128), 0) // HEAD_DIM + GROUP * g
        == lax.broadcasted_iota(jnp.int32, (WIDE, 128), 1),
        1.0,
        0.0,
    ).astype(BF)
    for span in range(2):
        lo = span * SPAN
        hi = lo + SPAN
        s = conv_of(buf, cwx_ref[...], span, WIDE)
        sg = sigmoid(s)
        x = s * sg
        xf[lo:hi, :] = x
        sig[lo:hi, :] = sg * (1.0 + s * (1.0 - sg))
        dtx[lo:hi, :] = split_dot(grp[0, lo:hi, :], spread)
        xt[lo:hi, :] = x * dtx[lo:hi, :]
        dyv = dy[lo:hi, :].astype(F32)
        dskip_ref[0:1, :] += jnp.sum(dyv * x, axis=0, keepdims=True)
        yin = y_ref[lo:hi, :] - skip * x
        dsum[lo:hi, :] = dyv * yin

    last = grp[1, SPAN - 1 : SPAN, :]
    wl = split_dot(jnp.exp2(last - grp[1, 0:SPAN, :]), spread)
    xw = (xt[0:SPAN, :] * wl).astype(BF)
    prior = (dot(bct[0:SPAN, :STATE], xw, TN) * cont).astype(BF)
    dye = (dy[SPAN:, :].astype(F32) * split_dot(jnp.exp2(grp[1, SPAN:, :]), spread)).astype(BF)
    dprior = (dot(bct[SPAN:, STATE:], dye, TN) * cont).astype(BF)
    dbcs[SPAN:, STATE:] += dot(dye, prior, NT)
    dbcs[0:SPAN, :STATE] += dot(xw, dprior, NT)
    dxt[0:SPAN, :] = dot(bct[0:SPAN, :STATE], dprior) * wl
    dxt[SPAN:, :] = jnp.zeros((SPAN, WIDE), F32)
    through = dxt[0:SPAN, :] * xt[0:SPAN, :]
    dcum[SPAN - 1 : SPAN, :] += split_dot(jnp.sum(through, axis=0, keepdims=True), pick)

    first = lax.broadcasted_iota(jnp.int32, (SPAN, 128), 1) < HEAD_DIM

    def pair(j):
        cs = pl.ds(pl.multiple_of(j * 128, 128), 128)
        group_rows = cumt[pl.ds(pl.multiple_of(g * GROUP, GROUP), GROUP), :]
        row = pltpu.roll(group_rows, lax.rem(GROUP - 2 * j, GROUP), 0)
        cols = pltpu.roll(grp[1], lax.rem(128 - 2 * j, 128), 1)
        for span in range(2):
            lo = span * SPAN
            hi = lo + SPAN
            dyp = dy[lo:hi, cs].astype(F32)
            dyt = dyp.T.astype(BF)
            xtb = xt[lo:hi, cs].astype(BF)
            parts = []
            for h in range(2):
                k = 2 * span + h
                for r in range(0, SPAN, CHUNK):
                    wide = 128 if r + CHUNK <= 128 else 256
                    gap = cols[lo + r : lo + r + CHUNK, h : h + 1] - row[h : h + 1, lo : lo + wide]
                    e = jnp.exp2(jnp.minimum(gap, 0.0))
                    decay[k, r : r + CHUNK, :wide] = e.astype(BF)
                    mix[k, r : r + CHUNK, :wide] = (scores[lo + r : lo + r + CHUNK, :wide] * e).astype(BF)
                    if wide < 256:
                        mix[k, r : r + CHUNK, wide:] = jnp.zeros((CHUNK, 256 - wide), BF)
                dmix = dot(jnp.where(first == (h == 0), dyp, 0.0).astype(BF), xtb, NT)
                top, low = dmix[:128, :128], dmix[128:, :]
                dscore[lo : lo + 128, :128] += top * decay[k, :128, :128].astype(F32)
                dscore[lo + 128 : hi, :] += low * decay[k, 128:, :].astype(F32)
                parts.append(dot(dyt[h * HEAD_DIM : (h + 1) * HEAD_DIM, :], mix[k]))
            dxt[lo:hi, cs] += jnp.concatenate(parts, axis=0).T

    def place(i, _):
        engine.pump(g * PUMPS + i, STEPS * PUMPS)

        @pl.when(i < GROUP // 2)
        def _():
            pair(i)

        return 0

    lax.fori_loop(0, PUMPS, place, 0)

    dcw_ref[...] = jnp.zeros_like(dcw_ref)
    for span in range(2):
        lo = span * SPAN
        hi = lo + SPAN
        x = xf[lo:hi, :]
        xtv = xt[lo:hi, :]
        dv = dxt[lo:hi, :]
        dcum[lo:hi, :] += split_dot(dsum[lo:hi, :] - dv * xtv.astype(BF).astype(F32), pick)
        ddt[lo:hi, :] += split_dot(dv * x, pick)
        dxt[lo:hi, :] = (dv * dtx[lo:hi, :] + dy[lo:hi, :].astype(F32) * skip) * sig[lo:hi, :]
        conv_weights(dcw_ref, buf, dxt[lo:hi, :], span, WIDE)
    back_halo(buf, dxt[...], cont, WIDE)
    for span in range(2):
        lo = span * SPAN
        dx_ref[lo : lo + SPAN, :] = conv_back(buf, cwx_ref[...], span, WIDE).astype(BF)

    engine.group_done(g)

    @pl.when(g == STEPS - 1)
    def _():
        load_halo(buf, bc_ref[...], cont, 2 * STATE)
        dcwbc_ref[...] = jnp.zeros_like(dcwbc_ref)
        for span in range(2):
            lo = span * SPAN
            hi = lo + SPAN
            ds = jnp.where(lower_tri(), dscore[lo:hi, :], 0.0).astype(BF)
            dbcs[lo:hi, :STATE] += dot(ds, bct[lo:hi, STATE:], TN)
            dbcs[lo:hi, STATE:] += dot(ds, bct[lo:hi, :STATE])
            s = conv_of(buf, cwbc_ref[...], span, 2 * STATE)
            sg = sigmoid(s)
            dcv = dbcs[lo:hi, :] * (sg * (1.0 + s * (1.0 - sg)))
            dbcs[lo:hi, :] = dcv
            conv_weights(dcwbc_ref, buf, dcv, span, 2 * STATE)
        back_halo(buf, dbcs[...], cont, 2 * STATE)
        for span in range(2):
            lo = span * SPAN
            dbc_ref[lo : lo + SPAN, : 2 * STATE] = conv_back(buf, cwbc_ref[...], span, 2 * STATE).astype(BF)
        lane = lax.broadcasted_iota(jnp.int32, (TOK, 128), 1)
        raw = jnp.where(lane < HEADS, dt_ref[...], 0.0) + hp_ref[0:1, :]
        decay_rate = -jnp.exp(hp_ref[1:2, :])
        tri = jnp.where(lower_tri(), 1.0, 0.0)
        da = jnp.concatenate(
            [dot(tri, dcum[lo : lo + SPAN, :], TN, HIGHEST) for lo in (0, SPAN)], axis=0
        )
        draw = jnp.where(lane < HEADS, (ddt[...] + decay_rate * da) * sigmoid(raw), 0.0)
        dbc_ref[:, 2 * STATE : 2 * STATE + 128] = draw.astype(BF)
        dbc_ref[:, 2 * STATE + 128 :] = jnp.zeros((TOK, BC_WIDE - 2 * STATE - 128), BF)
        dhp_ref[...] = jnp.zeros_like(dhp_ref)
        dhp_ref[0:1, :] = jnp.sum(draw, axis=0, keepdims=True)
        dhp_ref[1:2, :] = jnp.sum(da * decay_rate * dts[...], axis=0, keepdims=True)
        engine.close()


def conv_weights(out, buf, dcv, span, width):
    for k in range(CONV):
        out[3 - k : 4 - k, :] += jnp.sum(dcv * shifted(buf, k, span, width), axis=0, keepdims=True)
    out[4:5, :] += jnp.sum(dcv, axis=0, keepdims=True)


def back_halo(buf, dcv, cont, width):
    buf[0:SPAN, :width] = dcv[0:SPAN]
    buf[SPAN : SPAN + HALO, :width] = dcv[SPAN : SPAN + HALO] * cont
    buf[SPAN + HALO : 2 * SPAN + HALO, :width] = dcv[SPAN:]
    buf[2 * SPAN + HALO : 2 * (SPAN + HALO), :width] = jnp.zeros((HALO, width), F32)


def conv_back(buf, cw, span, width):
    base = span * (SPAN + HALO)
    total = cw[3:4, :] * buf[base : base + SPAN, :width]
    for k in range(1, CONV):
        total = total + cw[3 - k : 4 - k, :] * buf[base + k : base + k + SPAN, :width]
    return total


def scan_bwd(zx, cont, side_row, y, dy, work):
    hp, cw, cp = head_rows(side_row), conv_rows(side_row), column_rows(side_row)
    full = lambda shape: pl.BlockSpec(shape, lambda g: (0,) * len(shape))
    by_g = lambda rows_: pl.BlockSpec((rows_, WIDE), lambda g: (0, g))
    vmem = lambda *shape: pltpu.VMEM(shape, F32)
    return pl.pallas_call(
        partial(scan_kernel, work),
        grid=(STEPS,),
        out_shape=tuple(work.out_shapes),
        in_specs=[
            pl.BlockSpec(memory_space=pltpu.SMEM),
            pl.BlockSpec((TOK, WIDE), lambda g: (0, STEPS + g)),
            pl.BlockSpec((TOK, 2 * STATE), lambda g: (0, 2 * INNER // (2 * STATE))),
            pl.BlockSpec((TOK, 128), lambda g: (0, (INNER + XBC) // 128)),
            by_g(8),
            pl.BlockSpec((8, 2 * STATE), lambda g: (0, INNER // (2 * STATE))),
            full((8, 128)),
            by_g(8),
            by_g(TOK),
            by_g(TOK),
            *work.in_specs,
        ],
        out_specs=tuple(work.out_specs),
        scratch_shapes=[
            *work.scratch,
            vmem(2 * (HALO + SPAN), WIDE),
            pltpu.VMEM((TOK, 2 * STATE), BF),
            vmem(TOK, SPAN),
            vmem(TOK, 128),
            vmem(TOK, 128),
            vmem(128, TOK),
            pltpu.VMEM((4, SPAN, SPAN), BF),
            pltpu.VMEM((4, SPAN, SPAN), BF),
            vmem(TOK, WIDE),
            vmem(TOK, WIDE),
            vmem(TOK, WIDE),
            vmem(TOK, WIDE),
            vmem(TOK, WIDE),
            vmem(TOK, WIDE),
            vmem(TOK, SPAN),
            vmem(TOK, 2 * STATE),
            vmem(TOK, 128),
            vmem(TOK, 128),
            vmem(2, TOK, 128),
        ],
        compiler_params=work.params(),
        cost_estimate=pl.CostEstimate(flops=4 * 10**10, bytes_accessed=60 * 2**20, transcendentals=2 * 10**7),
        name=f"scan_bwd{work.name}",
    )(cont, zx, zx, zx, cw, cw, hp, cp, y, dy, *work.inputs)


def mixer_side(dgain, dskip, dcw, dcwbc, dhp):
    return jnp.concatenate(
        [
            dgain[0],
            jnp.concatenate([dcw[: CONV + 1], dcwbc[: CONV + 1]], axis=1).reshape(-1),
            dhp[0, :HEADS],
            dhp[1, :HEADS],
            jnp.sum(dskip[0].reshape(HEADS, HEAD_DIM), axis=1),
        ]
    )


ROWS = 96
COLS = 256
HALF = COLS // 2
LAG = 2
SLOTS = 2 * LAG
OWN_SLOTS = LAG + 1
MESH = pl.DeviceIdType.MESH
STAGES_A = ("core", "y", "z", "far", "rep")
STAGES_B = ("core", "rep", "y", "z", "far", "rep")
STAGES_ODD = ("core", "rep", "z", "far", "y", "rep")
SIZES_A = (8 * ROWS, 4 * ROWS, 2 * ROWS, ROWS, ROWS)
SIZES_B = (8 * ROWS, 4 * ROWS, 2 * ROWS, ROWS, ROWS // 2, ROWS // 2)
IN_BLOCKS = 26
WIDTH = IN_BLOCKS * COLS
OUT_BLOCKS = 6
SIDE_WIDE = 3584
SIDE_STEPS = INNER + 2 * STATE
SCAN_TICKS = 28
SIDE_LINKS = ("core", "rep", "y", "z", "far")


def choose(j, even, odd):
    return even + (odd - even) * (j % 2)


class Place:
    def __init__(self):
        self.me = lax.axis_index("shard")
        self.rep = lax.axis_index("rep")
        me = self.me
        self.bits = (me // 8 % 2, me // 4 % 2, me // 2 % 2, me % 2)
        flips = {"far": 0, "z": 1, "y": 2, "core": 3}
        self.targets = {
            name: (self.rep, self.owner(*(int(k == bit) for k in range(4)))) for name, bit in flips.items()
        }
        self.targets["rep"] = (1 - self.rep, me)

    def target(self, even, odd, j):
        if even == odd:
            return self.targets[even]
        return (self.rep, choose(j, self.targets[even][1], self.targets[odd][1]))

    def owner(self, far, z, y, core):
        bits = [1 - b if d else b for b, d in zip(self.bits, (far, z, y, core))]
        return bits[0] * 8 + bits[1] * 4 + bits[2] * 2 + bits[3]

    def greet(self):
        barrier = pltpu.get_barrier_semaphore()
        for target in self.targets.values():
            pl.semaphore_signal(barrier, inc=1, device_id=target, device_id_type=MESH)
        pl.semaphore_wait(barrier, len(self.targets))


class NoEngine:
    def __init__(self, refs):
        self.refs = refs

    def outputs(self, g):
        return self.refs

    def open(self):
        pass

    def pump(self, now, pumps):
        pass

    def group_done(self, g):
        pass

    def close(self):
        pass


class NoWork:
    name, inputs, in_specs, scratch = "", [], [], []

    def __init__(self):
        shapes = (
            ((TOK, INNER), BF), ((8, INNER), F32), ((8, INNER), F32),
            ((TOK, BC_WIDE), BF), ((8, 2 * STATE), F32), ((8, 128), F32),
        )
        self.out_shapes = [jax.ShapeDtypeStruct(*s) for s in shapes]
        by_g = [pl.BlockSpec((a.shape[0], WIDE), lambda g: (0, g)) for a in self.out_shapes[:3]]
        self.out_specs = by_g + [pl.BlockSpec(a.shape, lambda g: (0, 0)) for a in self.out_shapes[3:]]

    def engine(self, refs, free):
        return NoEngine(refs)

    def params(self):
        return pltpu.CompilerParams(vmem_limit_bytes=60 * 2**20)


class Sums:
    name = "_sums"
    blocks = 2 * OUT_BLOCKS + IN_BLOCKS
    ticks = blocks + LAG * len(STAGES_B)

    def __init__(self, left, low, dz, dgain, hidden, inverse, gain, full_in):
        self.inputs = [left, low, dz, dgain, inverse, gain, hidden, full_in]
        once = lambda a: pl.BlockSpec(a.shape, lambda *_: (0,) * len(a.shape), pipeline_mode=pl.Buffered(1))
        self.in_specs = [once(a) for a in self.inputs[:-2]] + [pl.BlockSpec(memory_space=pl.ANY)] * 2
        self.out_shapes = [
            jax.ShapeDtypeStruct((TOK, D), F32),
            jax.ShapeDtypeStruct((ROWS, self.blocks * COLS), F32),
            jax.ShapeDtypeStruct((len(SIDE_LINKS) + 1, 8, SIDE_WIDE), F32),
        ]
        self.out_specs = [once(a) for a in self.out_shapes]
        self.out_specs[1] = pl.BlockSpec(memory_space=pl.ANY)
        self.scratch = [
            pltpu.VMEM((TOK, INNER), BF),
            pltpu.VMEM((8, WIDE), F32),
            pltpu.VMEM((8, WIDE), F32),
            pltpu.VMEM((TOK, BC_WIDE), BF),
            pltpu.VMEM((8, 2 * STATE), F32),
            pltpu.VMEM((8, 128), F32),
            pltpu.VMEM((2, D, COLS), BF),
            pltpu.SemaphoreType.DMA((5,)),
            pltpu.VMEM((len(SIDE_LINKS), 8, SIDE_WIDE), F32),
            pltpu.SemaphoreType.DMA((2, len(SIDE_LINKS))),
            pltpu.VMEM((16 * ROWS, COLS), F32),
            pltpu.VMEM((TOK, COLS), BF),
            pltpu.VMEM((SLOTS, ROWS, COLS), F32),
            pltpu.SemaphoreType.DMA((SLOTS,)),
        ]
        for links, sizes in ((STAGES_A, SIZES_A), (STAGES_B, SIZES_B)):
            self.scratch += [pltpu.VMEM((OWN_SLOTS, r, HALF), BF) for r in sizes]
            self.scratch += [pltpu.VMEM((SLOTS, r, HALF), BF) for r in sizes]
            self.scratch += [pltpu.VMEM((OWN_SLOTS, r, HALF), F32) for r in sizes[:-1]]
            self.scratch += [pltpu.SemaphoreType.DMA((len(links), SLOTS))] * 2

    def params(self):
        return pltpu.CompilerParams(collective_id=1, has_side_effects=True, vmem_limit_bytes=58 * 2**20)

    def engine(self, refs, free):
        return Engine(self, refs, free)


class Engine:
    def __init__(self, work, refs, free):
        self.work, self.free = work, free
        n = len(work.inputs)
        self.left, low, self.dz, self.dgain, self.inverse, self.gain, self.h, self.w = refs[:n]
        self.dr, self.out_ref, self.side_out = refs[n : n + 3]
        rest = refs[n + 3 :]
        self.dx, self.dskip, self.dcw, self.dbc, self.dcwbc, self.dhp = rest[:6]
        self.wbuf, self.wsem, self.side_in, self.side_sems, self.tmp, self.right, self.stage, self.out_sem = rest[6:14]
        rest = rest[14:]
        self.kinds = {}
        for kind, links in (("a", STAGES_A), ("b", STAGES_B)):
            n = len(links)
            src, rest = rest[:n], rest[n:]
            dst, rest = rest[:n], rest[n:]
            acc, rest = rest[: n - 1], rest[n - 1 :]
            self.kinds[kind] = (links, src, dst, acc, rest[0], rest[1])
            rest = rest[2:]
        self.operands = [(low, 2, OUT_BLOCKS), (self.dz, 1, 12), (self.dx, 1, 12), (self.dbc, 1, 2)]
        self.place = Place()

    def outputs(self, g):
        dx = self.dx.at[:, pl.ds(pl.multiple_of(g * WIDE, WIDE), WIDE)]
        return dx, self.dskip, self.dcw, self.dbc, self.dcwbc, self.dhp

    def group_done(self, g):
        cols = pl.ds(pl.multiple_of(g * WIDE, WIDE), WIDE)
        self.side_out[0, 0 : CONV + 1, cols] = self.dcw[0 : CONV + 1, :]
        self.side_out[0, 5:6, cols] = self.dskip[0:1, :]

    def weights(self, k):
        cols = pl.ds(pl.multiple_of(k * COLS, COLS), COLS)
        return pltpu.make_async_copy(self.w.at[:, cols], self.wbuf.at[k % 2], self.wsem.at[k % 2])

    def hidden(self, c):
        return pltpu.make_async_copy(self.h.at[:, c * WIDE : (c + 1) * WIDE], self.free[c], self.wsem.at[2 + c])

    def close(self):
        count = IN_BLOCKS
        side_tick = SCAN_TICKS + (count + 3) // 4
        self.weights(0).start()
        self.weights(1).start()
        for c in range(3):
            self.hidden(c).start()
        self.side_out[0, 6:7, 0:INNER] = self.dgain[0:1, :]
        self.side_out[0, 0 : CONV + 1, INNER:SIDE_STEPS] = self.dcwbc[0 : CONV + 1, :]
        self.side_out[0, 0:2, SIDE_STEPS : SIDE_STEPS + 128] = self.dhp[0:2, :]
        self.dr[...] = jnp.zeros_like(self.dr)
        bounds = ((self.dz, 0, 12), (self.dx, 12, 24), (self.dbc, 24, count))

        def product(k, _):
            self.weights(k).wait()
            for ref, lo, hi in bounds:

                @pl.when((k >= lo) & (k < hi))
                def _():
                    cols = pl.ds(pl.multiple_of((k - lo) * COLS, COLS), COLS)
                    self.right[...] = ref[:, cols]

            self.dr[...] += dot(self.right[...], self.wbuf[k % 2], NT)

            @pl.when(k + 2 < count)
            def _():
                self.weights(k + 2).start()

            return 0

        def step(t, _):
            self.tick(t)
            done = 4 * (t - SCAN_TICKS)
            lax.fori_loop(jnp.minimum(done, count), jnp.minimum(done + 4, count), product, 0)

            @pl.when(t == side_tick)
            def _():
                for c in range(3):
                    self.hidden(c).wait()
                    cols = slice(c * WIDE, (c + 1) * WIDE)
                    scaled = self.free[c][...] * self.inverse[:, 0:1]
                    self.side_out[0, 7:8, cols] = jnp.sum(self.dr[:, cols] * scaled, axis=0, keepdims=True)
                self.side_copy(0).start()

            for k in range(len(SIDE_LINKS)):

                @pl.when(t == side_tick + 2 * (k + 1))
                def _():
                    self.side_copy(k).wait()
                    self.side_out[k + 1] = self.side_out[k] + self.side_in[k]
                    if k + 1 < len(SIDE_LINKS):
                        self.side_copy(k + 1).start()

            return 0

        lax.fori_loop(SCAN_TICKS, self.work.ticks, step, 0)
        for j in range(self.work.blocks - SLOTS, self.work.blocks):
            self.leave(j).wait()
        inverse = self.inverse[:, 0:1]
        mean = 0.0
        for c in range(3):
            cols = slice(c * WIDE, (c + 1) * WIDE)
            scaled = self.free[c][...] * inverse
            dn = self.dr[:, cols] * self.gain[0:1, cols]
            self.free[c][...] = scaled
            self.dr[:, cols] = dn
            mean = mean + jnp.sum(dn * scaled, axis=1, keepdims=True)
        mean = mean * (1.0 / D)
        for c in range(3):
            cols = slice(c * WIDE, (c + 1) * WIDE)
            self.dr[:, cols] = inverse * (self.dr[:, cols] - self.free[c][...] * mean)

    def copy(self, kind, s, j):
        links, src, dst, _, ss, rs = self.kinds[kind]
        slot = j % SLOTS
        return pltpu.make_async_remote_copy(
            src_ref=src[s].at[j % OWN_SLOTS],
            dst_ref=dst[s].at[slot],
            send_sem=ss.at[s, slot],
            recv_sem=rs.at[s, slot],
            device_id=self.place.target(links[s], STAGES_ODD[s] if kind == "b" else links[s], j),
            device_id_type=MESH,
        )

    def multiply(self, j):
        first = 0
        for right_ref, k, n in self.operands:

            @pl.when((j >= first) & (j < first + k * n))
            def _():
                cols = pl.ds(pl.multiple_of((j - first) % n * COLS, COLS), COLS)
                self.right[...] = right_ref[:, cols]

            first += k * n
        left = jnp.where(j < 2 * OUT_BLOCKS, 1 + j // OUT_BLOCKS, 0)
        self.tmp[...] = dot(self.left[left], self.right[...])

    def begin(self, j):
        slot = j % OWN_SLOTS
        self.multiply(j)
        place, rep = self.place, self.place.rep
        src_a, acc_a = self.kinds["a"][1][0], self.kinds["a"][3][0]
        src_b, acc_b = self.kinds["b"][1][0], self.kinds["b"][3][0]
        for d_core in range(2):
            for b in range(8):
                owner = place.owner(b & 1, b >> 1 & 1, b >> 2 & 1, d_core)
                block = self.tmp[pl.ds(pl.multiple_of(owner * ROWS, ROWS), ROWS), :HALF]
                to = slice(b * ROWS, (b + 1) * ROWS)
                if d_core:
                    src_a[slot, to, :] = block.astype(BF)
                else:
                    acc_a[slot, to, :] = block
                owner = choose(j, owner, place.owner(b >> 1 & 1, b >> 2 & 1, b & 1, d_core))
                for d_rep in range(2):
                    top = owner * ROWS + (1 - rep if d_rep else rep) * (ROWS // 2)
                    block = self.tmp[pl.ds(pl.multiple_of(top, ROWS // 2), ROWS // 2), HALF:]
                    to = slice((d_rep * 8 + b) * (ROWS // 2), (d_rep * 8 + b + 1) * (ROWS // 2))
                    if d_core:
                        src_b[slot, to, :] = block.astype(BF)
                    else:
                        acc_b[slot, to, :] = block
        self.copy("a", 0, j).start()
        self.copy("b", 0, j).start()

    def go_on(self, kind, s, j):
        links, src, dst, acc, _, _ = self.kinds[kind]
        slot, own = j % SLOTS, j % OWN_SLOTS
        self.copy(kind, s - 1, j).wait()
        size = src[s].shape[1]
        if s == len(links) - 1:
            src[s][own] = (acc[s - 1][own] + dst[s - 1][slot].astype(F32)).astype(BF)
        else:
            src[s][own] = (acc[s - 1][own, size:, :] + dst[s - 1][slot, size:, :].astype(F32)).astype(BF)
            acc[s][own] = acc[s - 1][own, :size, :] + dst[s - 1][slot, :size, :].astype(F32)
        self.copy(kind, s, j).start()

    def leave(self, j):
        cols = pl.ds(pl.multiple_of(j * COLS, COLS), COLS)
        slot = j % SLOTS
        return pltpu.make_async_copy(self.stage.at[slot], self.out_ref.at[:, cols], self.out_sem.at[slot])

    def finish(self, kind, j):
        links, src, dst, _, _, _ = self.kinds[kind]
        slot, own = j % SLOTS, j % OWN_SLOTS
        self.copy(kind, len(links) - 1, j).wait()
        rep = self.place.rep
        if kind == "a":

            @pl.when(j >= SLOTS)
            def _():
                self.leave(j - SLOTS).wait()

            self.stage[slot, :, :HALF] = src[-1][own].astype(F32) + dst[-1][slot].astype(F32)
        else:
            mine = pl.ds(pl.multiple_of(rep * (ROWS // 2), ROWS // 2), ROWS // 2)
            theirs = pl.ds(pl.multiple_of((1 - rep) * (ROWS // 2), ROWS // 2), ROWS // 2)
            self.stage[slot, mine, HALF:] = src[-1][own].astype(F32)
            self.stage[slot, theirs, HALF:] = dst[-1][slot].astype(F32)
            self.leave(j).start()

    def side_copy(self, k):
        return pltpu.make_async_remote_copy(
            src_ref=self.side_out.at[k],
            dst_ref=self.side_in.at[k],
            send_sem=self.side_sems.at[0, k],
            recv_sem=self.side_sems.at[1, k],
            device_id=self.place.targets[SIDE_LINKS[k]],
            device_id_type=MESH,
        )

    def open(self):
        self.place.greet()
        self.side_out[0] = jnp.zeros((8, SIDE_WIDE), F32)

    def tick(self, t):
        n_a, n_b = len(STAGES_A), len(STAGES_B)
        for s in range(n_b, -1, -1):
            j = t - LAG * s

            @pl.when((j >= 0) & (j < self.work.blocks))
            def _():
                if s == 0:
                    self.begin(j)
                    return
                if s < n_b:
                    self.go_on("b", s, j)
                else:
                    self.finish("b", j)
                if s < n_a:
                    self.go_on("a", s, j)
                elif s == n_a:
                    self.finish("a", j)

    def pump(self, now, pumps):
        def more(t, _):
            self.tick(t)
            return 0

        lax.fori_loop(now * SCAN_TICKS // pumps, (now + 1) * SCAN_TICKS // pumps, more, 0)


def join_kernel(dh_ref, e_ref, branch_ref, e_out, low_out, factor_out):
    e = e_ref[...].astype(F32) + dh_ref[...]
    low = e.astype(BF)
    e_out[...] = e
    low_out[...] = low
    factor = jnp.sum(low.astype(F32) * branch_ref[...], axis=1, keepdims=True) * (1.0 / INNER)
    factor_out[...] = jnp.broadcast_to(factor, factor_out.shape)


def join(dh, gradient, branch):
    part = 128
    rows = lambda a: pl.BlockSpec((part, a), lambda k: (k, 0))
    shape = lambda a, t: jax.ShapeDtypeStruct(a, t)
    return pl.pallas_call(
        join_kernel,
        grid=(TOK // part,),
        out_shape=(shape((TOK, D), F32), shape((TOK, D), BF), shape((TOK, 128), F32)),
        in_specs=[rows(D), rows(D), rows(D)],
        out_specs=(rows(D), rows(D), rows(128)),
        compiler_params=pltpu.CompilerParams(vmem_limit_bytes=60 * 2**20),
        cost_estimate=pl.CostEstimate(flops=10**7, bytes_accessed=15 * 2**20, transcendentals=0),
        name="join",
    )(dh, gradient, branch)


def adamw_step(parameter, first_moment, second_moment, gradient, step_rate, decay_rate):
    first_new = BETA_ONE * first_moment + (1.0 - BETA_ONE) * gradient
    second_new = BETA_TWO * second_moment + (1.0 - BETA_TWO) * gradient * gradient
    correction_one = 1.0 - BETA_ONE**STEP
    correction_two = 1.0 - BETA_TWO**STEP
    update = first_new / correction_one / (jnp.sqrt(second_new / correction_two) + ADAM_EPSILON)
    return (parameter - step_rate * (update + decay_rate * parameter), first_new, second_new)


def adam_kernel(wi, mi, vi, wo, mo, vo, sums_0, sums_1, e_ref, dh_ref, *outs):
    outs[-1][...] = e_ref[...] + dh_ref[...]
    for layer, sums in enumerate((sums_0, sums_1)):

        @pl.when(pl.program_id(0) == layer)
        def _():
            width = wi.shape[2]
            todo = [((wi, mi, vi), outs[:3], 0, sums[:, 2 * D : 2 * D + width])]
            todo += [((wo, mo, vo), outs[3:6], (0, q), sums[:, q * D : (q + 1) * D]) for q in range(2)]
            for refs, to, at, gradient in todo:
                values = adamw_step(*(ref[at] for ref in refs), gradient, RATE_MATRIX, DECAY_MATRIX)
                for ref, value in zip(to, values):
                    ref[at] = value


def adam(inputs, outputs, sums, gradient, dh):
    part = 24
    outputs = [a.reshape(LAYERS, 2, ROWS, D) for a in outputs]
    width = inputs[0].shape[2]
    in_spec = pl.BlockSpec((1, part, width), lambda l, k: (l, k, 0))
    out_spec = pl.BlockSpec((1, 2, part, D), lambda l, k: (l, 0, k, 0))
    steps = ROWS // part
    row_spec = pl.BlockSpec((TOK // (LAYERS * steps), D), lambda l, k: (l * steps + k, 0))
    only_0 = lambda l, k: (jnp.where(l == 0, k, ROWS // part - 1), 0)
    only_1 = lambda l, k: (jnp.where(l == 1, k, 0), 0)
    done = pl.pallas_call(
        adam_kernel,
        grid=(LAYERS, ROWS // part),
        out_shape=tuple(jax.ShapeDtypeStruct(a.shape, F32) for a in (*inputs, *outputs, gradient)),
        in_specs=[in_spec] * 3
        + [out_spec] * 3
        + [pl.BlockSpec((part, a.shape[1]), at) for a, at in zip(sums, (only_0, only_1))]
        + [row_spec] * 2,
        out_specs=(in_spec,) * 3 + (out_spec,) * 3 + (row_spec,),
        compiler_params=pltpu.CompilerParams(vmem_limit_bytes=60 * 2**20),
        cost_estimate=pl.CostEstimate(flops=10**8, bytes_accessed=52 * 2**20, transcendentals=0),
        name="adam",
    )(*inputs, *outputs, *sums, gradient, dh)
    return done[:3], [a.reshape(LAYERS, 2 * ROWS, D) for a in done[3:6]], done[6]


GATHER_A = ("far", "z", "y", "core")
GATHER_B = ("far", "z", "y", "rep", "core")
GATHER_ODD = ("y", "far", "z", "rep", "core")
GATHER_SLOTS = 6 * LAG


def gather_kernel(
    blocks, w_in, w_out, r_ref, full_in, full_out, zx,
    own_in, own_out, buf_a, buf_b, natural, zbuf, local, flush, ss_a, rs_a, ss_b, rs_b,
):
    place = Place()
    rep = place.rep
    kinds = {"a": (GATHER_A, buf_a, ROWS, ss_a, rs_a), "b": (GATHER_B, buf_b, ROWS // 2, ss_b, rs_b)}
    valid = w_in.shape[2] - (IN_BLOCKS - 1) * COLS

    def copy(kind, s, j):
        links, buf, rows, ss, rs = kinds[kind]
        slot = j % GATHER_SLOTS
        size = rows << s
        return pltpu.make_async_remote_copy(
            src_ref=buf.at[slot, 0:size, :],
            dst_ref=buf.at[slot, size : 2 * size, :],
            send_sem=ss.at[s, slot],
            recv_sem=rs.at[s, slot],
            device_id=place.target(links[s], GATHER_ODD[s] if kind == "b" else links[s], j),
            device_id_type=MESH,
        )

    def begin(j):
        slot = j % GATHER_SLOTS
        mine = pl.ds(pl.multiple_of(rep * (ROWS // 2), ROWS // 2), ROWS // 2)

        @pl.when(j < IN_BLOCKS - 1)
        def _():
            lo = pl.multiple_of(j * COLS, COLS)
            buf_a[slot, 0:ROWS, :] = own_in[:, pl.ds(lo, HALF)].astype(BF)
            buf_b[slot, 0 : ROWS // 2, :] = own_in[mine, pl.ds(pl.multiple_of(lo + HALF, HALF), HALF)].astype(BF)

        @pl.when(j == IN_BLOCKS - 1)
        def _():
            buf_a[slot, 0:ROWS, :] = jnp.zeros((ROWS, HALF), BF)
            buf_b[slot, 0 : ROWS // 2, :] = jnp.zeros((ROWS // 2, HALF), BF)
            buf_a[slot, 0:ROWS, 0:valid] = own_in[:, (IN_BLOCKS - 1) * COLS :].astype(BF)

        if blocks > IN_BLOCKS:

            @pl.when(j >= IN_BLOCKS)
            def _():
                k = j - IN_BLOCKS
                q = k // OUT_BLOCKS
                lo = pl.multiple_of(k % OUT_BLOCKS * COLS, COLS)
                buf_a[slot, 0:ROWS, :] = own_out[q, :, pl.ds(lo, HALF)].astype(BF)
                buf_b[slot, 0 : ROWS // 2, :] = own_out[q, mine, pl.ds(pl.multiple_of(lo + HALF, HALF), HALF)].astype(BF)

        copy("a", 0, j).start()
        copy("b", 0, j).start()

    def out_copies(j):
        p = j % 2
        cols = pl.ds(pl.multiple_of(j * COLS, COLS), COLS)
        return (
            pltpu.make_async_copy(natural.at[p], full_in.at[:, :, cols], flush.at[0, p]),
            pltpu.make_async_copy(zbuf.at[p], zx.at[:, cols], flush.at[1, p]),
        )

    def row_copy(j):
        p = j % 2
        k = j - IN_BLOCKS
        cols = pl.ds(pl.multiple_of(k % OUT_BLOCKS * COLS, COLS), COLS)
        q = k // OUT_BLOCKS
        return pltpu.make_async_copy(natural.at[p], full_out.at[q // 2, :, q % 2, :, cols], flush.at[0, p])

    def flushed(j):
        @pl.when((j >= 0) & (j < IN_BLOCKS))
        def _():
            for c in out_copies(j):
                c.wait()

        if blocks > IN_BLOCKS:

            @pl.when(j >= IN_BLOCKS)
            def _():
                row_copy(j).wait()

    def finish(j):
        slot = j % GATHER_SLOTS
        p = j % 2
        copy("b", len(GATHER_B) - 1, j).wait()
        flushed(j - 2)
        for k in range(16):
            owner = place.owner(k & 1, k >> 1 & 1, k >> 2 & 1, k >> 3)
            natural[p, owner, :, :HALF] = buf_a[slot, k * ROWS : (k + 1) * ROWS, :]
            owner = choose(j, owner, place.owner(k >> 1 & 1, k >> 2 & 1, k & 1, k >> 3))
            for d_rep in range(2):
                at = (k & 7) + 8 * d_rep + 16 * (k >> 3)
                half = pl.ds(pl.multiple_of((1 - rep if d_rep else rep) * (ROWS // 2), ROWS // 2), ROWS // 2)
                natural[p, owner, half, HALF:] = buf_b[slot, at * (ROWS // 2) : (at + 1) * (ROWS // 2), :]

        @pl.when(j < IN_BLOCKS)
        def _():
            zbuf[p] = dot(r_ref[...], natural[p].reshape(16 * ROWS, COLS))
            for c in out_copies(j):
                c.start()

        if blocks > IN_BLOCKS:

            @pl.when(j >= IN_BLOCKS)
            def _():
                row_copy(j).start()

    loads = [pltpu.make_async_copy(w_in.at[0], own_in, local.at[0])]
    loads.append(pltpu.make_async_copy(w_out, own_out, local.at[1]))
    for load in loads:
        load.start()
    place.greet()
    for load in loads:
        load.wait()

    def tick(t, _):
        for s in range(len(GATHER_B), -1, -1):
            j = t - LAG * s

            @pl.when((j >= 0) & (j < blocks))
            def _():
                if s == 0:
                    begin(j)
                elif s == len(GATHER_B):
                    finish(j)
                else:
                    copy("b", s - 1, j).wait()
                    copy("b", s, j).start()
                    copy("a", s - 1, j).wait()
                    if s < len(GATHER_A):
                        copy("a", s, j).start()

        return 0

    lax.fori_loop(0, blocks + LAG * len(GATHER_B), tick, 0)
    flushed(jnp.int32(blocks - 2))
    flushed(jnp.int32(blocks - 1))


def gather_first(weight_in, weight_out, normed):
    outs = weight_out.reshape(2 * LAYERS, ROWS, D)
    blocks = IN_BLOCKS + outs.shape[0] * OUT_BLOCKS
    hbm = pl.BlockSpec(memory_space=pl.ANY)
    sems = pltpu.SemaphoreType.DMA
    full_in, full_out, zx = pl.pallas_call(
        partial(gather_kernel, blocks),
        out_shape=(
            jax.ShapeDtypeStruct((16, ROWS, WIDTH), BF),
            jax.ShapeDtypeStruct((LAYERS, 16, 2, ROWS, D), BF),
            jax.ShapeDtypeStruct((TOK, WIDTH), F32),
        ),
        in_specs=[hbm, hbm, pl.BlockSpec(memory_space=pltpu.VMEM)],
        out_specs=(hbm,) * 3,
        scratch_shapes=[
            pltpu.VMEM(weight_in.shape[1:], F32),
            pltpu.VMEM(outs.shape, F32),
            pltpu.VMEM((GATHER_SLOTS, 16 * ROWS, HALF), BF),
            pltpu.VMEM((GATHER_SLOTS, 16 * ROWS, HALF), BF),
            pltpu.VMEM((2, 16, ROWS, COLS), BF),
            pltpu.VMEM((2, TOK, COLS), F32),
            sems((2,)),
            sems((2, 2)),
            sems((len(GATHER_A), GATHER_SLOTS)),
            sems((len(GATHER_A), GATHER_SLOTS)),
            sems((len(GATHER_B), GATHER_SLOTS)),
            sems((len(GATHER_B), GATHER_SLOTS)),
        ],
        compiler_params=pltpu.CompilerParams(
            collective_id=4, has_side_effects=True, vmem_limit_bytes=60 * 2**20
        ),
        cost_estimate=pl.CostEstimate(flops=10**10, bytes_accessed=50 * 2**20, transcendentals=0),
        name="gather_first",
    )(weight_in, outs, normed)
    return full_in.reshape(16 * ROWS, WIDTH), full_out.reshape(LAYERS, INNER, D), zx


def project_kernel(r_ref, w_ref, out_ref):
    out_ref[...] = dot(r_ref[...], w_ref[...])


def project(normed, full_in):
    part = WIDTH // 4
    return pl.pallas_call(
        project_kernel,
        grid=(WIDTH // part,),
        out_shape=jax.ShapeDtypeStruct((TOK, WIDTH), F32),
        in_specs=[
            pl.BlockSpec((TOK, D), lambda k: (0, 0), pipeline_mode=pl.Buffered(1)),
            pl.BlockSpec((D, part), lambda k: (0, k)),
        ],
        out_specs=pl.BlockSpec((TOK, part), lambda k: (0, k)),
        compiler_params=pltpu.CompilerParams(vmem_limit_bytes=60 * 2**20),
        cost_estimate=pl.CostEstimate(flops=10**10, bytes_accessed=36 * 2**20, transcendentals=0),
        name="project",
    )(normed, full_in)


def rows_kernel(normed_ref, mixed_ref, out_ref):
    out_ref[0] = normed_ref[...].astype(F32).T.astype(BF)
    turned = mixed_ref[...].astype(F32).T.astype(BF)
    for i in range(turned.shape[0] // (2 * ROWS)):
        for q in range(2):
            lo = (2 * i + q) * ROWS
            out_ref[1 + q, i * ROWS : (i + 1) * ROWS, :] = turned[lo : lo + ROWS]


def left_rows(normed, mixed):
    steps = 4
    wide = D // steps
    return pl.pallas_call(
        rows_kernel,
        grid=(steps,),
        out_shape=jax.ShapeDtypeStruct((3, D, TOK), BF),
        in_specs=[
            pl.BlockSpec((TOK, wide), lambda k: (0, k)),
            pl.BlockSpec((TOK, 2 * wide), lambda k: (0, k)),
        ],
        out_specs=pl.BlockSpec((3, wide, TOK), lambda k: (0, k, 0)),
        compiler_params=pltpu.CompilerParams(vmem_limit_bytes=60 * 2**20),
        cost_estimate=pl.CostEstimate(flops=0, bytes_accessed=9 * 2**20, transcendentals=0),
        name="left_rows",
    )(normed, mixed)


def span_starts(seq_lengths):
    offsets = jnp.cumsum(seq_lengths) - seq_lengths
    places = jnp.arange(seq_lengths.shape[0], dtype=jnp.int32) * SPAN
    matches = (offsets[None, :] == places[:, None]) & (seq_lengths[None, :] > 0)
    return jnp.any(matches, axis=1)


def swap(value, axis, count, bit):
    return lax.ppermute(value, axis, [(i, i ^ bit) for i in range(count)])


def plain_owner_sum(left, right, reps):
    mine = lax.psum_scatter(dot(left, right, TN).astype(BF), "shard", scatter_dimension=0, tiled=True)
    total = mine.astype(F32)
    for bit in [1 << k for k in range(reps.bit_length() - 1)]:
        total = total + swap(total.astype(BF), "rep", reps, bit).astype(F32)
    return total


def side_gradient(block):
    conv = block[: CONV + 1, :SIDE_STEPS].reshape(-1)
    steps = block[:2, SIDE_STEPS : SIDE_STEPS + HEADS].reshape(-1)
    skip = jnp.sum(block[5, :INNER].reshape(HEADS, HEAD_DIM), axis=1)
    return jnp.concatenate([block[7, :D], block[6, :INNER], conv, steps, skip])


def pad_cast(weight, width):
    return jnp.pad(weight.astype(BF), ((0, 0), (0, width - weight.shape[1])))


def sums_plain(normed, mixed, dz, dxs, dbc, low, full_in, reps):
    right = jnp.concatenate([dz, *dxs, dbc], axis=1)
    used = 2 * INNER + 2 * STATE + HEADS
    sum_in = plain_owner_sum(normed, right[:, :used], reps)
    sum_out = plain_owner_sum(mixed, low, reps)
    return sum_in, sum_out, dot(right, full_in, NT)


def per_device(
    tokens, cotangent, lengths,
    weight_in, moment_in, second_in,
    weight_out, moment_out, second_out,
    side_params, side_moment, side_second,
    *, reps, shards,
):
    direct = shards == 16 and reps == 2
    cont = jnp.where(span_starts(lengths[0])[1], 0.0, 1.0).astype(F32).reshape(1, 1)
    hidden = tokens.astype(F32)
    saved = []
    layer_outs = []
    for layer in range(LAYERS):
        gain = side_params[layer, :D]
        inverse_in = lax.rsqrt(jnp.mean(hidden * hidden, axis=-1, keepdims=True) + EPSILON)
        normed = (hidden * inverse_in * gain).astype(BF)
        if direct and layer == 0:
            normed, later = lax.optimization_barrier((normed, pad_cast(weight_in[1], WIDTH)))
            first_in, both_out, zx = gather_first(weight_in, weight_out, normed)
            zx, later = lax.optimization_barrier((zx, later))
            second_in_full = lax.all_gather(later, "shard", axis=0, tiled=True)
            full_in, full_out = first_in, both_out[0]
        elif direct:
            full_in, full_out = second_in_full, both_out[1]
            zx = project(normed, full_in)
        else:
            full_in = lax.all_gather(pad_cast(weight_in[layer], WIDTH), "shard", axis=0, tiled=True)
            full_out = lax.all_gather(weight_out[layer].astype(BF), "shard", axis=0, tiled=True)
            zx = jnp.dot(normed, full_in, preferred_element_type=F32)
        mixed, y, inverse = mixer_fwd(zx, cont, side_params[layer])
        left = None
        if direct:
            mixed, left = lax.optimization_barrier((mixed, left_rows(normed, mixed)))
        branch = jnp.dot(mixed, full_out, preferred_element_type=F32)
        saved.append((full_in, full_out, hidden, inverse_in, normed, zx, mixed, y, inverse, branch, left))
        hidden = hidden + branch
        layer_outs.append(hidden)
    gradient = cotangent.astype(F32)
    low = cotangent
    factor = jnp.sum(gradient * saved[-1][-2], axis=1, keepdims=True) * (1.0 / INNER)
    sums = [None] * LAYERS
    sides = [None] * LAYERS
    for layer in reversed(range(LAYERS)):
        full_in, full_out, hidden, inverse_in, normed, zx, mixed, y, inverse, branch, left = saved[layer]
        side_row = side_params[layer]
        gain = side_row[:D]
        rows = jnp.concatenate([inverse[:, :1], factor[:, :1], jnp.zeros((TOK, 126), F32)], axis=1)
        dz, dy, dgain = gate_bwd(low, full_out, zx, side_row, y, rows)
        if direct:
            inverse_rows = jnp.broadcast_to(inverse_in, (TOK, 128))
            gain_rows = jnp.broadcast_to(gain, (8, D))
            work = Sums(left, low, dz, dgain, hidden, inverse_rows, gain_rows, full_in)
            back, sums[layer], side = scan_bwd(zx, cont, side_row, y, dy, work)
            sides[layer] = side_gradient(side[-1])
        else:
            dx, dskip, dcw, dbc, dcwbc, dhp = scan_bwd(zx, cont, side_row, y, dy, NoWork())
            side = mixer_side(dgain, dskip, dcw, dcwbc, dhp)
            sum_in, sum_out, back = sums_plain(normed, mixed, dz, [dx], dbc, low, full_in, reps)
            sums[layer] = (sum_in, sum_out)
            scaled = hidden * inverse_in
            side = jnp.concatenate([jnp.sum(back * scaled, axis=0), side])
            sides[layer] = lax.psum(side, ("rep", "shard"))
            dn = back * gain
            back = inverse_in * (dn - scaled * jnp.mean(dn * scaled, axis=1, keepdims=True))
        if layer:
            gradient, low, factor = join(back, gradient, saved[layer - 1][-2])
    if direct:
        new_in, new_out, gradient = adam(
            (weight_in, moment_in, second_in), (weight_out, moment_out, second_out), sums, gradient, back
        )
    else:
        gradient = gradient + back
        grad_in = jnp.stack([v[0] for v in sums])
        grad_out = jnp.stack([v[1] for v in sums])
        new_in = adamw_step(weight_in, moment_in, second_in, grad_in, RATE_MATRIX, DECAY_MATRIX)
        new_out = adamw_step(weight_out, moment_out, second_out, grad_out, RATE_MATRIX, DECAY_MATRIX)
    grad_side = jnp.stack(sides)
    return (
        jnp.stack(layer_outs),
        gradient,
        *new_in,
        *new_out,
        *adamw_step(side_params, side_moment, side_second, grad_side, RATE_SIDE, 0.0),
    )


def solution(mesh):
    rows = P(("rep", "shard"), None)
    owned = P(None, "shard", None)
    body = partial(per_device, reps=mesh.shape["rep"], shards=mesh.shape["shard"])
    return jax.shard_map(
        body,
        mesh=mesh,
        in_specs=(rows, rows, rows) + (owned,) * 6 + (P(),) * 3,
        out_specs=(P(None, ("rep", "shard"), None), rows) + (owned,) * 6 + (P(),) * 3,
        check_vma=False,
    )
```
